256 devices in a mesh: row: 32 (over y, x, core), col: 8 (over z).
Axes of the slice: x: 4, y: 4, z: 8, core: 2. Of those that a mesh axis runs over, the one named last changes fastest.
Arguments:
- embeddings: bfloat16 [24576, 1024], P(('row', 'col')), may hold values from -8 to 8
- labels: int32 [24576], P(('row', 'col')), may hold values from 0 to 999
Outputs:
- grad: float32 [24576, 1024], P(('row', 'col'))
- loss: float32 [], replicated
The draws below stay inside these ranges and needn't reach their ends.
All inputs are finite; a program needn't handle non-finite values.
Results may differ from the reference program's by a relative error of at most 0.0027.
Values may be sent and summed in bfloat16 or wider, within the bound.
A program may use at most 128 MiB of HBM per device.

```python
import jax
import jax.numpy as jnp
from jax import lax

D = 1024
CLASSES = 1000
ROW_DEV = 96
TOKENS = 24576
N_COL = 8


def class_labels(key):
    key = jax.random.fold_in(key, 101)
    first_key, second_key, third_key, level_key = jax.random.split(key, 4)
    position = jnp.arange(TOKENS, dtype=jnp.int32)
    column = position // ROW_DEV % N_COL
    grid_row = position // (ROW_DEV * N_COL)
    row_count = TOKENS // (ROW_DEV * N_COL)
    common_count = max(CLASSES // 16, 2)
    row_level = jax.random.randint(level_key, (row_count,), 150, 900)
    threshold = row_level[grid_row] * (N_COL - 1 + 2 * column) // (3 * (N_COL - 1))
    ticket = jax.random.randint(first_key, (TOKENS,), 0, 1000)
    common_label = jax.random.randint(second_key, (TOKENS,), 0, common_count)
    other_label = jax.random.randint(third_key, (TOKENS,), common_count, CLASSES)
    chosen = jnp.where(ticket < threshold, common_label, other_label)
    chosen = chosen.at[0].set(0)
    chosen = chosen.at[TOKENS - 1].set(CLASSES - 1)
    return chosen.astype(jnp.int32)


def draw_labels(key, part):
    return class_labels(key)


def draw_embeddings(key, part):
    chosen = class_labels(key)
    key = jax.random.fold_in(key, 7)
    mean_key = jax.random.fold_in(key, 0)
    noise_key = jax.random.fold_in(key, 1)
    stray_key = jax.random.fold_in(key, 3)
    pick_key = jax.random.fold_in(key, 4)
    amount_key = jax.random.fold_in(key, 5)
    centers = jax.random.normal(mean_key, ((CLASSES + 1) // 2, D), jnp.float32)
    stray = jax.random.randint(stray_key, (TOKENS,), 0, 5) == 0
    other_class = jax.random.randint(pick_key, (TOKENS,), 0, CLASSES)
    center_index = jnp.where(stray, other_class, chosen) // 2
    row_count = TOKENS // (ROW_DEV * N_COL)
    grid_row = jnp.arange(TOKENS, dtype=jnp.int32) // (ROW_DEV * N_COL)
    region_amount = jax.random.uniform(amount_key, (row_count, 1), jnp.float32, 0.6, 1.6)
    noise_amount = region_amount[grid_row]
    noise = jax.random.normal(noise_key, (TOKENS, D), jnp.float32)
    values = (centers[center_index] + noise * noise_amount) * 0.7
    return jnp.clip(values, -8.0, 8.0).astype(jnp.bfloat16)


def setup_inputs(seed: int = 0) -> dict:
    key_list = jax.random.split(jax.random.key(seed), 3)
    embeddings = draw_embeddings(jax.random.fold_in(key_list[2], 71), 0)
    labels = draw_labels(jax.random.fold_in(key_list[2], 71), 0)
    return {"embeddings": embeddings, "labels": labels}


LOGIT_HEAT_SCALE = 0.1
SHIFT = 10.0

def reference(embeddings, labels):
    widened = embeddings.astype(jnp.float32)
    inverse = lax.rsqrt(lax.optimization_barrier(jnp.sum(widened * widened, axis=1, keepdims=True)) + 1e-06)
    unit_float = widened * inverse
    unit_length_embedding = unit_float.astype(jnp.bfloat16)
    total_rows = unit_length_embedding.shape[0]
    block_size = ROW_DEV * N_COL
    sample_index = jnp.arange(total_rows, dtype=jnp.int32)
    starts = jnp.arange(total_rows // block_size, dtype=jnp.int32) * block_size

    def one_block(carry, block_start):
        target_side_derivative, loss_sum = carry
        reference_embedding_matrix = lax.dynamic_slice_in_dim(unit_length_embedding, block_start, block_size, 0)
        anchor_labels = lax.dynamic_slice_in_dim(labels, block_start, block_size, 0)
        scaled_cosine_matrix = jnp.dot(reference_embedding_matrix, unit_length_embedding.T, preferred_element_type=jnp.float32) / LOGIT_HEAT_SCALE
        anchor_index = block_start + jnp.arange(block_size, dtype=jnp.int32)
        on_diagonal = anchor_index[:, None] == sample_index[None, :]
        weights = jnp.where(on_diagonal, 0.0, jnp.exp(scaled_cosine_matrix - SHIFT))
        positive = jnp.where((anchor_labels[:, None] == labels[None, :]) & ~on_diagonal, 1.0, 0.0).astype(jnp.float32)
        exp_total = lax.optimization_barrier(jnp.sum(weights, axis=1))
        pos_total = lax.optimization_barrier(jnp.sum(positive * scaled_cosine_matrix, axis=1))
        pos_count = lax.optimization_barrier(jnp.sum(positive, axis=1))
        log_total = jnp.log(exp_total) + SHIFT
        divisor = jnp.maximum(pos_count, 1.0)
        anchor_loss = -(pos_total - pos_count * log_total) / divisor
        positive_match_factor = (weights / exp_total[:, None] - positive / divisor[:, None]).astype(jnp.bfloat16)
        source_side_derivative = jnp.dot(positive_match_factor, unit_length_embedding, preferred_element_type=jnp.float32) / LOGIT_HEAT_SCALE
        target_side_derivative = target_side_derivative + jnp.dot(positive_match_factor.T, reference_embedding_matrix, preferred_element_type=jnp.float32) / LOGIT_HEAT_SCALE
        return ((target_side_derivative, loss_sum + jnp.sum(anchor_loss)), source_side_derivative)
    start_carry = (jnp.zeros(unit_length_embedding.shape, jnp.float32), jnp.zeros((), jnp.float32))
    (target_side_derivative, loss_sum), query_parts = lax.scan(one_block, start_carry, starts)
    unit_grad = query_parts.reshape(total_rows, -1) + target_side_derivative
    grad = (unit_grad - unit_float * lax.optimization_barrier(jnp.sum(unit_float * unit_grad, axis=1, keepdims=True))) * inverse
    loss = loss_sum / total_rows
    return (grad, loss)
```

```python
import jax
import jax.numpy as jnp
from jax import lax
from jax.experimental import pallas as pl
from jax.experimental.pallas import tpu as pltpu
from jax.sharding import PartitionSpec as P

F32 = jnp.float32
BF16 = jnp.bfloat16
MESH = pl.DeviceIdType.MESH
LOG2E = 1.4426950408889634
NT = (((1,), (1,)), ((), ()))

BLOCK = 96
HALF = 48
DEPTH = 1024
N_Z = 8
ANCHORS = N_Z * BLOCK
KEYS = 32 * BLOCK
GROUP = 8 * BLOCK
CHUNKS = 4
WIDE = DEPTH // CHUNKS
TOKENS = 24576

A_POS = {0: 0, 7: 1, 1: 2, 6: 3, 2: 4, 5: 5, 3: 6, 4: 7}
K_ORDER = [
    (0, 0), (0, 3), (0, 1), (3, 0),
    (1, 0), (0, 2), (3, 3), (1, 3),
    (3, 1), (1, 1), (2, 0), (3, 2),
    (1, 2), (2, 3), (2, 1), (2, 2),
]
K_POS = {d: i for i, d in enumerate(K_ORDER)}
SHIFTS = (0, 96, 64, 32)
ARRIVALS = [
    ("A", 7, 0), ("A", 1, 0), ("K", 0, 3, 0), ("K", 0, 1, 0), ("K", 3, 0, 0), ("K", 1, 0, 0),
    ("A", 7, 1), ("A", 1, 1), ("K", 0, 3, 1), ("K", 0, 1, 1), ("K", 3, 0, 1), ("K", 1, 0, 1),
    ("K", 0, 2, 0), ("K", 0, 2, 1), ("A", 6, 0), ("A", 2, 0), ("K", 3, 3, 0), ("K", 1, 3, 0),
    ("A", 6, 1), ("A", 2, 1), ("K", 3, 1, 0), ("K", 1, 1, 0), ("K", 3, 3, 1), ("K", 1, 3, 1),
    ("K", 2, 0, 0), ("K", 3, 1, 1), ("K", 1, 1, 1), ("K", 2, 0, 1),
    ("A", 5, 0), ("A", 3, 0), ("A", 5, 1), ("A", 3, 1), ("K", 3, 2, 0), ("K", 1, 2, 0),
    ("K", 2, 3, 0), ("K", 3, 2, 1), ("K", 1, 2, 1), ("K", 2, 3, 1),
    ("A", 4, 0), ("A", 4, 1), ("K", 2, 1, 0), ("K", 2, 1, 1), ("K", 2, 2, 0), ("K", 2, 2, 1),
]


def key_row(core, dq, dp):
    q = K_POS[(dq, dp)]
    return (q // 4) * GROUP + core * (GROUP // 2) + (q % 4) * BLOCK


def key_slot(core, dq, dp):
    return core * 16 + K_POS[(dq, dp)]


class Semaphores:
    def __init__(self):
        self.numbers = {}

    def __call__(self, name):
        return self.numbers.setdefault(name, len(self.numbers))


N_SEM = 260


def kernel(emb, lab, grad, loss,
           au, ku, w, cm, g, uf, inv,
           var, al, kl, labc, klab,
           est, pst, cst, s1o, s1i, s2o, s2i, iec, idc, kev, ke, kie,
           lo, li, sb, rb, send, recv):
    row, z = lax.axis_index("row"), lax.axis_index("col")
    core, x, y = row % 2, (row // 2) % 4, row // 8
    number = Semaphores()
    pending = []

    def chip(dp, dq, other):
        px = (x + dp + core * (dq - dp) + 8) % 4
        py = (y + dq + core * (dp - dq) + 8) % 4
        pc = 1 - core if other else core
        return ((py * 4 + px) * 2 + pc, z)

    def up(dz):
        return (row, (z + dz + 8) % 8)

    def message(name, src, dst, to):
        i = number(name)
        return pltpu.make_async_remote_copy(
            src_ref=src, dst_ref=dst, send_sem=send.at[i], recv_sem=recv.at[i], device_id=to, device_id_type=MESH
        )

    def post(name, src, dst, to):
        copy = message(name, src, dst, to)
        copy.start()
        pending.append(copy)

    def arrived(name, dst):
        message(name, dst, dst, up(1)).wait_recv()

    def a_ref(dz, h):
        return au.at[pl.ds(A_POS[dz] * BLOCK + h * HALF, HALF), :]

    def k_ref(s, dq, dp, h):
        return ku.at[pl.ds(key_row(s, dq, dp) + h * HALF, HALF), :]

    peers = [(s, dq, dp) for s in (0, 1) for dq, dp in K_ORDER if (s, dq, dp) != (0, 0, 0)]

    barrier = pltpu.get_barrier_semaphore()
    for dz in range(1, N_Z):
        pl.semaphore_signal(barrier, inc=1, device_id=up(dz), device_id_type=MESH)
    for s, dq, dp in peers:
        pl.semaphore_signal(barrier, inc=1, device_id=chip(-dp, -dq, s), device_id_type=MESH)

    wide = emb[...].astype(F32)
    scale = lax.rsqrt(jnp.sum(wide * wide, axis=1, keepdims=True) + 1e-6)
    unit = wide * scale
    uf[...] = unit
    inv[...] = jnp.broadcast_to(scale, (BLOCK, 128))
    own = unit.astype(BF16)
    au[pl.ds(0, BLOCK), :] = own
    ku[pl.ds(0, BLOCK), :] = own
    own_label = lab[...].astype(F32)
    al[0] = own_label
    for p, shift in enumerate(SHIFTS):
        var[p] = pltpu.roll(own_label, shift, 1) if shift else own_label
    kl[0] = own_label
    est[...] = jnp.zeros_like(est)
    pst[...] = jnp.zeros_like(pst)
    cst[...] = jnp.zeros_like(cst)
    pl.semaphore_wait(barrier, N_Z - 1 + len(peers))

    def hand_on(what):
        if what[0] == "A":
            _, dz, h = what
            if dz == 0:
                ways = ((1, 7), (-1, 1))
            elif dz in (7, 6) or (dz == 5 and h == 0):
                ways = ((1, dz - 1),)
            elif dz in (1, 2) or (dz == 3 and h == 1):
                ways = ((-1, dz + 1),)
            else:
                ways = ()
            for step, there in ways:
                post(("A", there, h), a_ref(dz, h), a_ref(there, h), up(step))
            return
        _, dq, dp, h = what
        src = k_ref(0, dq, dp, h)
        ways = []
        if dq == 0:
            if dp == 0:
                ways += [(1, 0, 0, 3), (-1, 0, 0, 1)]
            elif dp == 3 and h == 0:
                ways += [(1, 0, 0, 2)]
            elif dp == 1 and h == 1:
                ways += [(-1, 0, 0, 2)]
            ways += [(0, 1, 3, dp), (0, -1, 1, dp)]
        elif dq == 3 and h == 0:
            ways += [(0, 1, 2, dp)]
        elif dq == 1 and h == 1:
            ways += [(0, -1, 2, dp)]
        for tp, tq, nq, np_ in ways:
            post(("K", nq, np_, h), src, k_ref(0, nq, np_, h), chip(tp, tq, False))
        post(("S", dq, dp, h), src, k_ref(1, dq, dp, h), chip(0, 0, True))

    for h in (0, 1):
        hand_on(("A", 0, h))
        hand_on(("K", 0, 0, h))
    for dz in range(1, N_Z):
        post(("L", 8 - dz), al.at[0], al.at[8 - dz], up(dz))
    for s, dq, dp in peers:
        post(("M", s, dq, dp), var.at[K_POS[(dq, dp)] % 4], kl.at[key_slot(s, dq, dp)], chip(-dp, -dq, s))

    lane = lax.broadcasted_iota(jnp.int32, (1, 128), 1)

    def columns(rows):
        stack = jnp.concatenate(list(rows) + [jnp.zeros((128 - N_Z, 128), F32)], axis=0)
        turned = jnp.transpose(stack)
        return [jnp.broadcast_to(turned[:BLOCK, p : p + 1], (BLOCK, 128)) for p in range(N_Z)]

    def key_line(slots, out):
        for s in (0, 1):
            for q in range(4):
                m = [slots[s * 16 + q * 4 + p] for p in range(4)]
                base = q * GROUP + s * (GROUP // 2)
                for t, (cut, a, b) in enumerate(((96, 0, 1), (64, 1, 2), (32, 2, 3))):
                    line = jnp.where(lane < cut, m[a], m[b])
                    out[:, pl.ds(base + t * 128, 128)] = jnp.broadcast_to(line, (8, 128))

    def labels_ready():
        for dz in range(1, N_Z):
            arrived(("L", dz), al.at[dz])
        for s, dq, dp in peers:
            arrived(("M", s, dq, dp), kl.at[key_slot(s, dq, dp)])
        by_pos = sorted(A_POS, key=A_POS.get)
        for p, block in enumerate(columns([al[dz] for dz in by_pos])):
            labc[pl.ds(p * BLOCK, BLOCK), :] = block
        key_line(kl, klab)

    def on_diagonal(rows):
        r = lax.broadcasted_iota(jnp.int32, (rows, 128), 0)
        c = lax.broadcasted_iota(jnp.int32, (rows, 128), 1)
        return (r == c) & (r < BLOCK)

    def score(r0, rows, c0, cols):
        at = pl.ds(r0, rows)
        acc = lax.dot_general(au[at, :], ku[pl.ds(c0, cols), :], NT, preferred_element_type=F32)
        label = labc[at, :]
        total = positive = count = None
        for t in range(cols // 128):
            here = pl.ds(c0 + t * 128, 128)
            s = acc[:, t * 128 : (t + 1) * 128]
            e = jnp.exp2(s * (10.0 * LOG2E) - 10.0 * LOG2E)
            same = label == klab[0:1, here]
            if r0 == 0 and c0 + t == 0:
                diagonal = on_diagonal(rows)
                e = jnp.where(diagonal, 0.0, e)
                same = same & ~diagonal
            w[at, here] = e
            ps, cs = jnp.where(same, s, 0.0), jnp.where(same, 1.0, 0.0)
            if t == 0:
                total, positive, count = e, ps, cs
            else:
                total, positive, count = total + e, positive + ps, count + cs
        est[at, :] += total
        pst[at, :] += positive
        cst[at, :] += count

    def need(r0, rows, c0, cols):
        wants = set()
        for dz, p in A_POS.items():
            if dz and p * BLOCK < r0 + rows and (p + 1) * BLOCK > r0:
                wants |= {("A", dz, 0), ("A", dz, 1)}
        for s in (0, 1):
            for dq, dp in K_ORDER:
                k0 = key_row(s, dq, dp)
                if k0 < c0 + cols and k0 + BLOCK > c0 and (s, dq, dp) != (0, 0, 0):
                    wants |= {("S" if s else "K", dq, dp, h) for h in (0, 1)}
        return wants

    work = []
    for c in range(0, GROUP, 256):
        work.append((0, 480, c, 256))
    for c in range(0, GROUP, 256):
        work.append((0, 480, GROUP + c, 256))
    for c in range(0, 2 * GROUP, 256):
        work.append((480, 288, c, 256))
    for c in range(0, GROUP, 256):
        work.append((0, 768, 2 * GROUP + c, 256))
    for c in range(0, GROUP, 256):
        work.append((0, 768, 3 * GROUP + c, 256))

    seen = set()

    def receive(what):
        if what in seen:
            return
        seen.add(what)
        if what[0] == "A":
            arrived(what, a_ref(what[1], what[2]))
        else:
            arrived(what, k_ref(1 if what[0] == "S" else 0, *what[1:]))
        if what[0] != "S":
            hand_on(what)

    def can_run(wants):
        return all(v in seen for v in wants if v[0] != "S")

    ready = False
    for n, what in enumerate(ARRIVALS):
        receive(what)
        if n == 11:
            labels_ready()
            ready = True
        if ready and work and n < len(ARRIVALS) - 1:
            wants = need(*work[0])
            if can_run(wants) and all(("K",) + v[1:] in set(ARRIVALS[: max(n - 5, 0)]) | {("K", 0, 0, 0), ("K", 0, 0, 1)}
                                      for v in wants if v[0] == "S"):
                for v in sorted(wants - seen):
                    receive(v)
                score(*work.pop(0))
    for job in work:
        for v in sorted(need(*job) - seen):
            receive(v)
        score(*job)

    for dz in (4, 3, 5, 2, 6, 1, 7, 0):
        for i, stat in enumerate((est, pst, cst)):
            part = jnp.transpose(stat[pl.ds(A_POS[dz] * BLOCK, 128), :])
            s1o[dz, i : i + 1, :] = jnp.sum(part, axis=0, keepdims=True)
        if dz:
            post(("T", 8 - dz), s1o.at[dz], s1i.at[8 - dz], up(dz))
    sums = s1o[0]
    for dz in range(1, N_Z):
        arrived(("T", dz), s1i.at[dz])
        sums = sums + s1i[dz]
    real = lane < BLOCK
    exp_total = jnp.where(real, sums[0:1], 1.0)
    pos_total = jnp.where(real, sums[1:2], 0.0) * 10.0
    pos_count = jnp.where(real, sums[2:3], 0.0)
    divisor = jnp.maximum(pos_count, 1.0)
    anchor_loss = -(pos_total - pos_count * (jnp.log(exp_total) + 10.0)) / divisor
    inverse_total = 1.0 / exp_total
    s2o[0:1, :] = inverse_total
    s2o[1:2, :] = 2.0 / divisor
    s2o[2:3, :] = jnp.where(real, anchor_loss, 0.0)
    s2o[3:4, :] = jnp.zeros((1, 128), F32)
    s2i[0] = s2o[...]
    for p, shift in enumerate(SHIFTS):
        kev[p] = pltpu.roll(inverse_total, shift, 1) if shift else inverse_total
    ke[0] = inverse_total
    for dz in range(1, N_Z):
        post(("U", 8 - dz), s2o, s2i.at[8 - dz], up(dz))
    for s, dq, dp in peers:
        post(("V", s, dq, dp), kev.at[K_POS[(dq, dp)] % 4], ke.at[key_slot(s, dq, dp)], chip(-dp, -dq, s))
    for dz in range(1, N_Z):
        arrived(("U", dz), s2i.at[dz])
    by_pos = sorted(A_POS, key=A_POS.get)
    for p, block in enumerate(columns([s2i[dz, 0:1, :] for dz in by_pos])):
        iec[pl.ds(p * BLOCK, BLOCK), :] = block
    for p, block in enumerate(columns([s2i[dz, 1:2, :] for dz in by_pos])):
        idc[pl.ds(p * BLOCK, BLOCK), :] = block
    lo[...] = sum(s2i[dz, 2:3, :] for dz in range(N_Z))
    for s, dq, dp in peers:
        arrived(("V", s, dq, dp), ke.at[key_slot(s, dq, dp)])
    key_line(ke, kie)

    def coupling(c0):
        for r in range(0, ANCHORS, 16):
            at = pl.ds(r, 16)
            ie, d2, label = iec[at, :], idc[at, :], labc[at, :]
            for t in range(GROUP // 128):
                here = pl.ds(c0 + t * 128, 128)
                same = label == klab[0:1, here]
                if c0 + t == 0 and r < BLOCK:
                    i = lax.broadcasted_iota(jnp.int32, (16, 128), 0) + r
                    same = same & (i != lax.broadcasted_iota(jnp.int32, (16, 128), 1))
                v = w[at, here] * (ie + kie[0:1, here]) - jnp.where(same, d2, 0.0)
                cm[at, here] = v.astype(BF16)

    def part(j, dz, lo_, n):
        return g[j, pl.ds(A_POS[dz] * BLOCK + lo_, n), :]

    def push(j, step):
        for way, sign in enumerate((1, -1)):
            dz = (sign * (4 - step)) % 8
            if step == 0:
                at, n = way * HALF, HALF
                value = part(j, dz, at, n)
            else:
                at, n = 0, BLOCK
                value = part(j, dz, 0, BLOCK)
                if step == 1:
                    got = slice(way * HALF, (way + 1) * HALF)
                    arrived(("R", j, way, 0), rb.at[j, way, 0, pl.ds(way * HALF, HALF), :])
                    far = rb[j, way, 0, got, :].astype(F32)
                    pieces = [value[:HALF], value[HALF:]]
                    pieces[way] = pieces[way] + far
                    value = jnp.concatenate(pieces, axis=0)
                else:
                    arrived(("R", j, way, step - 1), rb.at[j, way, step - 1])
                    value = value + rb[j, way, step - 1].astype(F32)
            sb[j, way, step, at : at + n, :] = value.astype(BF16)
            rows = pl.ds(at, n)
            post(("R", j, way, step), sb.at[j, way, step, rows, :], rb.at[j, way, step, rows, :], up(sign))

    def product(j):
        g[j] = jnp.dot(cm[...], ku[:, j * WIDE : (j + 1) * WIDE], preferred_element_type=F32)

    for q in range(4):
        coupling(q * GROUP)
    for n in range(CHUNKS + 3):
        if n < CHUNKS:
            product(n)
            push(n, 0)
        for j in range(min(n - 1, CHUNKS - 1), -1, -1):
            if 0 < n - j < 4:
                push(j, n - j)
        if n == 1:
            for s, dq, dp in peers:
                post(("W", s, dq, dp), lo, li.at[key_slot(s, dq, dp)], chip(-dp, -dq, s))

    every = lo[...]
    for s, dq, dp in peers:
        arrived(("W", s, dq, dp), li.at[key_slot(s, dq, dp)])
        every = every + li[key_slot(s, dq, dp)]
    loss[...] = jnp.broadcast_to(jnp.sum(every, axis=1, keepdims=True) * (1.0 / TOKENS), (1, 128))

    for j in range(CHUNKS):
        value = part(j, 0, 0, BLOCK)
        for way in (0, 1):
            arrived(("R", j, way, 3), rb.at[j, way, 3])
            value = value + rb[j, way, 3].astype(F32)
        g[j, pl.ds(0, BLOCK), :] = value * 10.0
    along = jnp.zeros((BLOCK, 1), F32)
    for j in range(CHUNKS):
        cut = slice(j * WIDE, (j + 1) * WIDE)
        along = along + jnp.sum(uf[:, cut] * g[j, pl.ds(0, BLOCK), :], axis=1, keepdims=True)
    scale = inv[:, 0:1]
    for j in range(CHUNKS):
        cut = slice(j * WIDE, (j + 1) * WIDE)
        grad[:, cut] = (g[j, pl.ds(0, BLOCK), :] - uf[:, cut] * along) * scale

    for copy in pending:
        copy.wait_send()
    assert len(number.numbers) <= N_SEM


def per_device(embeddings, labels):
    vmem = pl.BlockSpec(memory_space=pltpu.VMEM)
    line = jnp.pad(labels, (0, 128 - BLOCK)).reshape(1, 128)
    scratch = [
        ((ANCHORS, DEPTH), BF16),
        ((KEYS, DEPTH), BF16),
        ((ANCHORS, KEYS), F32),
        ((ANCHORS, KEYS), BF16),
        ((CHUNKS, ANCHORS, WIDE), F32),
        ((BLOCK, DEPTH), F32),
        ((BLOCK, 128), F32),
        ((4, 1, 128), F32),
        ((N_Z, 1, 128), F32),
        ((32, 1, 128), F32),
        ((ANCHORS, 128), F32),
        ((8, KEYS), F32),
        ((ANCHORS + 32, 128), F32),
        ((ANCHORS + 32, 128), F32),
        ((ANCHORS + 32, 128), F32),
        ((N_Z, 4, 128), F32),
        ((N_Z, 4, 128), F32),
        ((4, 128), F32),
        ((N_Z, 4, 128), F32),
        ((ANCHORS, 128), F32),
        ((ANCHORS, 128), F32),
        ((4, 1, 128), F32),
        ((32, 1, 128), F32),
        ((8, KEYS), F32),
        ((1, 128), F32),
        ((32, 1, 128), F32),
        ((CHUNKS, 2, 4, BLOCK, WIDE), BF16),
        ((CHUNKS, 2, 4, BLOCK, WIDE), BF16),
    ]
    grad, loss = pl.pallas_call(
        kernel,
        out_shape=(
            jax.ShapeDtypeStruct((BLOCK, DEPTH), F32),
            jax.ShapeDtypeStruct((1, 128), F32),
        ),
        in_specs=[vmem, vmem],
        out_specs=(vmem, vmem),
        scratch_shapes=[pltpu.VMEM(s, t) for s, t in scratch]
        + [pltpu.SemaphoreType.DMA((N_SEM,)), pltpu.SemaphoreType.DMA((N_SEM,))],
        compiler_params=pltpu.CompilerParams(
            collective_id=0, has_side_effects=True, vmem_limit_bytes=60 * 2**20
        ),
        cost_estimate=pl.CostEstimate(flops=2 * 2 * ANCHORS * KEYS * DEPTH, bytes_accessed=2**20, transcendentals=0),
    )(embeddings, line)
    return grad, loss[0, 0]


def solution(mesh):
    placed = (P(("row", "col"), None), P(("row", "col")))
    return jax.shard_map(
        per_device,
        mesh=mesh,
        in_specs=placed,
        out_specs=(P(("row", "col"), None), P()),
        check_vma=False,
    )
```

```python
import jax
import jax.numpy as jnp
from jax import lax
from jax.experimental import pallas as pl
from jax.experimental.pallas import tpu as pltpu
from jax.sharding import PartitionSpec as P

F32 = jnp.float32
BF16 = jnp.bfloat16
MESH = pl.DeviceIdType.MESH
LOG2E = 1.4426950408889634
NT = (((1,), (1,)), ((), ()))

BLOCK = 96
HALF = 48
DEPTH = 1024
N_Z = 8
ANCHORS = N_Z * BLOCK
KEYS = 32 * BLOCK
GROUP = 8 * BLOCK
CHUNKS = 4
WIDE = DEPTH // CHUNKS
TOKENS = 24576

A_POS = {0: 0, 7: 1, 1: 2, 6: 3, 2: 4, 5: 5, 3: 6, 4: 7}
K_ORDER = [
    (0, 0), (0, 3), (0, 1), (3, 0),
    (1, 0), (0, 2), (3, 3), (1, 3),
    (3, 1), (1, 1), (2, 0), (3, 2),
    (1, 2), (2, 3), (2, 1), (2, 2),
]
K_POS = {d: i for i, d in enumerate(K_ORDER)}
SHIFTS = (0, 96, 64, 32)
ARRIVALS = [
    ("A", 7, 0), ("A", 1, 0), ("K", 0, 3, 0), ("K", 0, 1, 0), ("K", 0, 3, 1), ("K", 0, 1, 1),
    ("A", 7, 1), ("A", 1, 1), ("K", 3, 0, 0), ("K", 1, 0, 0), ("K", 3, 0, 1), ("K", 1, 0, 1),
    ("A", 6, 0), ("A", 2, 0), ("K", 3, 1, 0), ("K", 1, 1, 0), ("K", 0, 2, 0), ("K", 0, 2, 1),
    ("K", 3, 3, 0), ("K", 1, 3, 0), ("A", 6, 1), ("A", 2, 1), ("K", 3, 1, 1), ("K", 1, 1, 1),
    ("K", 3, 3, 1), ("K", 1, 3, 1), ("A", 5, 0), ("A", 3, 0), ("K", 2, 0, 0), ("K", 2, 0, 1),
    ("A", 5, 1), ("A", 3, 1), ("K", 3, 2, 0), ("K", 1, 2, 0), ("K", 2, 1, 0), ("K", 3, 2, 1),
    ("K", 1, 2, 1), ("K", 2, 1, 1), ("K", 2, 3, 0), ("K", 2, 3, 1), ("A", 4, 0), ("A", 4, 1),
    ("K", 2, 2, 0), ("K", 2, 2, 1),
]
LABELS_AT = 13
LAG = 6


def key_row(core, dq, dp):
    q = K_POS[(dq, dp)]
    return (q // 4) * GROUP + core * (GROUP // 2) + (q % 4) * BLOCK


def key_slot(core, dq, dp):
    return core * 16 + K_POS[(dq, dp)]


class Semaphores:
    def __init__(self):
        self.numbers = {}

    def __call__(self, name):
        return self.numbers.setdefault(name, len(self.numbers))


N_SEM = 260


def kernel(emb, lab, grad, loss,
           own, au, ku, w, cm, g, uf, inv,
           var, al, kl, labc, klab,
           est, pst, cst, cto, cti, eto, eti, eio, iec, idc, kev, ke, kie,
           lz, lzi, lo, li, sb, rb, load, send, recv):
    row, z = lax.axis_index("row"), lax.axis_index("col")
    core, x, y = row % 2, (row // 2) % 4, row // 8
    number = Semaphores()
    pending = []

    def chip(dp, dq, other):
        px = (x + dp + core * (dq - dp) + 8) % 4
        py = (y + dq + core * (dp - dq) + 8) % 4
        pc = 1 - core if other else core
        return ((py * 4 + px) * 2 + pc, z)

    def up(dz):
        return (row, (z + dz + 8) % 8)

    def message(name, src, dst, to):
        i = number(name)
        return pltpu.make_async_remote_copy(
            src_ref=src, dst_ref=dst, send_sem=send.at[i], recv_sem=recv.at[i], device_id=to, device_id_type=MESH
        )

    def post(name, src, dst, to):
        copy = message(name, src, dst, to)
        copy.start()
        pending.append(copy)

    def arrived(name, dst):
        message(name, dst, dst, up(1)).wait_recv()

    def a_ref(dz, h):
        return au.at[pl.ds(A_POS[dz] * BLOCK + h * HALF, HALF), :]

    def k_ref(s, dq, dp, h):
        return ku.at[pl.ds(key_row(s, dq, dp) + h * HALF, HALF), :]

    peers = [(s, dq, dp) for s in (0, 1) for dq, dp in K_ORDER if (s, dq, dp) != (0, 0, 0)]

    barrier = pltpu.get_barrier_semaphore()
    for dz in range(1, N_Z):
        pl.semaphore_signal(barrier, inc=1, device_id=up(dz), device_id_type=MESH)
    for s, dq, dp in peers:
        pl.semaphore_signal(barrier, inc=1, device_id=chip(-dp, -dq, s), device_id_type=MESH)

    fetch = pltpu.make_async_copy(emb, own, load)
    fetch.start()
    own_label = jnp.zeros((1, 128), F32)
    al[0] = own_label
    al[0, :, 0:BLOCK] = lab[...].astype(F32)
    own_label = al[0]
    for p, shift in enumerate(SHIFTS):
        var[p] = pltpu.roll(own_label, shift, 1) if shift else own_label
    kl[0] = own_label
    est[...] = jnp.zeros_like(est)
    pst[...] = jnp.zeros_like(pst)
    cst[...] = jnp.zeros_like(cst)
    fetch.wait()
    wide = own[...].astype(F32)
    scale = lax.rsqrt(jnp.sum(wide * wide, axis=1, keepdims=True) + 1e-6)
    unit = wide * scale
    uf[...] = unit
    inv[...] = jnp.broadcast_to(scale, (BLOCK, 128))
    rounded = unit.astype(BF16)
    au[pl.ds(0, BLOCK), :] = rounded
    ku[pl.ds(0, BLOCK), :] = rounded
    pl.semaphore_wait(barrier, N_Z - 1 + len(peers))

    def ways_of(what):
        if what[0] == "A":
            _, dz, h = what
            if dz == 0:
                return [(0, 0, 1, 0, ("A", 7, h)), (0, 0, -1, 0, ("A", 1, h))]
            if dz in (7, 6) or (dz == 5 and h == 0):
                return [(0, 0, 1, 0, ("A", dz - 1, h))]
            if dz in (1, 2) or (dz == 3 and h == 1):
                return [(0, 0, -1, 0, ("A", dz + 1, h))]
            return []
        _, dq, dp, h = what
        ways = []
        if (dq, dp) == (0, 0):
            ways += [(1, 0, 0, 0, ("K", 0, 3, h)), (-1, 0, 0, 0, ("K", 0, 1, h))]
        elif (dq, dp, h) == (0, 3, 0):
            ways += [(1, 0, 0, 0, ("K", 0, 2, h))]
        elif (dq, dp, h) == (0, 1, 1):
            ways += [(-1, 0, 0, 0, ("K", 0, 2, h))]
        if dq == 0:
            ways += [(0, 1, 0, 0, ("K", 3, dp, h)), (0, -1, 0, 0, ("K", 1, dp, h))]
        elif dq == 3 and h == 0:
            ways += [(0, 1, 0, 0, ("K", 2, dp, h))]
        elif dq == 1 and h == 1:
            ways += [(0, -1, 0, 0, ("K", 2, dp, h))]
        return ways + [(0, 0, 0, 1, ("S", dq, dp, h))]

    def place(what):
        if what[0] == "A":
            return a_ref(what[1], what[2])
        return k_ref(1 if what[0] == "S" else 0, *what[1:])

    def forward(what, way):
        tp, tq, tz, ts, there = way
        post(there, place(what), place(there), up(tz) if tz else chip(tp, tq, bool(ts)))

    def hand_on(what):
        for way in ways_of(what):
            forward(what, way)

    for axes in ((0, 2), (1,), (3,)):
        for h in (0, 1):
            for what in (("K", 0, 0, h), ("A", 0, h)):
                for way in ways_of(what):
                    if any(way[i] for i in axes):
                        forward(what, way)
    for dz in range(1, N_Z):
        post(("L", 8 - dz), al.at[0], al.at[8 - dz], up(dz))
    for s, dq, dp in peers:
        post(("M", s, dq, dp), var.at[K_POS[(dq, dp)] % 4], kl.at[key_slot(s, dq, dp)], chip(-dp, -dq, s))

    lane = lax.broadcasted_iota(jnp.int32, (1, 128), 1)

    def columns(rows, out):
        turned = jnp.transpose(jnp.concatenate([rows, jnp.zeros((128 - N_Z, 128), F32)], axis=0))
        for dz, p in A_POS.items():
            out[pl.ds(p * BLOCK, BLOCK), :] = jnp.broadcast_to(turned[:BLOCK, dz : dz + 1], (BLOCK, 128))

    def lines(stat, out):
        for dz in range(N_Z):
            part = jnp.transpose(stat[pl.ds(A_POS[dz] * BLOCK, 128), :])
            out[dz : dz + 1, :] = jnp.sum(part, axis=0, keepdims=True)

    def exchange(name, out, into):
        for dz in (4, 3, 5, 2, 6, 1, 7):
            post((name, 8 - dz), out, into.at[8 - dz], up(dz))

    def gathered(name, out, into):
        total = out[...]
        for dz in range(1, N_Z):
            arrived((name, dz), into.at[dz])
            total = total + pltpu.roll(into[dz], dz, 0)
        return total

    def key_line(slots, out):
        for s in (0, 1):
            for q in range(4):
                m = [slots[s * 16 + q * 4 + p] for p in range(4)]
                base = q * GROUP + s * (GROUP // 2)
                for t, (cut, a, b) in enumerate(((96, 0, 1), (64, 1, 2), (32, 2, 3))):
                    line = jnp.where(lane < cut, m[a], m[b])
                    out[:, pl.ds(base + t * 128, 128)] = jnp.broadcast_to(line, (8, 128))

    def labels_ready():
        for dz in range(1, N_Z):
            arrived(("L", dz), al.at[dz])
        for s, dq, dp in peers:
            arrived(("M", s, dq, dp), kl.at[key_slot(s, dq, dp)])
        columns(jnp.concatenate([al[dz] for dz in range(N_Z)], axis=0), labc)
        key_line(kl, klab)

    def count(r0):
        for r in range(r0, r0 + 192, 32):
            label = labc[pl.ds(r, 32), :]
            total = jnp.zeros((32, 128), F32)
            for t in range(KEYS // 128):
                total = total + jnp.where(label == klab[0:1, t * 128 : (t + 1) * 128], 1.0, 0.0)
            cst[pl.ds(r, 32), :] = total
        if r0 == ANCHORS - 192:
            lines(cst, cto)
            exchange("C", cto, cti)

    def counts_ready():
        positives = gathered("C", cto, cti) - 1.0
        cto8 = jnp.where(lane < BLOCK, 2.0 / jnp.maximum(positives, 1.0), 0.0)
        columns(cto8, idc)
        eio[...] = positives[0:1] / jnp.maximum(positives[0:1], 1.0)

    def on_diagonal(rows):
        r = lax.broadcasted_iota(jnp.int32, (rows, 128), 0)
        c = lax.broadcasted_iota(jnp.int32, (rows, 128), 1)
        return (r == c) & (r < BLOCK)

    def score(r0, rows, c0, cols):
        at = pl.ds(r0, rows)
        acc = lax.dot_general(au[at, :], ku[pl.ds(c0, cols), :], NT, preferred_element_type=F32)
        label = labc[at, :]
        total = positive = None
        for t in range(cols // 128):
            here = pl.ds(c0 + t * 128, 128)
            s = acc[:, t * 128 : (t + 1) * 128]
            e = jnp.exp2(s * (10.0 * LOG2E) - 10.0 * LOG2E)
            same = label == klab[0:1, here]
            if r0 == 0 and c0 + t == 0:
                diagonal = on_diagonal(rows)
                e = jnp.where(diagonal, 0.0, e)
                same = same & ~diagonal
            w[at, here] = e
            ps = jnp.where(same, s, 0.0)
            if t == 0:
                total, positive = e, ps
            else:
                total, positive = total + e, positive + ps
        est[at, :] += total
        pst[at, :] += positive

    def need(r0, rows, c0, cols):
        wants = set()
        for dz, p in A_POS.items():
            if dz and p * BLOCK < r0 + rows and (p + 1) * BLOCK > r0:
                wants |= {("A", dz, 0), ("A", dz, 1)}
        for s in (0, 1):
            for dq, dp in K_ORDER:
                k0 = key_row(s, dq, dp)
                if k0 < c0 + cols and k0 + BLOCK > c0 and (s, dq, dp) != (0, 0, 0):
                    wants |= {("S" if s else "K", dq, dp, h) for h in (0, 1)}
        return wants

    work = [("count", r) for r in range(0, ANCHORS, 192)]
    for c in range(0, GROUP, 256):
        work.append((0, 480, c, 256))
    for c in range(0, GROUP, 256):
        work.append((0, 480, GROUP + c, 256))
    work.append(("done",))
    for c in range(0, 2 * GROUP, 256):
        work.append((480, 288, c, 256))
    for c in range(0, 2 * GROUP, 256):
        work.append((0, 768, 2 * GROUP + c, 256))

    seen = set()

    def receive(what):
        if what in seen:
            return
        seen.add(what)
        if what[0] == "A":
            arrived(what, a_ref(what[1], what[2]))
        else:
            arrived(what, k_ref(1 if what[0] == "S" else 0, *what[1:]))
        if what[0] != "S":
            hand_on(what)

    def can_run(wants):
        return all(v in seen for v in wants if v[0] != "S")

    def do(job):
        if job[0] == "count":
            count(job[1])
        elif job[0] == "done":
            counts_ready()
        else:
            for v in sorted(need(*job) - seen):
                receive(v)
            score(*job)

    def can_run(job, n):
        if isinstance(job[0], str):
            return True
        early = set(ARRIVALS[: max(n - LAG, 0)]) | {("K", 0, 0, 0), ("K", 0, 0, 1)}
        return all(v in seen or (v[0] == "S" and ("K",) + v[1:] in early) for v in need(*job))

    for n, what in enumerate(ARRIVALS):
        receive(what)
        if n == LABELS_AT:
            labels_ready()
        if n > LABELS_AT and work and n < len(ARRIVALS) - 1 and can_run(work[0], n):
            do(work.pop(0))
    for job in work:
        do(job)

    lines(est, eto)
    exchange("E", eto, eti)
    real = lane < BLOCK
    totals = jnp.where(real, gathered("E", eto, eti), 1.0)
    inverse_total = 1.0 / totals
    mine = inverse_total[0:1]
    for p, shift in enumerate(SHIFTS):
        kev[p] = pltpu.roll(mine, shift, 1) if shift else mine
    ke[0] = mine
    for s, dq, dp in reversed(peers):
        post(("V", s, dq, dp), kev.at[K_POS[(dq, dp)] % 4], ke.at[key_slot(s, dq, dp)], chip(-dp, -dq, s))
    columns(inverse_total, iec)
    share = jnp.sum(pst[0:ANCHORS, :] * idc[...], axis=0, keepdims=True) * -5.0
    tail = jnp.where(real, eio[...] * (jnp.log(totals[0:1]) + 10.0), 0.0)
    lz[...] = share + tail
    for dz in range(1, N_Z):
        post(("P", 8 - dz), lz, lzi.at[8 - dz], up(dz))
    for s, dq, dp in peers:
        arrived(("V", s, dq, dp), ke.at[key_slot(s, dq, dp)])
    key_line(ke, kie)

    def coupling(r0, rows):
        for r in range(r0, r0 + rows, 16):
            at = pl.ds(r, 16)
            ie, d2, label = iec[at, :], idc[at, :], labc[at, :]
            for c in range(0, KEYS, 128):
                here = pl.ds(c, 128)
                same = label == klab[0:1, here]
                if c == 0 and r < BLOCK:
                    i = lax.broadcasted_iota(jnp.int32, (16, 128), 0) + r
                    same = same & (i != lax.broadcasted_iota(jnp.int32, (16, 128), 1))
                v = w[at, here] * (ie + kie[0:1, here]) - jnp.where(same, d2, 0.0)
                cm[at, here] = v.astype(BF16)

    def product(j, r0, rows):
        at = pl.ds(r0, rows)
        g[j, at, :] = jnp.dot(cm[at, :], ku[:, j * WIDE : (j + 1) * WIDE], preferred_element_type=F32)

    def part(j, dz, first, n):
        return g[j, pl.ds(A_POS[dz] * BLOCK + first, n), :]

    def push(j, step):
        for way, sign in enumerate((1, -1)):
            dz = (sign * (4 - step)) % 8
            at, n = (way * HALF, HALF) if step == 0 else (0, BLOCK)
            value = part(j, dz, at, n)
            rows = pl.ds(at, n)
            if step == 1:
                half = pl.ds(way * HALF, HALF)
                arrived(("R", j, way, 0), rb.at[j, way, 0, half, :])
                pieces = [value[:HALF], value[HALF:]]
                pieces[way] = pieces[way] + rb[j, way, 0, half, :].astype(F32)
                sb[j, way, step, 0:HALF, :] = pieces[0].astype(BF16)
                sb[j, way, step, HALF:BLOCK, :] = pieces[1].astype(BF16)
            else:
                if step > 1:
                    arrived(("R", j, way, step - 1), rb.at[j, way, step - 1])
                    value = value + rb[j, way, step - 1].astype(F32)
                sb[j, way, step, rows, :] = value.astype(BF16)
            post(("R", j, way, step), sb.at[j, way, step, rows, :], rb.at[j, way, step, rows, :], up(sign))

    coupling(672, 96)
    for j in range(CHUNKS):
        product(j, 672, 96)
        push(j, 0)
    coupling(480, 192)
    for j in range(CHUNKS):
        product(j, 480, 192)
    coupling(288, 192)
    for j in range(CHUNKS):
        push(j, 1)
        product(j, 288, 192)
    coupling(96, 192)
    for j in range(CHUNKS):
        product(j, 96, 192)
    coupling(0, 96)
    for j in range(CHUNKS):
        push(j, 2)
        product(j, 0, 96)
    whole = lz[...]
    for dz in range(1, N_Z):
        arrived(("P", dz), lzi.at[dz])
        whole = whole + lzi[dz]
    lo[...] = whole
    for s, dq, dp in peers:
        post(("W", s, dq, dp), lo, li.at[key_slot(s, dq, dp)], chip(-dp, -dq, s))
    for j in range(CHUNKS):
        push(j, 3)

    every = lo[...]
    for s, dq, dp in peers:
        arrived(("W", s, dq, dp), li.at[key_slot(s, dq, dp)])
        every = every + li[key_slot(s, dq, dp)]
    loss[...] = jnp.broadcast_to(jnp.sum(every, axis=1, keepdims=True) * (1.0 / TOKENS), (1, 128))

    along = jnp.zeros((BLOCK, 1), F32)
    for j in range(CHUNKS):
        value = part(j, 0, 0, BLOCK)
        for way in (0, 1):
            arrived(("R", j, way, 3), rb.at[j, way, 3])
            value = value + rb[j, way, 3].astype(F32)
        value = value * 10.0
        g[j, pl.ds(0, BLOCK), :] = value
        along = along + jnp.sum(uf[:, j * WIDE : (j + 1) * WIDE] * value, axis=1, keepdims=True)
    scale = inv[:, 0:1]
    for j in range(CHUNKS):
        cut = slice(j * WIDE, (j + 1) * WIDE)
        grad[:, cut] = (g[j, pl.ds(0, BLOCK), :] - uf[:, cut] * along) * scale

    for copy in pending:
        copy.wait_send()
    assert len(number.numbers) <= N_SEM


def per_device(embeddings, labels):
    vmem = pl.BlockSpec(memory_space=pltpu.VMEM)
    line = labels.reshape(1, BLOCK)
    scratch = [
        ((BLOCK, DEPTH), BF16),
        ((ANCHORS, DEPTH), BF16),
        ((KEYS, DEPTH), BF16),
        ((ANCHORS, KEYS), F32),
        ((ANCHORS, KEYS), BF16),
        ((CHUNKS, ANCHORS, WIDE), F32),
        ((BLOCK, DEPTH), F32),
        ((BLOCK, 128), F32),
        ((4, 1, 128), F32),
        ((N_Z, 1, 128), F32),
        ((32, 1, 128), F32),
        ((ANCHORS, 128), F32),
        ((8, KEYS), F32),
        ((ANCHORS + 32, 128), F32),
        ((ANCHORS + 32, 128), F32),
        ((ANCHORS + 32, 128), F32),
        ((N_Z, 128), F32),
        ((N_Z, N_Z, 128), F32),
        ((N_Z, 128), F32),
        ((N_Z, N_Z, 128), F32),
        ((1, 128), F32),
        ((ANCHORS, 128), F32),
        ((ANCHORS, 128), F32),
        ((4, 1, 128), F32),
        ((32, 1, 128), F32),
        ((8, KEYS), F32),
        ((1, 128), F32),
        ((N_Z, 1, 128), F32),
        ((1, 128), F32),
        ((32, 1, 128), F32),
        ((CHUNKS, 2, 4, BLOCK, WIDE), BF16),
        ((CHUNKS, 2, 4, BLOCK, WIDE), BF16),
    ]
    grad, loss = pl.pallas_call(
        kernel,
        out_shape=(
            jax.ShapeDtypeStruct((BLOCK, DEPTH), F32),
            jax.ShapeDtypeStruct((1, 128), F32),
        ),
        in_specs=[pl.BlockSpec(memory_space=pl.ANY), vmem],
        out_specs=(vmem, vmem),
        scratch_shapes=[pltpu.VMEM(s, t) for s, t in scratch]
        + [pltpu.SemaphoreType.DMA, pltpu.SemaphoreType.DMA((N_SEM,)), pltpu.SemaphoreType.DMA((N_SEM,))],
        compiler_params=pltpu.CompilerParams(
            collective_id=0, has_side_effects=True, vmem_limit_bytes=60 * 2**20
        ),
        cost_estimate=pl.CostEstimate(flops=2 * 2 * ANCHORS * KEYS * DEPTH, bytes_accessed=2**20, transcendentals=0),
    )(embeddings, line)
    return grad, loss[0, 0]


def solution(mesh):
    placed = (P(("row", "col"), None), P(("row", "col")))
    return jax.shard_map(
        per_device,
        mesh=mesh,
        in_specs=placed,
        out_specs=(P(("row", "col"), None), P()),
        check_vma=False,
    )
```

```python
import jax
import jax.numpy as jnp
from jax import lax
from jax.experimental import pallas as pl
from jax.experimental.pallas import tpu as pltpu
from jax.sharding import PartitionSpec as P

F32 = jnp.float32
BF16 = jnp.bfloat16
MESH = pl.DeviceIdType.MESH
LOG2E = 1.4426950408889634
NT = (((1,), (1,)), ((), ()))

BLOCK = 96
HALF = 48
PIECES = 3
PIECE = BLOCK // PIECES
DEPTH = 1024
N_Z = 8
ANCHORS = N_Z * BLOCK
KEYS = 32 * BLOCK
GROUP = 8 * BLOCK
CHUNKS = 4
WIDE = DEPTH // CHUNKS
TOKENS = 24576

A_POS = {0: 0, 7: 1, 1: 2, 6: 3, 2: 4, 5: 5, 3: 6, 4: 7}
K_ORDER = [
    (0, 0), (0, 3), (0, 1), (3, 0),
    (1, 0), (0, 2), (3, 3), (1, 3),
    (3, 1), (1, 1), (2, 0), (3, 2),
    (1, 2), (2, 3), (2, 1), (2, 2),
]
K_POS = {d: i for i, d in enumerate(K_ORDER)}
SHIFTS = (0, 96, 64, 32)
ARRIVALS = [
    ("K", 0, 3, 0), ("K", 0, 1, 0), ("K", 0, 3, 1), ("K", 0, 1, 1), ("A", 7, 0), ("A", 1, 0),
    ("K", 0, 3, 2), ("K", 0, 1, 2), ("K", 3, 0, 0), ("K", 1, 0, 0), ("A", 7, 1), ("A", 1, 1),
    ("K", 3, 0, 1), ("K", 1, 0, 1), ("K", 3, 0, 2), ("K", 1, 0, 2), ("A", 7, 2), ("A", 1, 2),
    ("K", 1, 3, 0), ("K", 0, 2, 0), ("K", 3, 3, 0), ("K", 1, 1, 0), ("K", 3, 1, 0), ("K", 1, 3, 1),
    ("A", 6, 0), ("A", 2, 0), ("K", 3, 3, 1), ("K", 1, 1, 1), ("K", 0, 2, 1), ("K", 3, 1, 1),
    ("A", 6, 1), ("A", 2, 1), ("K", 3, 3, 2), ("K", 1, 3, 2), ("K", 3, 1, 2), ("A", 6, 2),
    ("A", 2, 2), ("K", 0, 2, 2), ("K", 1, 1, 2), ("K", 2, 0, 0), ("K", 2, 0, 1), ("K", 2, 0, 2),
    ("K", 3, 2, 0), ("K", 1, 2, 0), ("K", 2, 3, 0), ("K", 2, 3, 1), ("A", 5, 0), ("A", 3, 0),
    ("K", 2, 1, 0), ("K", 1, 2, 1), ("K", 3, 2, 1), ("K", 2, 3, 2), ("A", 5, 1), ("K", 2, 1, 1),
    ("K", 1, 2, 2), ("K", 3, 2, 2), ("A", 3, 2), ("K", 2, 1, 2), ("A", 3, 1), ("K", 2, 2, 0),
    ("K", 2, 2, 1), ("A", 5, 2), ("K", 2, 2, 2), ("A", 4, 2), ("A", 4, 0), ("A", 4, 1),
]
LABELS_AT = 17
LAG = 9


def key_row(core, dq, dp):
    q = K_POS[(dq, dp)]
    return (q // 4) * GROUP + core * (GROUP // 2) + (q % 4) * BLOCK


def key_slot(core, dq, dp):
    return core * 16 + K_POS[(dq, dp)]


class Semaphores:
    def __init__(self):
        self.numbers = {}

    def __call__(self, name):
        return self.numbers.setdefault(name, len(self.numbers))


N_SEM = 260


def kernel(emb, lab, grad, loss,
           own, au, ku, w, cm, g, uf, inv,
           var, al, kl, labc, klab,
           est, pst, cst, cto, cti, eto, eti, eio, iec, idc, cs, kso, ksi, kvo, kvi, kie,
           lz, lzi, lo, li, sb, rb, load, send, recv):
    row, z = lax.axis_index("row"), lax.axis_index("col")
    core, x, y = row % 2, (row // 2) % 4, row // 8
    number = Semaphores()
    pending = []

    def chip(dp, dq, other):
        px = (x + dp + core * (dq - dp) + 8) % 4
        py = (y + dq + core * (dp - dq) + 8) % 4
        pc = 1 - core if other else core
        return ((py * 4 + px) * 2 + pc, z)

    def up(dz):
        return (row, (z + dz + 8) % 8)

    def message(name, src, dst, to):
        i = number(name)
        return pltpu.make_async_remote_copy(
            src_ref=src, dst_ref=dst, send_sem=send.at[i], recv_sem=recv.at[i], device_id=to, device_id_type=MESH
        )

    def post(name, src, dst, to):
        copy = message(name, src, dst, to)
        copy.start()
        pending.append(copy)

    def arrived(name, dst):
        message(name, dst, dst, up(1)).wait_recv()

    def a_ref(dz, h):
        return au.at[pl.ds(A_POS[dz] * BLOCK + h * PIECE, PIECE), :]

    def k_ref(s, dq, dp, h):
        return ku.at[pl.ds(key_row(s, dq, dp) + h * PIECE, PIECE), :]

    peers = [(s, dq, dp) for s in (0, 1) for dq, dp in K_ORDER if (s, dq, dp) != (0, 0, 0)]

    barrier = pltpu.get_barrier_semaphore()
    for dz in range(1, N_Z):
        pl.semaphore_signal(barrier, inc=1, device_id=up(dz), device_id_type=MESH)
    for s, dq, dp in peers:
        pl.semaphore_signal(barrier, inc=1, device_id=chip(-dp, -dq, s), device_id_type=MESH)

    fetch = pltpu.make_async_copy(emb, own, load)
    fetch.start()
    own_label = jnp.zeros((1, 128), F32)
    al[0] = own_label
    al[0, :, 0:BLOCK] = lab[...].astype(F32)
    own_label = al[0]
    for p, shift in enumerate(SHIFTS):
        var[p] = pltpu.roll(own_label, shift, 1) if shift else own_label
    kl[0] = own_label
    est[...] = jnp.zeros_like(est)
    pst[...] = jnp.zeros_like(pst)
    cst[...] = jnp.zeros_like(cst)
    cs[...] = jnp.zeros_like(cs)
    fetch.wait()
    wide = own[...].astype(F32)
    scale = lax.rsqrt(jnp.sum(wide * wide, axis=1, keepdims=True) + 1e-6)
    unit = wide * scale
    uf[...] = unit
    inv[...] = jnp.broadcast_to(scale, (BLOCK, 128))
    rounded = unit.astype(BF16)
    au[pl.ds(0, BLOCK), :] = rounded
    ku[pl.ds(0, BLOCK), :] = rounded
    pl.semaphore_wait(barrier, N_Z - 1 + len(peers))

    def upward(dp, h):
        return h == 0 or (h == 1 and dp < 2)

    def ways_of(what):
        if what[0] == "A":
            _, dz, h = what
            if dz == 0:
                return [(0, 0, 1, 0, ("A", 7, h)), (0, 0, -1, 0, ("A", 1, h))]
            if dz in (7, 6) or (dz == 5 and upward(0, h)):
                return [(0, 0, 1, 0, ("A", dz - 1, h))]
            if dz in (1, 2) or (dz == 3 and not upward(0, h)):
                return [(0, 0, -1, 0, ("A", dz + 1, h))]
            return []
        _, dq, dp, h = what
        ways = []
        if (dq, dp) == (0, 0):
            ways += [(1, 0, 0, 0, ("K", 0, 3, h)), (-1, 0, 0, 0, ("K", 0, 1, h))]
        elif (dq, dp) == (0, 3) and upward(2, h):
            ways += [(1, 0, 0, 0, ("K", 0, 2, h))]
        elif (dq, dp) == (0, 1) and not upward(2, h):
            ways += [(-1, 0, 0, 0, ("K", 0, 2, h))]
        if dq == 0:
            ways += [(0, 1, 0, 0, ("K", 3, dp, h)), (0, -1, 0, 0, ("K", 1, dp, h))]
        elif dq == 3 and upward(dp, h):
            ways += [(0, 1, 0, 0, ("K", 2, dp, h))]
        elif dq == 1 and not upward(dp, h):
            ways += [(0, -1, 0, 0, ("K", 2, dp, h))]
        return ways + [(0, 0, 0, 1, ("S", dq, dp, h))]

    def place(what):
        if what[0] == "A":
            return a_ref(what[1], what[2])
        return k_ref(1 if what[0] == "S" else 0, *what[1:])

    def forward(what, way):
        tp, tq, tz, ts, there = way
        post(there, place(what), place(there), up(tz) if tz else chip(tp, tq, bool(ts)))

    def hand_on(what):
        for way in ways_of(what):
            forward(what, way)

    for axes in ((0, 2), (1,), (3,)):
        for h in range(PIECES):
            for what in (("K", 0, 0, h), ("A", 0, h)):
                for way in ways_of(what):
                    if any(way[i] for i in axes):
                        forward(what, way)
    for dz in range(1, N_Z):
        post(("L", 8 - dz), al.at[0], al.at[8 - dz], up(dz))
    for s, dq, dp in peers:
        post(("M", s, dq, dp), var.at[K_POS[(dq, dp)] % 4], kl.at[key_slot(s, dq, dp)], chip(-dp, -dq, s))

    lane = lax.broadcasted_iota(jnp.int32, (1, 128), 1)

    def columns(rows, out):
        turned = jnp.transpose(jnp.concatenate([rows, jnp.zeros((128 - N_Z, 128), F32)], axis=0))
        for dz, p in A_POS.items():
            out[pl.ds(p * BLOCK, BLOCK), :] = jnp.broadcast_to(turned[:BLOCK, dz : dz + 1], (BLOCK, 128))

    def lines(stat, out):
        for dz in range(N_Z):
            part = jnp.transpose(stat[pl.ds(A_POS[dz] * BLOCK, 128), :])
            out[dz : dz + 1, :] = jnp.sum(part, axis=0, keepdims=True)

    def exchange(name, out, into):
        for dz in (4, 3, 5, 2, 6, 1, 7):
            post((name, 8 - dz), out, into.at[8 - dz], up(dz))

    def gathered(name, out, into):
        total = out[...]
        for dz in range(1, N_Z):
            arrived((name, dz), into.at[dz])
            total = total + pltpu.roll(into[dz], dz, 0)
        return total

    def key_line(line_of, out):
        for s in (0, 1):
            for q in range(4):
                m = [line_of(s, q * 4 + p) for p in range(4)]
                base = q * GROUP + s * (GROUP // 2)
                for t, (cut, a, b) in enumerate(((96, 0, 1), (64, 1, 2), (32, 2, 3))):
                    line = jnp.where(lane < cut, m[a], m[b])
                    out[:, pl.ds(base + t * 128, 128)] = jnp.broadcast_to(line, (8, 128))

    def labels_ready():
        for dz in range(1, N_Z):
            arrived(("L", dz), al.at[dz])
        for s, dq, dp in peers:
            arrived(("M", s, dq, dp), kl.at[key_slot(s, dq, dp)])
        columns(jnp.concatenate([al[dz] for dz in range(N_Z)], axis=0), labc)
        key_line(lambda s, q: kl[s * 16 + q], klab)

    def count(r0):
        for r in range(r0, r0 + 192, 32):
            label = labc[pl.ds(r, 32), :]
            total = jnp.zeros((32, 128), F32)
            for t in range(KEYS // 128):
                total = total + jnp.where(label == klab[0:1, t * 128 : (t + 1) * 128], 1.0, 0.0)
            cst[pl.ds(r, 32), :] = total
        if r0 == ANCHORS - 192:
            lines(cst, cto)
            exchange("C", cto, cti)

    def counts_ready():
        positives = gathered("C", cto, cti) - 1.0
        cto8 = jnp.where(lane < BLOCK, 2.0 / jnp.maximum(positives, 1.0), 0.0)
        columns(cto8, idc)
        eio[...] = positives[0:1] / jnp.maximum(positives[0:1], 1.0)

    def on_diagonal(rows):
        r = lax.broadcasted_iota(jnp.int32, (rows, 128), 0)
        c = lax.broadcasted_iota(jnp.int32, (rows, 128), 1)
        return (r == c) & (r < BLOCK)

    def score(r0, rows, c0, cols):
        at = pl.ds(r0, rows)
        acc = lax.dot_general(au[at, :], ku[pl.ds(c0, cols), :], NT, preferred_element_type=F32)
        label = labc[at, :]
        total = positive = None
        for t in range(cols // 128):
            here = pl.ds(c0 + t * 128, 128)
            s = acc[:, t * 128 : (t + 1) * 128]
            e = jnp.exp2(s * (10.0 * LOG2E) - 10.0 * LOG2E)
            same = label == klab[0:1, here]
            if r0 == 0 and c0 + t == 0:
                diagonal = on_diagonal(rows)
                e = jnp.where(diagonal, 0.0, e)
                same = same & ~diagonal
            w[at, here] = e
            cs[:, here] += jnp.sum(e.reshape(rows // 8, 8, 128), axis=0)
            ps = jnp.where(same, s, 0.0)
            if t == 0:
                total, positive = e, ps
            else:
                total, positive = total + e, positive + ps
        est[at, :] += total
        pst[at, :] += positive

    def need(r0, rows, c0, cols):
        wants = set()
        for dz, p in A_POS.items():
            if dz and p * BLOCK < r0 + rows and (p + 1) * BLOCK > r0:
                wants |= {("A", dz, h) for h in range(PIECES)}
        for s in (0, 1):
            for dq, dp in K_ORDER:
                k0 = key_row(s, dq, dp)
                if k0 < c0 + cols and k0 + BLOCK > c0 and (s, dq, dp) != (0, 0, 0):
                    wants |= {("S" if s else "K", dq, dp, h) for h in range(PIECES)}
        return wants

    work = [("count", r) for r in range(0, ANCHORS, 192)]
    for c in range(0, GROUP, 256):
        work.append((0, 480, c, 256))
    for c in range(0, GROUP, 256):
        work.append((0, 480, GROUP + c, 256))
    work.append(("done",))
    for c in range(0, 2 * GROUP, 256):
        work.append((480, 288, c, 256))
    for c in range(0, 2 * GROUP, 256):
        work.append((0, 768, 2 * GROUP + c, 256))

    seen = set()

    def receive(what):
        if what in seen:
            return
        seen.add(what)
        if what[0] == "A":
            arrived(what, a_ref(what[1], what[2]))
        else:
            arrived(what, k_ref(1 if what[0] == "S" else 0, *what[1:]))
        if what[0] != "S":
            hand_on(what)

    def can_run(wants):
        return all(v in seen for v in wants if v[0] != "S")

    def do(job):
        if job[0] == "count":
            count(job[1])
        elif job[0] == "done":
            counts_ready()
        else:
            for v in sorted(need(*job) - seen):
                receive(v)
            score(*job)

    def can_run(job, n):
        if isinstance(job[0], str):
            return True
        early = set(ARRIVALS[: max(n - LAG, 0)]) | {("K", 0, 0, h) for h in range(PIECES)}
        return all(v in seen or (v[0] == "S" and ("K",) + v[1:] in early) for v in need(*job))

    for n, what in enumerate(ARRIVALS):
        receive(what)
        if n == LABELS_AT:
            labels_ready()
        if n > LABELS_AT and work and n < len(ARRIVALS) - 1 and can_run(work[0], n):
            do(work.pop(0))
    for job in work:
        do(job)

    tiles = [jnp.sum(cs[:, t * 128 : (t + 1) * 128], axis=0, keepdims=True) for t in range(KEYS // 128)]
    for s in (0, 1):
        for dq, dp in K_ORDER:
            t, off = divmod(key_row(s, dq, dp), 128)
            line = tiles[t]
            if off:
                line = pltpu.roll(line, 128 - off, 1)
                if off + BLOCK > 128:
                    line = jnp.where(lane < 128 - off, line, pltpu.roll(tiles[t + 1], 128 - off, 1))
            r = s * 16 + dq * 4 + dp
            kso[r : r + 1, :] = line
    post(("X",), kso, ksi, chip(0, 0, True))
    lines(est, eto)
    exchange("E", eto, eti)
    arrived(("X",), ksi)
    both = [kso[0:16, :] + ksi[16:32, :], kso[16:32, :] + ksi[0:16, :]]
    kvo[0:16, :] = both[0].astype(BF16)
    kvo[16:32, :] = both[1].astype(BF16)
    plane = [(dq, dp) for dq, dp in reversed(K_ORDER) if (dq, dp) != (0, 0)]
    for dq, dp in plane:
        post(("V", dq, dp), kvo, kvi.at[dq * 4 + dp], chip(-dp, -dq, False))
    real = lane < BLOCK
    totals = jnp.where(real, gathered("E", eto, eti), 1.0)
    inverse_total = 1.0 / totals
    columns(inverse_total, iec)
    share = jnp.sum(pst[0:ANCHORS, :] * idc[...], axis=0, keepdims=True) * -5.0
    tail = jnp.where(real, eio[...] * (jnp.log(totals[0:1]) + 10.0), 0.0)
    lz[...] = share + tail
    for dz in range(1, N_Z):
        post(("P", 8 - dz), lz, lzi.at[8 - dz], up(dz))
    for dq, dp in plane:
        arrived(("V", dq, dp), kvi.at[dq * 4 + dp])
    within = lax.broadcasted_iota(jnp.int32, (16, 128), 0) % 4
    turned = []
    for s in (0, 1):
        total = both[s]
        for b in range(4):
            by_q = None
            for a in range(4):
                dq, dp = (b, a) if s else (a, b)
                if (dq, dp) == (0, 0):
                    continue
                value = kvi[dq * 4 + dp, s * 16 : s * 16 + 16, :].astype(F32)
                if a:
                    value = pltpu.roll(value, 4 * a, 0)
                by_q = value if by_q is None else by_q + value
            if b:
                by_q = jnp.where(within < b, pltpu.roll(by_q, 12 + b, 0), pltpu.roll(by_q, b, 0))
            total = total + by_q
        inverse = 1.0 / total
        turned.append([pltpu.roll(inverse, shift, 1) if shift else inverse for shift in SHIFTS])

    def inverse_line(s, q):
        dq, dp = K_ORDER[q]
        r = dq * 4 + dp
        return turned[s][q % 4][r : r + 1, :]

    key_line(inverse_line, kie)

    def coupling(r0, rows):
        for r in range(r0, r0 + rows, 16):
            at = pl.ds(r, 16)
            ie, d2, label = iec[at, :], idc[at, :], labc[at, :]
            for c in range(0, KEYS, 128):
                here = pl.ds(c, 128)
                same = label == klab[0:1, here]
                if c == 0 and r < BLOCK:
                    i = lax.broadcasted_iota(jnp.int32, (16, 128), 0) + r
                    same = same & (i != lax.broadcasted_iota(jnp.int32, (16, 128), 1))
                v = w[at, here] * (ie + kie[0:1, here]) - jnp.where(same, d2, 0.0)
                cm[at, here] = v.astype(BF16)

    def product(j, r0, rows):
        at = pl.ds(r0, rows)
        g[j, at, :] = jnp.dot(cm[at, :], ku[:, j * WIDE : (j + 1) * WIDE], preferred_element_type=F32)

    def part(j, dz, first, n):
        return g[j, pl.ds(A_POS[dz] * BLOCK + first, n), :]

    def push(j, step):
        for way, sign in enumerate((1, -1)):
            dz = (sign * (4 - step)) % 8
            at, n = (way * HALF, HALF) if step == 0 else (0, BLOCK)
            value = part(j, dz, at, n)
            rows = pl.ds(at, n)
            if step == 1:
                half = pl.ds(way * HALF, HALF)
                arrived(("R", j, way, 0), rb.at[j, way, 0, half, :])
                pieces = [value[:HALF], value[HALF:]]
                pieces[way] = pieces[way] + rb[j, way, 0, half, :].astype(F32)
                sb[j, way, step, 0:HALF, :] = pieces[0].astype(BF16)
                sb[j, way, step, HALF:BLOCK, :] = pieces[1].astype(BF16)
            else:
                if step > 1:
                    arrived(("R", j, way, step - 1), rb.at[j, way, step - 1])
                    value = value + rb[j, way, step - 1].astype(F32)
                sb[j, way, step, rows, :] = value.astype(BF16)
            post(("R", j, way, step), sb.at[j, way, step, rows, :], rb.at[j, way, step, rows, :], up(sign))

    coupling(672, 96)
    for j in range(CHUNKS):
        product(j, 672, 96)
        push(j, 0)
    coupling(480, 192)
    for j in range(CHUNKS):
        product(j, 480, 192)
    coupling(288, 192)
    for j in range(CHUNKS):
        push(j, 1)
        product(j, 288, 192)
    coupling(96, 192)
    for j in range(CHUNKS):
        product(j, 96, 192)
    coupling(0, 96)
    for j in range(CHUNKS):
        push(j, 2)
        product(j, 0, 96)
    whole = lz[...]
    for dz in range(1, N_Z):
        arrived(("P", dz), lzi.at[dz])
        whole = whole + lzi[dz]
    lo[...] = whole
    for s, dq, dp in peers:
        post(("W", s, dq, dp), lo, li.at[key_slot(s, dq, dp)], chip(-dp, -dq, s))
    for j in range(CHUNKS):
        push(j, 3)

    every = lo[...]
    for s, dq, dp in peers:
        arrived(("W", s, dq, dp), li.at[key_slot(s, dq, dp)])
        every = every + li[key_slot(s, dq, dp)]
    loss[...] = jnp.broadcast_to(jnp.sum(every, axis=1, keepdims=True) * (1.0 / TOKENS), (1, 128))

    along = jnp.zeros((BLOCK, 1), F32)
    for j in range(CHUNKS):
        value = part(j, 0, 0, BLOCK)
        for way in (0, 1):
            arrived(("R", j, way, 3), rb.at[j, way, 3])
            value = value + rb[j, way, 3].astype(F32)
        value = value * 10.0
        g[j, pl.ds(0, BLOCK), :] = value
        along = along + jnp.sum(uf[:, j * WIDE : (j + 1) * WIDE] * value, axis=1, keepdims=True)
    scale = inv[:, 0:1]
    for j in range(CHUNKS):
        cut = slice(j * WIDE, (j + 1) * WIDE)
        grad[:, cut] = (g[j, pl.ds(0, BLOCK), :] - uf[:, cut] * along) * scale

    for copy in pending:
        copy.wait_send()
    assert len(number.numbers) <= N_SEM


def per_device(embeddings, labels):
    vmem = pl.BlockSpec(memory_space=pltpu.VMEM)
    line = labels.reshape(1, BLOCK)
    scratch = [
        ((BLOCK, DEPTH), BF16),
        ((ANCHORS, DEPTH), BF16),
        ((KEYS, DEPTH), BF16),
        ((ANCHORS, KEYS), F32),
        ((ANCHORS, KEYS), BF16),
        ((CHUNKS, ANCHORS, WIDE), F32),
        ((BLOCK, DEPTH), F32),
        ((BLOCK, 128), F32),
        ((4, 1, 128), F32),
        ((N_Z, 1, 128), F32),
        ((32, 1, 128), F32),
        ((ANCHORS, 128), F32),
        ((8, KEYS), F32),
        ((ANCHORS + 32, 128), F32),
        ((ANCHORS + 32, 128), F32),
        ((ANCHORS + 32, 128), F32),
        ((N_Z, 128), F32),
        ((N_Z, N_Z, 128), F32),
        ((N_Z, 128), F32),
        ((N_Z, N_Z, 128), F32),
        ((1, 128), F32),
        ((ANCHORS, 128), F32),
        ((ANCHORS, 128), F32),
        ((8, KEYS), F32),
        ((32, 128), F32),
        ((32, 128), F32),
        ((32, 128), BF16),
        ((16, 32, 128), BF16),
        ((8, KEYS), F32),
        ((1, 128), F32),
        ((N_Z, 1, 128), F32),
        ((1, 128), F32),
        ((32, 1, 128), F32),
        ((CHUNKS, 2, 4, BLOCK, WIDE), BF16),
        ((CHUNKS, 2, 4, BLOCK, WIDE), BF16),
    ]
    grad, loss = pl.pallas_call(
        kernel,
        out_shape=(
            jax.ShapeDtypeStruct((BLOCK, DEPTH), F32),
            jax.ShapeDtypeStruct((1, 128), F32),
        ),
        in_specs=[pl.BlockSpec(memory_space=pltpu.HBM), vmem],
        out_specs=(vmem, vmem),
        scratch_shapes=[pltpu.VMEM(s, t) for s, t in scratch]
        + [pltpu.SemaphoreType.DMA, pltpu.SemaphoreType.DMA((N_SEM,)), pltpu.SemaphoreType.DMA((N_SEM,))],
        compiler_params=pltpu.CompilerParams(
            collective_id=0, has_side_effects=True, vmem_limit_bytes=44 * 2**20
        ),
        cost_estimate=pl.CostEstimate(flops=2 * 2 * ANCHORS * KEYS * DEPTH, bytes_accessed=2**20, transcendentals=0),
    )(embeddings, line)
    return grad, loss[0, 0]


def solution(mesh):
    placed = (P(("row", "col"), None), P(("row", "col")))
    return jax.shard_map(
        per_device,
        mesh=mesh,
        in_specs=placed,
        out_specs=(P(("row", "col"), None), P()),
        check_vma=False,
    )
```

```python
import jax
import jax.numpy as jnp
from jax import lax
from jax.experimental import pallas as pl
from jax.experimental.pallas import tpu as pltpu
from jax.sharding import PartitionSpec as P

F32 = jnp.float32
BF16 = jnp.bfloat16
MESH = pl.DeviceIdType.MESH
LOG2E = 1.4426950408889634
NT = (((1,), (1,)), ((), ()))

BLOCK = 96
HALF = 48
PIECES = 3
PIECE = BLOCK // PIECES
DEPTH = 1024
N_Z = 8
ANCHORS = N_Z * BLOCK
KEYS = 32 * BLOCK
GROUP = 8 * BLOCK
CHUNKS = 4
WIDE = DEPTH // CHUNKS
TOKENS = 24576

A_POS = {0: 0, 7: 1, 1: 2, 6: 3, 2: 4, 5: 5, 3: 6, 4: 7}
K_ORDER = [
    (0, 0), (0, 3), (0, 1), (3, 0),
    (1, 0), (3, 3), (1, 3), (3, 1),
    (0, 2), (1, 1), (2, 0), (2, 3),
    (1, 2), (3, 2), (2, 1), (2, 2),
]
K_POS = {d: i for i, d in enumerate(K_ORDER)}
SHIFTS = (0, 96, 64, 32)
ARRIVALS = [
    ("K", 0, 3, 0), ("K", 0, 1, 0), ("K", 0, 3, 1), ("K", 0, 1, 1), ("A", 7, 0), ("A", 1, 0),
    ("K", 0, 3, 2), ("K", 0, 1, 2), ("K", 3, 0, 0), ("K", 1, 0, 0), ("A", 7, 1), ("A", 1, 1),
    ("K", 3, 0, 1), ("K", 1, 0, 1), ("K", 3, 0, 2), ("K", 1, 0, 2), ("A", 7, 2), ("A", 1, 2),
    ("K", 1, 3, 0), ("K", 0, 2, 0), ("K", 3, 3, 0), ("K", 1, 1, 0), ("K", 3, 1, 0), ("K", 1, 3, 1),
    ("A", 6, 0), ("A", 2, 0), ("K", 3, 3, 1), ("K", 1, 1, 1), ("K", 0, 2, 1), ("K", 3, 1, 1),
    ("A", 6, 1), ("A", 2, 1), ("K", 3, 3, 2), ("K", 1, 3, 2), ("K", 3, 1, 2), ("A", 6, 2),
    ("A", 2, 2), ("K", 0, 2, 2), ("K", 1, 1, 2), ("K", 2, 0, 0), ("K", 2, 0, 1), ("K", 2, 0, 2),
    ("K", 3, 2, 0), ("K", 1, 2, 0), ("K", 2, 3, 0), ("K", 2, 3, 1), ("A", 5, 0), ("A", 3, 0),
    ("K", 2, 1, 0), ("K", 1, 2, 1), ("K", 3, 2, 1), ("K", 2, 3, 2), ("A", 5, 1), ("A", 3, 1),
    ("K", 2, 1, 1), ("K", 1, 2, 2), ("K", 3, 2, 2), ("A", 3, 2), ("A", 5, 2), ("K", 2, 1, 2),
    ("K", 2, 2, 0), ("K", 2, 2, 1), ("K", 2, 2, 2), ("A", 4, 2), ("A", 4, 0), ("A", 4, 1),
]
LABELS_AT = 17
JOBS_AFTER = {
    17: (0,), 18: (1, 2), 21: (3, 4), 25: (5,), 26: (6,), 36: (7, 8, 9, 11), 41: (12, 13), 44: (10,), 58: (14,), 59: (15, 16, 17), 60: (18, 19, 20), 61: (21, 22), 62: (23, 24),
}


def key_row(core, dq, dp):
    q = K_POS[(dq, dp)]
    return (q // 4) * GROUP + core * (GROUP // 2) + (q % 4) * BLOCK


def key_slot(core, dq, dp):
    return core * 16 + K_POS[(dq, dp)]


class Semaphores:
    def __init__(self):
        self.numbers = {}

    def __call__(self, name):
        return self.numbers.setdefault(name, len(self.numbers))


N_SEM = 260


def kernel(emb, lab, grad, loss,
           own, own_line, au, ku, w, cm, g, uf, inv,
           var, al, kl, labc, klab,
           est, pst, cst, cto, cti, eto, eti, eio, iec, idc, cs, kso, ksi, kvo, kvi, kie,
           lz, lzi, lo, li, sb, rb, load, send, recv):
    row, z = lax.axis_index("row"), lax.axis_index("col")
    core, x, y = row % 2, (row // 2) % 4, row // 8
    number = Semaphores()
    pending = []

    def chip(dp, dq, other):
        px = (x + dp + core * (dq - dp) + 8) % 4
        py = (y + dq + core * (dp - dq) + 8) % 4
        pc = 1 - core if other else core
        return ((py * 4 + px) * 2 + pc, z)

    def up(dz):
        return (row, (z + dz + 8) % 8)

    def message(name, src, dst, to):
        i = number(name)
        return pltpu.make_async_remote_copy(
            src_ref=src, dst_ref=dst, send_sem=send.at[i], recv_sem=recv.at[i], device_id=to, device_id_type=MESH
        )

    def post(name, src, dst, to):
        copy = message(name, src, dst, to)
        copy.start()
        pending.append(copy)

    def arrived(name, dst):
        message(name, dst, dst, up(1)).wait_recv()

    def a_ref(dz, h):
        return au.at[pl.ds(A_POS[dz] * BLOCK + h * PIECE, PIECE), :]

    def k_ref(s, dq, dp, h):
        return ku.at[pl.ds(key_row(s, dq, dp) + h * PIECE, PIECE), :]

    peers = [(s, dq, dp) for s in (0, 1) for dq, dp in K_ORDER if (s, dq, dp) != (0, 0, 0)]

    barrier = pltpu.get_barrier_semaphore()
    for dz in range(1, N_Z):
        pl.semaphore_signal(barrier, inc=1, device_id=up(dz), device_id_type=MESH)
    for s, dq, dp in peers:
        pl.semaphore_signal(barrier, inc=1, device_id=chip(-dp, -dq, s), device_id_type=MESH)

    fetch = pltpu.make_async_copy(emb, own, load.at[0])
    fetch.start()
    fetch_line = pltpu.make_async_copy(lab, own_line, load.at[1])
    fetch_line.start()
    est[...] = jnp.zeros_like(est)
    pst[...] = jnp.zeros_like(pst)
    cst[...] = jnp.zeros_like(cst)
    cs[...] = jnp.zeros_like(cs)
    al[0] = jnp.zeros((1, 128), F32)
    fetch_line.wait()
    al[0, :, 0:BLOCK] = own_line[...].astype(F32)
    own_label = al[0]
    for p, shift in enumerate(SHIFTS):
        var[p] = pltpu.roll(own_label, shift, 1) if shift else own_label
    kl[0] = own_label
    fetch.wait()
    wide = own[...].astype(F32)
    scale = lax.rsqrt(jnp.sum(wide * wide, axis=1, keepdims=True) + 1e-6)
    unit = wide * scale
    uf[...] = unit
    inv[...] = jnp.broadcast_to(scale, (BLOCK, 128))
    rounded = unit.astype(BF16)
    au[pl.ds(0, BLOCK), :] = rounded
    ku[pl.ds(0, BLOCK), :] = rounded
    pl.semaphore_wait(barrier, N_Z - 1 + len(peers))

    def upward(dp, h):
        return h == 0 or (h == 1 and dp < 2)

    def ways_of(what):
        if what[0] == "A":
            _, dz, h = what
            if dz == 0:
                return [(0, 0, 1, 0, ("A", 7, h)), (0, 0, -1, 0, ("A", 1, h))]
            if dz in (7, 6) or (dz == 5 and upward(0, h)):
                return [(0, 0, 1, 0, ("A", dz - 1, h))]
            if dz in (1, 2) or (dz == 3 and not upward(0, h)):
                return [(0, 0, -1, 0, ("A", dz + 1, h))]
            return []
        _, dq, dp, h = what
        ways = []
        if (dq, dp) == (0, 0):
            ways += [(1, 0, 0, 0, ("K", 0, 3, h)), (-1, 0, 0, 0, ("K", 0, 1, h))]
        elif (dq, dp) == (0, 3) and upward(2, h):
            ways += [(1, 0, 0, 0, ("K", 0, 2, h))]
        elif (dq, dp) == (0, 1) and not upward(2, h):
            ways += [(-1, 0, 0, 0, ("K", 0, 2, h))]
        if dq == 0:
            ways += [(0, 1, 0, 0, ("K", 3, dp, h)), (0, -1, 0, 0, ("K", 1, dp, h))]
        elif dq == 3 and upward(dp, h):
            ways += [(0, 1, 0, 0, ("K", 2, dp, h))]
        elif dq == 1 and not upward(dp, h):
            ways += [(0, -1, 0, 0, ("K", 2, dp, h))]
        return ways + [(0, 0, 0, 1, ("S", dq, dp, h))]

    def place(what):
        if what[0] == "A":
            return a_ref(what[1], what[2])
        return k_ref(1 if what[0] == "S" else 0, *what[1:])

    def forward(what, way):
        tp, tq, tz, ts, there = way
        post(there, place(what), place(there), up(tz) if tz else chip(tp, tq, bool(ts)))

    def hand_on(what):
        for way in ways_of(what):
            forward(what, way)

    for axes in ((0, 2), (1,), (3,)):
        for h in range(PIECES):
            for what in (("K", 0, 0, h), ("A", 0, h)):
                for way in ways_of(what):
                    if any(way[i] for i in axes):
                        forward(what, way)
    for dz in range(1, N_Z):
        post(("L", 8 - dz), al.at[0], al.at[8 - dz], up(dz))
    for s, dq, dp in peers:
        post(("M", s, dq, dp), var.at[K_POS[(dq, dp)] % 4], kl.at[key_slot(s, dq, dp)], chip(-dp, -dq, s))

    lane = lax.broadcasted_iota(jnp.int32, (1, 128), 1)

    def columns(rows, out):
        turned = jnp.transpose(jnp.concatenate([rows, jnp.zeros((128 - N_Z, 128), F32)], axis=0))
        for dz, p in A_POS.items():
            out[pl.ds(p * BLOCK, BLOCK), :] = jnp.broadcast_to(turned[:BLOCK, dz : dz + 1], (BLOCK, 128))

    def lines(stat, out):
        for dz in range(N_Z):
            part = jnp.transpose(stat[pl.ds(A_POS[dz] * BLOCK, 128), :])
            out[dz : dz + 1, :] = jnp.sum(part, axis=0, keepdims=True)

    def exchange(name, out, into):
        for dz in (4, 3, 5, 2, 6, 1, 7):
            post((name, 8 - dz), out, into.at[8 - dz], up(dz))

    def gathered(name, out, into):
        total = out[...]
        for dz in range(1, N_Z):
            arrived((name, dz), into.at[dz])
            total = total + pltpu.roll(into[dz], dz, 0)
        return total

    def key_line(line_of, out):
        for s in (0, 1):
            for q in range(4):
                m = [line_of(s, q * 4 + p) for p in range(4)]
                base = q * GROUP + s * (GROUP // 2)
                for t, (cut, a, b) in enumerate(((96, 0, 1), (64, 1, 2), (32, 2, 3))):
                    line = jnp.where(lane < cut, m[a], m[b])
                    out[:, pl.ds(base + t * 128, 128)] = jnp.broadcast_to(line, (8, 128))

    def labels_ready():
        for dz in range(1, N_Z):
            arrived(("L", dz), al.at[dz])
        for s, dq, dp in peers:
            arrived(("M", s, dq, dp), kl.at[key_slot(s, dq, dp)])
        columns(jnp.concatenate([al[dz] for dz in range(N_Z)], axis=0), labc)
        key_line(lambda s, q: kl[s * 16 + q], klab)

    def count(r0):
        for r in range(r0, r0 + 192, 32):
            label = labc[pl.ds(r, 32), :]
            total = jnp.zeros((32, 128), F32)
            for t in range(KEYS // 128):
                total = total + jnp.where(label == klab[0:1, t * 128 : (t + 1) * 128], 1.0, 0.0)
            cst[pl.ds(r, 32), :] = total
        if r0 == ANCHORS - 192:
            lines(cst, cto)
            exchange("C", cto, cti)

    def counts_ready():
        positives = gathered("C", cto, cti) - 1.0
        cto8 = jnp.where(lane < BLOCK, 2.0 / jnp.maximum(positives, 1.0), 0.0)
        columns(cto8, idc)
        eio[...] = positives[0:1] / jnp.maximum(positives[0:1], 1.0)

    def on_diagonal(rows):
        r = lax.broadcasted_iota(jnp.int32, (rows, 128), 0)
        c = lax.broadcasted_iota(jnp.int32, (rows, 128), 1)
        return (r == c) & (r < BLOCK)

    def score(r0, rows, c0, cols):
        at = pl.ds(r0, rows)
        acc = lax.dot_general(au[at, :], ku[pl.ds(c0, cols), :], NT, preferred_element_type=F32)
        label = labc[at, :]
        total = positive = None
        for t in range(cols // 128):
            here = pl.ds(c0 + t * 128, 128)
            s = acc[:, t * 128 : (t + 1) * 128]
            e = jnp.exp2(s * (10.0 * LOG2E) - 10.0 * LOG2E)
            same = label == klab[0:1, here]
            if r0 == 0 and c0 + t == 0:
                diagonal = on_diagonal(rows)
                e = jnp.where(diagonal, 0.0, e)
                same = same & ~diagonal
            w[at, here] = e
            cs[:, here] += jnp.sum(e.reshape(rows // 8, 8, 128), axis=0)
            ps = jnp.where(same, s, 0.0)
            if t == 0:
                total, positive = e, ps
            else:
                total, positive = total + e, positive + ps
        est[at, :] += total
        pst[at, :] += positive

    def need(r0, rows, c0, cols):
        wants = set()
        for dz, p in A_POS.items():
            if dz and p * BLOCK < r0 + rows and (p + 1) * BLOCK > r0:
                wants |= {("A", dz, h) for h in range(PIECES)}
        for s in (0, 1):
            for dq, dp in K_ORDER:
                k0 = key_row(s, dq, dp)
                if k0 < c0 + cols and k0 + BLOCK > c0 and (s, dq, dp) != (0, 0, 0):
                    wants |= {("S" if s else "K", dq, dp, h) for h in range(PIECES)}
        return wants

    work = [("count", r) for r in range(0, ANCHORS, 192)]
    for r0, rows, c0, c1, wide in (
        (0, 288, 0, GROUP, 256),
        (288, 192, 0, GROUP, 256),
        (0, 480, GROUP, 2 * GROUP, 256),
        (480, 192, 0, 2 * GROUP, 256),
        (0, 672, 2 * GROUP, 3 * GROUP, 256),
        (0, 672, 3 * GROUP, 3 * GROUP + 512, 256),
        (672, 96, 0, 3 * GROUP, GROUP),
        (0, 672, 3 * GROUP + 512, 4 * GROUP, 256),
        (672, 96, 3 * GROUP, 4 * GROUP, GROUP),
    ):
        work += [(r0, rows, c, wide) for c in range(c0, c1, wide)]
    work.insert(10, ("done",))

    seen = set()

    def receive(what):
        if what in seen:
            return
        seen.add(what)
        if what[0] == "A":
            arrived(what, a_ref(what[1], what[2]))
        else:
            arrived(what, k_ref(1 if what[0] == "S" else 0, *what[1:]))
        if what[0] != "S":
            hand_on(what)

    def can_run(wants):
        return all(v in seen for v in wants if v[0] != "S")

    def do(job):
        if job[0] == "count":
            count(job[1])
        elif job[0] == "done":
            counts_ready()
        else:
            for v in sorted(need(*job) - seen):
                receive(v)
            score(*job)

    left = list(range(len(work)))
    for n, what in enumerate(ARRIVALS):
        receive(what)
        if n == LABELS_AT:
            labels_ready()
        for i in JOBS_AFTER.get(n, ()):
            do(work[i])
            left.remove(i)
    for i in left:
        do(work[i])

    tiles = [jnp.sum(cs[:, t * 128 : (t + 1) * 128], axis=0, keepdims=True) for t in range(KEYS // 128)]
    for s in (0, 1):
        for dq, dp in K_ORDER:
            t, off = divmod(key_row(s, dq, dp), 128)
            line = tiles[t]
            if off:
                line = pltpu.roll(line, 128 - off, 1)
                if off + BLOCK > 128:
                    line = jnp.where(lane < 128 - off, line, pltpu.roll(tiles[t + 1], 128 - off, 1))
            r = s * 16 + dq * 4 + dp
            kso[r : r + 1, :] = line
    post(("X",), kso, ksi, chip(0, 0, True))
    lines(est, eto)
    exchange("E", eto, eti)
    arrived(("X",), ksi)
    both = [kso[0:16, :] + ksi[16:32, :], kso[16:32, :] + ksi[0:16, :]]
    kvo[0:16, :] = both[0].astype(BF16)
    kvo[16:32, :] = both[1].astype(BF16)
    plane = [(dq, dp) for dq, dp in reversed(K_ORDER) if (dq, dp) != (0, 0)]
    for dq, dp in plane:
        post(("V", dq, dp), kvo, kvi.at[dq * 4 + dp], chip(-dp, -dq, False))
    real = lane < BLOCK
    totals = jnp.where(real, gathered("E", eto, eti), 1.0)
    inverse_total = 1.0 / totals
    columns(inverse_total, iec)
    share = jnp.sum(pst[0:ANCHORS, :] * idc[...], axis=0, keepdims=True) * -5.0
    tail = jnp.where(real, eio[...] * (jnp.log(totals[0:1]) + 10.0), 0.0)
    lz[...] = share + tail
    for dz in range(1, N_Z):
        post(("P", 8 - dz), lz, lzi.at[8 - dz], up(dz))
    for dq, dp in plane:
        arrived(("V", dq, dp), kvi.at[dq * 4 + dp])
    within = lax.broadcasted_iota(jnp.int32, (16, 128), 0) % 4
    turned = []
    for s in (0, 1):
        total = both[s]
        for b in range(4):
            by_q = None
            for a in range(4):
                dq, dp = (b, a) if s else (a, b)
                if (dq, dp) == (0, 0):
                    continue
                value = kvi[dq * 4 + dp, s * 16 : s * 16 + 16, :].astype(F32)
                if a:
                    value = pltpu.roll(value, 4 * a, 0)
                by_q = value if by_q is None else by_q + value
            if b:
                by_q = jnp.where(within < b, pltpu.roll(by_q, 12 + b, 0), pltpu.roll(by_q, b, 0))
            total = total + by_q
        inverse = 1.0 / total
        turned.append([pltpu.roll(inverse, shift, 1) if shift else inverse for shift in SHIFTS])

    def inverse_line(s, q):
        dq, dp = K_ORDER[q]
        r = dq * 4 + dp
        return turned[s][q % 4][r : r + 1, :]

    key_line(inverse_line, kie)

    def coupling(r0, rows):
        for r in range(r0, r0 + rows, 16):
            at = pl.ds(r, 16)
            ie, d2, label = iec[at, :], idc[at, :], labc[at, :]
            for c in range(0, KEYS, 128):
                here = pl.ds(c, 128)
                same = label == klab[0:1, here]
                if c == 0 and r < BLOCK:
                    i = lax.broadcasted_iota(jnp.int32, (16, 128), 0) + r
                    same = same & (i != lax.broadcasted_iota(jnp.int32, (16, 128), 1))
                v = w[at, here] * (ie + kie[0:1, here]) - jnp.where(same, d2, 0.0)
                cm[at, here] = v.astype(BF16)

    def product(j, r0, rows):
        at = pl.ds(r0, rows)
        g[j, at, :] = jnp.dot(cm[at, :], ku[:, j * WIDE : (j + 1) * WIDE], preferred_element_type=F32)

    def part(j, dz, first, n):
        return g[j, pl.ds(A_POS[dz] * BLOCK + first, n), :]

    def push(j, step):
        for way, sign in enumerate((1, -1)):
            dz = (sign * (4 - step)) % 8
            at, n = (way * HALF, HALF) if step == 0 else (0, BLOCK)
            value = part(j, dz, at, n)
            rows = pl.ds(at, n)
            if step == 1:
                half = pl.ds(way * HALF, HALF)
                arrived(("R", j, way, 0), rb.at[j, way, 0, half, :])
                pieces = [value[:HALF], value[HALF:]]
                pieces[way] = pieces[way] + rb[j, way, 0, half, :].astype(F32)
                sb[j, way, step, 0:HALF, :] = pieces[0].astype(BF16)
                sb[j, way, step, HALF:BLOCK, :] = pieces[1].astype(BF16)
            else:
                if step > 1:
                    arrived(("R", j, way, step - 1), rb.at[j, way, step - 1])
                    value = value + rb[j, way, step - 1].astype(F32)
                sb[j, way, step, rows, :] = value.astype(BF16)
            post(("R", j, way, step), sb.at[j, way, step, rows, :], rb.at[j, way, step, rows, :], up(sign))

    coupling(672, 96)
    for j in range(CHUNKS):
        product(j, 672, 96)
        push(j, 0)
    coupling(480, 192)
    for j in range(CHUNKS):
        product(j, 480, 192)
    coupling(288, 192)
    for j in range(CHUNKS):
        push(j, 1)
        product(j, 288, 192)
    coupling(96, 192)
    for j in range(CHUNKS):
        product(j, 96, 192)
    coupling(0, 96)
    for j in range(CHUNKS):
        push(j, 2)
        product(j, 0, 96)
    whole = lz[...]
    for dz in range(1, N_Z):
        arrived(("P", dz), lzi.at[dz])
        whole = whole + lzi[dz]
    lo[...] = whole
    for s, dq, dp in peers:
        post(("W", s, dq, dp), lo, li.at[key_slot(s, dq, dp)], chip(-dp, -dq, s))
    for j in range(CHUNKS):
        push(j, 3)

    every = lo[...]
    for s, dq, dp in peers:
        arrived(("W", s, dq, dp), li.at[key_slot(s, dq, dp)])
        every = every + li[key_slot(s, dq, dp)]
    loss[...] = jnp.broadcast_to(jnp.sum(every, axis=1, keepdims=True) * (1.0 / TOKENS), (1, 128))

    along = jnp.zeros((BLOCK, 1), F32)
    for j in range(CHUNKS):
        value = part(j, 0, 0, BLOCK)
        for way in (0, 1):
            arrived(("R", j, way, 3), rb.at[j, way, 3])
            value = value + rb[j, way, 3].astype(F32)
        value = value * 10.0
        g[j, pl.ds(0, BLOCK), :] = value
        along = along + jnp.sum(uf[:, j * WIDE : (j + 1) * WIDE] * value, axis=1, keepdims=True)
    scale = inv[:, 0:1]
    for j in range(CHUNKS):
        cut = slice(j * WIDE, (j + 1) * WIDE)
        grad[:, cut] = (g[j, pl.ds(0, BLOCK), :] - uf[:, cut] * along) * scale

    for copy in pending:
        copy.wait_send()
    assert len(number.numbers) <= N_SEM


def per_device(embeddings, labels):
    vmem = pl.BlockSpec(memory_space=pltpu.VMEM)
    line = labels.reshape(1, BLOCK)
    scratch = [
        ((BLOCK, DEPTH), BF16),
        ((1, BLOCK), jnp.int32),
        ((ANCHORS, DEPTH), BF16),
        ((KEYS, DEPTH), BF16),
        ((ANCHORS, KEYS), F32),
        ((ANCHORS, KEYS), BF16),
        ((CHUNKS, ANCHORS, WIDE), F32),
        ((BLOCK, DEPTH), F32),
        ((BLOCK, 128), F32),
        ((4, 1, 128), F32),
        ((N_Z, 1, 128), F32),
        ((32, 1, 128), F32),
        ((ANCHORS, 128), F32),
        ((8, KEYS), F32),
        ((ANCHORS + 32, 128), F32),
        ((ANCHORS + 32, 128), F32),
        ((ANCHORS + 32, 128), F32),
        ((N_Z, 128), F32),
        ((N_Z, N_Z, 128), F32),
        ((N_Z, 128), F32),
        ((N_Z, N_Z, 128), F32),
        ((1, 128), F32),
        ((ANCHORS, 128), F32),
        ((ANCHORS, 128), F32),
        ((8, KEYS), F32),
        ((32, 128), F32),
        ((32, 128), F32),
        ((32, 128), BF16),
        ((16, 32, 128), BF16),
        ((8, KEYS), F32),
        ((1, 128), F32),
        ((N_Z, 1, 128), F32),
        ((1, 128), F32),
        ((32, 1, 128), F32),
        ((CHUNKS, 2, 4, BLOCK, WIDE), BF16),
        ((CHUNKS, 2, 4, BLOCK, WIDE), BF16),
    ]
    grad, loss = pl.pallas_call(
        kernel,
        out_shape=(
            pltpu.VMEM((BLOCK, DEPTH), F32),
            jax.ShapeDtypeStruct((1, 128), F32),
        ),
        in_specs=[pl.BlockSpec(memory_space=pl.ANY)] * 2,
        out_specs=(vmem, vmem),
        scratch_shapes=[pltpu.VMEM(s, t) for s, t in scratch]
        + [pltpu.SemaphoreType.DMA((2,)), pltpu.SemaphoreType.DMA((N_SEM,)), pltpu.SemaphoreType.DMA((N_SEM,))],
        compiler_params=pltpu.CompilerParams(
            collective_id=0, has_side_effects=True, vmem_limit_bytes=60 * 2**20
        ),
        cost_estimate=pl.CostEstimate(flops=2 * 2 * ANCHORS * KEYS * DEPTH, bytes_accessed=2**20, transcendentals=0),
    )(embeddings, line)
    return grad, loss[0, 0]


def solution(mesh):
    placed = (P(("row", "col"), None), P(("row", "col")))
    return jax.shard_map(
        per_device,
        mesh=mesh,
        in_specs=placed,
        out_specs=(P(("row", "col"), None), P()),
        check_vma=False,
    )
```

```python
import jax
import jax.numpy as jnp
from jax import lax
from jax.experimental import pallas as pl
from jax.experimental.pallas import tpu as pltpu
from jax.sharding import PartitionSpec as P

F32 = jnp.float32
BF16 = jnp.bfloat16
MESH = pl.DeviceIdType.MESH
LOG2E = 1.4426950408889634
NT = (((1,), (1,)), ((), ()))

BLOCK = 96
HALF = 48
PIECES = 3
PIECE = BLOCK // PIECES
DEPTH = 1024
N_Z = 8
ANCHORS = N_Z * BLOCK
KEYS = 32 * BLOCK
GROUP = 8 * BLOCK
CHUNKS = 4
WIDE = DEPTH // CHUNKS
TOKENS = 24576

A_POS = {0: 0, 7: 1, 1: 2, 6: 3, 2: 4, 5: 5, 3: 6, 4: 7}
K_ORDER = [
    (0, 0), (0, 3), (0, 1), (3, 0),
    (1, 0), (3, 3), (1, 3), (3, 1),
    (0, 2), (1, 1), (2, 0), (2, 3),
    (1, 2), (3, 2), (2, 1), (2, 2),
]
K_POS = {d: i for i, d in enumerate(K_ORDER)}
SHIFTS = (0, 96, 64, 32)
ARRIVALS = [
    ("K", 0, 3, 0), ("K", 0, 1, 0), ("K", 0, 3, 1), ("K", 0, 1, 1), ("A", 7, 0), ("A", 1, 0),
    ("K", 0, 3, 2), ("K", 0, 1, 2), ("K", 3, 0, 0), ("K", 1, 0, 0), ("A", 7, 1), ("A", 1, 1),
    ("K", 3, 0, 1), ("K", 1, 0, 1), ("K", 3, 0, 2), ("K", 1, 0, 2), ("A", 7, 2), ("A", 1, 2),
    ("K", 1, 3, 0), ("K", 0, 2, 0), ("K", 3, 3, 0), ("K", 1, 1, 0), ("K", 3, 1, 0), ("K", 1, 3, 1),
    ("A", 6, 0), ("A", 2, 0), ("K", 3, 3, 1), ("K", 1, 1, 1), ("K", 0, 2, 1), ("K", 3, 1, 1),
    ("A", 6, 1), ("A", 2, 1), ("K", 3, 3, 2), ("K", 1, 3, 2), ("K", 3, 1, 2), ("A", 6, 2),
    ("A", 2, 2), ("K", 0, 2, 2), ("K", 1, 1, 2), ("K", 2, 0, 0), ("K", 2, 0, 1), ("K", 2, 0, 2),
    ("K", 3, 2, 0), ("K", 1, 2, 0), ("K", 2, 3, 0), ("K", 2, 3, 1), ("A", 5, 0), ("A", 3, 0),
    ("K", 2, 1, 0), ("K", 1, 2, 1), ("K", 3, 2, 1), ("K", 2, 3, 2), ("A", 5, 1), ("A", 3, 1),
    ("K", 2, 1, 1), ("K", 1, 2, 2), ("K", 3, 2, 2), ("A", 3, 2), ("A", 5, 2), ("K", 2, 1, 2),
    ("K", 2, 2, 0), ("K", 2, 2, 1), ("K", 2, 2, 2), ("A", 4, 2), ("A", 4, 0), ("A", 4, 1),
]
JOBS_AFTER = {
    17: (0, 1), 21: (2,), 36: (3, 4, 5), 39: (6,), 41: (7, 8), 59: (9, 10, 11), 60: (12, 13, 14, 15), 61: (16, 17),

}


def key_row(core, dq, dp):
    q = K_POS[(dq, dp)]
    return (q // 4) * GROUP + core * (GROUP // 2) + (q % 4) * BLOCK


def key_slot(core, dq, dp):
    return core * 16 + K_POS[(dq, dp)]


class Semaphores:
    def __init__(self):
        self.numbers = {}

    def __call__(self, name):
        return self.numbers.setdefault(name, len(self.numbers))


N_SEM = 340


def kernel(emb, lab, grad, loss,
           own, own_line, au, ku, w, cm, g, uf, inv,
           al, kl, labc, klab,
           est, pst, cst, cto, cti, eto, eti, eio, iec, idc, cs, kso, ksi, kvo, kvi, kie,
           lz, lzi, lo, li, sb, rb, load, send, recv):
    row, z = lax.axis_index("row"), lax.axis_index("col")
    core, x, y = row % 2, (row // 2) % 4, row // 8
    number = Semaphores()
    pending = []

    def chip(dp, dq, other):
        px = (x + dp + core * (dq - dp) + 8) % 4
        py = (y + dq + core * (dp - dq) + 8) % 4
        pc = 1 - core if other else core
        return ((py * 4 + px) * 2 + pc, z)

    def up(dz):
        return (row, (z + dz + 8) % 8)

    def message(name, src, dst, to):
        i = number(name)
        return pltpu.make_async_remote_copy(
            src_ref=src, dst_ref=dst, send_sem=send.at[i], recv_sem=recv.at[i], device_id=to, device_id_type=MESH
        )

    def post(name, src, dst, to):
        copy = message(name, src, dst, to)
        copy.start()
        pending.append(copy)

    def arrived(name, dst):
        message(name, dst, dst, up(1)).wait_recv()

    def a_ref(dz, h):
        return au.at[pl.ds(A_POS[dz] * BLOCK + h * PIECE, PIECE), :]

    def k_ref(s, dq, dp, h):
        return ku.at[pl.ds(key_row(s, dq, dp) + h * PIECE, PIECE), :]

    peers = [(s, dq, dp) for s in (0, 1) for dq, dp in K_ORDER if (s, dq, dp) != (0, 0, 0)]

    near = [up(1), up(-1), chip(1, 0, 0), chip(-1, 0, 0), chip(0, 1, 0), chip(0, -1, 0), chip(0, 0, 1)]
    barrier = pltpu.get_barrier_semaphore()
    for other in near:
        pl.semaphore_signal(barrier, inc=1, device_id=other, device_id_type=MESH)

    fetch = pltpu.make_async_copy(emb, own, load.at[0])
    fetch.start()
    fetch_line = pltpu.make_async_copy(lab, own_line, load.at[1])
    fetch_line.start()
    est[...] = jnp.zeros_like(est)
    cst[...] = jnp.zeros_like(cst)
    cs[...] = jnp.zeros_like(cs)
    al[0] = jnp.zeros((1, 128), F32)
    fetch_line.wait()
    al[0, :, 0:BLOCK] = own_line[...].astype(F32)
    kl[0] = al[0]
    fetch.wait()
    wide = own[...].astype(F32)
    scale = lax.rsqrt(jnp.sum(wide * wide, axis=1, keepdims=True) + 1e-6)
    unit = wide * scale
    uf[...] = unit
    inv[...] = jnp.broadcast_to(scale, (BLOCK, 128))
    rounded = unit.astype(BF16)
    au[pl.ds(0, BLOCK), :] = rounded
    ku[pl.ds(0, BLOCK), :] = rounded
    pl.semaphore_wait(barrier, len(near))

    def upward(dp, h):
        return h == 0 or (h == 1 and dp < 2)

    def ways_of(what):
        if what[0] == "A":
            _, dz, h = what
            if dz == 0:
                return [(0, 0, 1, 0, ("A", 7, h)), (0, 0, -1, 0, ("A", 1, h))]
            if dz in (7, 6) or (dz == 5 and upward(0, h)):
                return [(0, 0, 1, 0, ("A", dz - 1, h))]
            if dz in (1, 2) or (dz == 3 and not upward(0, h)):
                return [(0, 0, -1, 0, ("A", dz + 1, h))]
            return []
        _, dq, dp, h = what
        ways = []
        if (dq, dp) == (0, 0):
            ways += [(1, 0, 0, 0, ("K", 0, 3, h)), (-1, 0, 0, 0, ("K", 0, 1, h))]
        elif (dq, dp) == (0, 3) and upward(2, h):
            ways += [(1, 0, 0, 0, ("K", 0, 2, h))]
        elif (dq, dp) == (0, 1) and not upward(2, h):
            ways += [(-1, 0, 0, 0, ("K", 0, 2, h))]
        if dq == 0:
            ways += [(0, 1, 0, 0, ("K", 3, dp, h)), (0, -1, 0, 0, ("K", 1, dp, h))]
        elif dq == 3 and upward(dp, h):
            ways += [(0, 1, 0, 0, ("K", 2, dp, h))]
        elif dq == 1 and not upward(dp, h):
            ways += [(0, -1, 0, 0, ("K", 2, dp, h))]
        return ways + [(0, 0, 0, 1, ("S", dq, dp, h))]

    def place(what):
        if what[0] == "A":
            return a_ref(what[1], what[2])
        return k_ref(1 if what[0] == "S" else 0, *what[1:])

    def line_place(what):
        if what[0] == "A":
            return al.at[what[1]]
        return kl.at[key_slot(1 if what[0] == "S" else 0, what[1], what[2])]

    def forward(what, way):
        tp, tq, tz, ts, there = way
        to = up(tz) if tz else chip(tp, tq, bool(ts))
        if what[-1] == 0:
            post(("L",) + there, line_place(what), line_place(there), to)
        post(there, place(what), place(there), to)

    def hand_on(what):
        for way in ways_of(what):
            forward(what, way)

    for axes in ((0, 2), (1,), (3,)):
        for h in range(PIECES):
            for what in (("K", 0, 0, h), ("A", 0, h)):
                for way in ways_of(what):
                    if any(way[i] for i in axes):
                        forward(what, way)
    lane = lax.broadcasted_iota(jnp.int32, (1, 128), 1)

    def columns(rows, out):
        turned = jnp.transpose(jnp.concatenate([rows, jnp.zeros((128 - N_Z, 128), F32)], axis=0))
        for dz, p in A_POS.items():
            out[pl.ds(p * BLOCK, BLOCK), :] = jnp.broadcast_to(turned[:BLOCK, dz : dz + 1], (BLOCK, 128))

    def lines(stat, out):
        for dz in range(N_Z):
            part = jnp.transpose(stat[pl.ds(A_POS[dz] * BLOCK, 128), :])
            out[dz : dz + 1, :] = jnp.sum(part, axis=0, keepdims=True)

    def exchange(name, out, into):
        for dz in (4, 3, 5, 2, 6, 1, 7):
            post((name, 8 - dz), out, into.at[8 - dz], up(dz))

    def gathered(name, out, into):
        total = out[...]
        for dz in range(1, N_Z):
            arrived((name, dz), into.at[dz])
            total = total + pltpu.roll(into[dz], dz, 0)
        return total

    def key_line(line_of, out):
        for s in (0, 1):
            for q in range(4):
                m = [line_of(s, q * 4 + p) for p in range(4)]
                base = q * GROUP + s * (GROUP // 2)
                for t, (cut, a, b) in enumerate(((96, 0, 1), (64, 1, 2), (32, 2, 3))):
                    line = jnp.where(lane < cut, m[a], m[b])
                    out[:, pl.ds(base + t * 128, 128)] = jnp.broadcast_to(line, (8, 128))

    def labels_ready():
        columns(jnp.concatenate([al[dz] for dz in range(N_Z)], axis=0), labc)

        def label_line(s, q):
            line = kl[s * 16 + q]
            return pltpu.roll(line, SHIFTS[q % 4], 1) if q % 4 else line

        key_line(label_line, klab)

    def count():
        for r in range(0, ANCHORS, 32):
            label = labc[pl.ds(r, 32), :]
            total = jnp.zeros((32, 128), F32)
            for t in range(KEYS // 128):
                total = total + jnp.where(label == klab[0:1, t * 128 : (t + 1) * 128], 1.0, 0.0)
            cst[pl.ds(r, 32), :] = total
        lines(cst, cto)
        exchange("C", cto, cti)

    def counts_ready():
        others = gathered("C", cto, cti) - 1.0
        columns(jnp.where(lane < BLOCK, 2.0 / jnp.maximum(others, 1.0), 0.0), idc)
        eio[...] = others[0:1] / jnp.maximum(others[0:1], 1.0)

    def on_diagonal(rows):
        r = lax.broadcasted_iota(jnp.int32, (rows, 128), 0)
        c = lax.broadcasted_iota(jnp.int32, (rows, 128), 1)
        return (r == c) & (r < BLOCK)

    def score(r0, rows, c0, cols):
        at = pl.ds(r0, rows)
        acc = lax.dot_general(au[at, :], ku[pl.ds(c0, cols), :], NT, preferred_element_type=F32)
        total = None
        for t in range(cols // 128):
            here = pl.ds(c0 + t * 128, 128)
            s = acc[:, t * 128 : (t + 1) * 128]
            w[at, here] = s
            e = jnp.exp2(s * (10.0 * LOG2E))
            if r0 == 0 and c0 + t == 0:
                e = jnp.where(on_diagonal(rows), 0.0, e)
            cs[:, here] += jnp.sum(e.reshape(rows // 8, 8, 128), axis=0)
            total = e if t == 0 else total + e
        est[at, :] += total

    def positives():
        for r in range(0, ANCHORS, 32):
            at = pl.ds(r, 32)
            label = labc[at, :]
            total = jnp.zeros((32, 128), F32)
            for c in range(0, KEYS, 128):
                here = pl.ds(c, 128)
                same = label == klab[0:1, here]
                if c == 0 and r < BLOCK:
                    i = lax.broadcasted_iota(jnp.int32, (32, 128), 0) + r
                    same = same & (i != lax.broadcasted_iota(jnp.int32, (32, 128), 1))
                total = total + jnp.where(same, w[at, here], 0.0)
            pst[at, :] = total

    def need(r0, rows, c0, cols):
        wants = set()
        for dz, p in A_POS.items():
            if dz and p * BLOCK < r0 + rows and (p + 1) * BLOCK > r0:
                wants |= {("A", dz, h) for h in range(PIECES)}
        for s in (0, 1):
            for dq, dp in K_ORDER:
                k0 = key_row(s, dq, dp)
                if k0 < c0 + cols and k0 + BLOCK > c0 and (s, dq, dp) != (0, 0, 0):
                    wants |= {("S" if s else "K", dq, dp, h) for h in range(PIECES)}
        return wants

    work = []
    for r0, rows, c0, c1, wide in (
        (0, 288, 0, GROUP, 256),
        (288, 192, 0, GROUP, 256),
        (0, 480, GROUP, 2 * GROUP, 256),
        (480, 192, 0, 2 * GROUP, 256),
        (0, 672, 2 * GROUP, 3 * GROUP, 256),
        (672, 96, 0, 3 * GROUP, GROUP),
        (0, 768, 3 * GROUP, 4 * GROUP, 256),
    ):
        work += [(r0, rows, c, wide) for c in range(c0, c1, wide)]
    seen = set()

    def receive(what):
        if what in seen:
            return
        seen.add(what)
        if what[-1] == 0:
            arrived(("L",) + what, line_place(what))
        arrived(what, place(what))
        if what[0] != "S":
            hand_on(what)

    def can_run(wants):
        return all(v in seen for v in wants if v[0] != "S")

    def do(job):
        for v in sorted(need(*job) - seen):
            receive(v)
        score(*job)

    left = list(range(len(work)))
    for n, what in enumerate(ARRIVALS):
        receive(what)
        for i in JOBS_AFTER.get(n, ()):
            do(work[i])
            left.remove(i)
    for i in left:
        do(work[i])
    assert len(seen) == PIECES * (N_Z - 1 + 15 + 16)

    tiles = [jnp.sum(cs[:, t * 128 : (t + 1) * 128], axis=0, keepdims=True) for t in range(KEYS // 128)]
    for s in (0, 1):
        for dq, dp in K_ORDER:
            t, off = divmod(key_row(s, dq, dp), 128)
            line = tiles[t]
            if off:
                line = pltpu.roll(line, 128 - off, 1)
                if off + BLOCK > 128:
                    line = jnp.where(lane < 128 - off, line, pltpu.roll(tiles[t + 1], 128 - off, 1))
            r = s * 16 + dq * 4 + dp
            kso[r : r + 1, :] = line
    post(("X",), kso, ksi, chip(0, 0, True))
    lines(est, eto)
    exchange("E", eto, eti)
    labels_ready()
    arrived(("X",), ksi)
    both = [kso[0:16, :] + ksi[16:32, :], kso[16:32, :] + ksi[0:16, :]]
    kvo[0:16, :] = both[0].astype(BF16)
    kvo[16:32, :] = both[1].astype(BF16)
    plane = [(dq, dp) for dq, dp in reversed(K_ORDER) if (dq, dp) != (0, 0)]
    for dq, dp in plane:
        post(("V", dq, dp), kvo, kvi.at[dq * 4 + dp], chip(-dp, -dq, False))
    count()
    positives()
    real = lane < BLOCK
    totals = jnp.where(real, gathered("E", eto, eti), 1.0)
    inverse_total = 1.0 / totals
    columns(inverse_total, iec)
    counts_ready()
    share = jnp.sum(pst[0:ANCHORS, :] * idc[...], axis=0, keepdims=True) * -5.0
    tail = jnp.where(real, eio[...] * jnp.log(totals[0:1]), 0.0)
    lz[...] = share + tail
    for dz in range(1, N_Z):
        post(("P", 8 - dz), lz, lzi.at[8 - dz], up(dz))
    for dq, dp in plane:
        arrived(("V", dq, dp), kvi.at[dq * 4 + dp])
    within = lax.broadcasted_iota(jnp.int32, (16, 128), 0) % 4
    turned = []
    for s in (0, 1):
        total = both[s]
        for b in range(4):
            by_q = None
            for a in range(4):
                dq, dp = (b, a) if s else (a, b)
                if (dq, dp) == (0, 0):
                    continue
                value = kvi[dq * 4 + dp, s * 16 : s * 16 + 16, :].astype(F32)
                if a:
                    value = pltpu.roll(value, 4 * a, 0)
                by_q = value if by_q is None else by_q + value
            if b:
                by_q = jnp.where(within < b, pltpu.roll(by_q, 12 + b, 0), pltpu.roll(by_q, b, 0))
            total = total + by_q
        inverse = 1.0 / total
        turned.append([pltpu.roll(inverse, shift, 1) if shift else inverse for shift in SHIFTS])

    def inverse_line(s, q):
        dq, dp = K_ORDER[q]
        r = dq * 4 + dp
        return turned[s][q % 4][r : r + 1, :]

    key_line(inverse_line, kie)

    def coupling(r0, rows):
        for r in range(r0, r0 + rows, 16):
            at = pl.ds(r, 16)
            ie, d2, label = iec[at, :], idc[at, :], labc[at, :]
            for c in range(0, KEYS, 128):
                here = pl.ds(c, 128)
                same = label == klab[0:1, here]
                e = jnp.exp2(w[at, here] * (10.0 * LOG2E))
                if c == 0 and r < BLOCK:
                    i = lax.broadcasted_iota(jnp.int32, (16, 128), 0) + r
                    other = i != lax.broadcasted_iota(jnp.int32, (16, 128), 1)
                    same, e = same & other, jnp.where(other, e, 0.0)
                v = e * (ie + kie[0:1, here]) - jnp.where(same, d2, 0.0)
                cm[at, here] = v.astype(BF16)

    def product(j, r0, rows):
        at = pl.ds(r0, rows)
        g[j, at, :] = jnp.dot(cm[at, :], ku[:, j * WIDE : (j + 1) * WIDE], preferred_element_type=F32)

    def part(j, dz, first, n):
        return g[j, pl.ds(A_POS[dz] * BLOCK + first, n), :]

    def push(j, step):
        for way, sign in enumerate((1, -1)):
            dz = (sign * (4 - step)) % 8
            at, n = (way * HALF, HALF) if step == 0 else (0, BLOCK)
            value = part(j, dz, at, n)
            rows = pl.ds(at, n)
            if step == 1:
                half = pl.ds(way * HALF, HALF)
                arrived(("R", j, way, 0), rb.at[j, way, 0, half, :])
                pieces = [value[:HALF], value[HALF:]]
                pieces[way] = pieces[way] + rb[j, way, 0, half, :].astype(F32)
                sb[j, way, step, 0:HALF, :] = pieces[0].astype(BF16)
                sb[j, way, step, HALF:BLOCK, :] = pieces[1].astype(BF16)
            else:
                if step > 1:
                    arrived(("R", j, way, step - 1), rb.at[j, way, step - 1])
                    value = value + rb[j, way, step - 1].astype(F32)
                sb[j, way, step, rows, :] = value.astype(BF16)
            post(("R", j, way, step), sb.at[j, way, step, rows, :], rb.at[j, way, step, rows, :], up(sign))

    coupling(672, 96)
    for j in range(CHUNKS):
        product(j, 672, 96)
        push(j, 0)
    coupling(480, 192)
    for j in range(CHUNKS):
        product(j, 480, 192)
    coupling(288, 192)
    for j in range(CHUNKS):
        push(j, 1)
        product(j, 288, 192)
    coupling(96, 192)
    for j in range(CHUNKS):
        product(j, 96, 192)
    coupling(0, 96)
    for j in range(CHUNKS):
        push(j, 2)
        product(j, 0, 96)
    whole = lz[...]
    for dz in range(1, N_Z):
        arrived(("P", dz), lzi.at[dz])
        whole = whole + lzi[dz]
    lo[...] = whole
    for s, dq, dp in peers:
        post(("W", s, dq, dp), lo, li.at[key_slot(s, dq, dp)], chip(-dp, -dq, s))
    for j in range(CHUNKS):
        push(j, 3)

    every = lo[...]
    for s, dq, dp in peers:
        arrived(("W", s, dq, dp), li.at[key_slot(s, dq, dp)])
        every = every + li[key_slot(s, dq, dp)]
    loss[...] = jnp.broadcast_to(jnp.sum(every, axis=1, keepdims=True) * (1.0 / TOKENS), (1, 128))

    along = jnp.zeros((BLOCK, 1), F32)
    for j in range(CHUNKS):
        value = part(j, 0, 0, BLOCK)
        for way in (0, 1):
            arrived(("R", j, way, 3), rb.at[j, way, 3])
            value = value + rb[j, way, 3].astype(F32)
        value = value * 10.0
        g[j, pl.ds(0, BLOCK), :] = value
        along = along + jnp.sum(uf[:, j * WIDE : (j + 1) * WIDE] * value, axis=1, keepdims=True)
    scale = inv[:, 0:1]
    for j in range(CHUNKS):
        cut = slice(j * WIDE, (j + 1) * WIDE)
        grad[:, cut] = (g[j, pl.ds(0, BLOCK), :] - uf[:, cut] * along) * scale

    for copy in pending:
        copy.wait_send()
    assert len(number.numbers) <= N_SEM


def per_device(embeddings, labels):
    vmem = pl.BlockSpec(memory_space=pltpu.VMEM)
    line = labels.reshape(1, BLOCK)
    scratch = [
        ((BLOCK, DEPTH), BF16),
        ((1, BLOCK), jnp.int32),
        ((ANCHORS, DEPTH), BF16),
        ((KEYS, DEPTH), BF16),
        ((ANCHORS, KEYS), F32),
        ((ANCHORS, KEYS), BF16),
        ((CHUNKS, ANCHORS, WIDE), F32),
        ((BLOCK, DEPTH), F32),
        ((BLOCK, 128), F32),
        ((N_Z, 1, 128), F32),
        ((32, 1, 128), F32),
        ((ANCHORS, 128), F32),
        ((8, KEYS), F32),
        ((ANCHORS + 32, 128), F32),
        ((ANCHORS + 32, 128), F32),
        ((ANCHORS + 32, 128), F32),
        ((N_Z, 128), F32),
        ((N_Z, N_Z, 128), F32),
        ((N_Z, 128), F32),
        ((N_Z, N_Z, 128), F32),
        ((1, 128), F32),
        ((ANCHORS, 128), F32),
        ((ANCHORS, 128), F32),
        ((8, KEYS), F32),
        ((32, 128), F32),
        ((32, 128), F32),
        ((32, 128), BF16),
        ((16, 32, 128), BF16),
        ((8, KEYS), F32),
        ((1, 128), F32),
        ((N_Z, 1, 128), F32),
        ((1, 128), F32),
        ((32, 1, 128), F32),
        ((CHUNKS, 2, 4, BLOCK, WIDE), BF16),
        ((CHUNKS, 2, 4, BLOCK, WIDE), BF16),
    ]
    grad, loss = pl.pallas_call(
        kernel,
        out_shape=(
            pltpu.VMEM((BLOCK, DEPTH), F32),
            jax.ShapeDtypeStruct((1, 128), F32),
        ),
        in_specs=[pl.BlockSpec(memory_space=pl.ANY)] * 2,
        out_specs=(vmem, vmem),
        scratch_shapes=[pltpu.VMEM(s, t) for s, t in scratch]
        + [pltpu.SemaphoreType.DMA((2,)), pltpu.SemaphoreType.DMA((N_SEM,)), pltpu.SemaphoreType.DMA((N_SEM,))],
        compiler_params=pltpu.CompilerParams(
            collective_id=0, has_side_effects=True, vmem_limit_bytes=60 * 2**20
        ),
        cost_estimate=pl.CostEstimate(flops=2 * 2 * ANCHORS * KEYS * DEPTH, bytes_accessed=2**20, transcendentals=0),
    )(embeddings, line)
    return grad, loss[0, 0]


def solution(mesh):
    placed = (P(("row", "col"), None), P(("row", "col")))
    return jax.shard_map(
        per_device,
        mesh=mesh,
        in_specs=placed,
        out_specs=(P(("row", "col"), None), P()),
        check_vma=False,
    )
```

```python
import jax
import jax.numpy as jnp
from jax import lax
from jax.experimental import pallas as pl
from jax.experimental.pallas import tpu as pltpu
from jax.sharding import PartitionSpec as P

F32 = jnp.float32
BF16 = jnp.bfloat16
MESH = pl.DeviceIdType.MESH
LOG2E = 1.4426950408889634
NT = (((1,), (1,)), ((), ()))

BLOCK = 96
HALF = 48
PIECES = 3
PIECE = BLOCK // PIECES
DEPTH = 1024
N_Z = 8
ANCHORS = N_Z * BLOCK
KEYS = 32 * BLOCK
GROUP = 8 * BLOCK
CHUNKS = 4
WIDE = DEPTH // CHUNKS
TOKENS = 24576

A_POS = {0: 0, 7: 1, 1: 2, 6: 3, 2: 4, 5: 5, 3: 6, 4: 7}
K_ORDER = [
    (0, 0), (0, 3), (0, 1), (3, 0),
    (1, 0), (3, 3), (1, 3), (3, 1),
    (0, 2), (1, 1), (2, 0), (2, 3),
    (1, 2), (3, 2), (2, 1), (2, 2),
]
K_POS = {d: i for i, d in enumerate(K_ORDER)}
SHIFTS = (0, 96, 64, 32)
ARRIVALS = [
    ("K", 0, 3, 0), ("K", 0, 1, 0), ("K", 0, 3, 1), ("K", 0, 1, 1), ("A", 7, 0), ("A", 1, 0),
    ("K", 0, 3, 2), ("K", 0, 1, 2), ("K", 3, 0, 0), ("K", 1, 0, 0), ("A", 7, 1), ("A", 1, 1),
    ("K", 3, 0, 1), ("K", 1, 0, 1), ("K", 3, 0, 2), ("K", 1, 0, 2), ("A", 7, 2), ("A", 1, 2),
    ("K", 1, 3, 0), ("K", 0, 2, 0), ("K", 3, 3, 0), ("K", 1, 1, 0), ("K", 3, 1, 0), ("K", 1, 3, 1),
    ("A", 6, 0), ("A", 2, 0), ("K", 3, 3, 1), ("K", 1, 1, 1), ("K", 0, 2, 1), ("K", 3, 1, 1),
    ("A", 6, 1), ("A", 2, 1), ("K", 3, 3, 2), ("K", 1, 3, 2), ("K", 3, 1, 2), ("A", 6, 2),
    ("A", 2, 2), ("K", 0, 2, 2), ("K", 1, 1, 2), ("K", 2, 0, 0), ("K", 2, 0, 1), ("K", 2, 0, 2),
    ("K", 3, 2, 0), ("K", 1, 2, 0), ("K", 2, 3, 0), ("K", 2, 3, 1), ("A", 5, 0), ("A", 3, 0),
    ("K", 2, 1, 0), ("K", 1, 2, 1), ("K", 3, 2, 1), ("K", 2, 3, 2), ("A", 5, 1), ("A", 3, 1),
    ("K", 2, 1, 1), ("K", 1, 2, 2), ("K", 3, 2, 2), ("A", 3, 2), ("A", 5, 2), ("K", 2, 1, 2),
    ("K", 2, 2, 0), ("K", 2, 2, 1), ("K", 2, 2, 2), ("A", 4, 2), ("A", 4, 0), ("A", 4, 1),
]
LABELS_AT = 17
JOBS_AFTER = {
    17: (0,), 18: (1, 2), 21: (3, 4), 25: (5,), 26: (6,), 36: (7, 8, 9, 11), 41: (12, 13), 44: (10,), 58: (14,), 59: (15, 16, 17), 60: (18, 19, 20), 61: (21, 22),
}


def key_row(core, dq, dp):
    q = K_POS[(dq, dp)]
    return (q // 4) * GROUP + core * (GROUP // 2) + (q % 4) * BLOCK


def key_slot(core, dq, dp):
    return core * 16 + K_POS[(dq, dp)]


class Semaphores:
    def __init__(self):
        self.numbers = {}

    def __call__(self, name):
        return self.numbers.setdefault(name, len(self.numbers))


N_SEM = 260


def kernel(emb, lab, grad, loss,
           own, own_line, au, ku, w, cm, g, uf, inv,
           var, al, kl, labc, klab,
           est, pst, cst, cto, cti, eto, eti, eio, iec, idc, cs, kso, ksi, kvo, kvi, kie,
           lz, lzi, lo, li, sb, rb, load, send, recv):
    row, z = lax.axis_index("row"), lax.axis_index("col")
    core, x, y = row % 2, (row // 2) % 4, row // 8
    number = Semaphores()
    pending = []

    def chip(dp, dq, other):
        px = (x + dp + core * (dq - dp) + 8) % 4
        py = (y + dq + core * (dp - dq) + 8) % 4
        pc = 1 - core if other else core
        return ((py * 4 + px) * 2 + pc, z)

    def up(dz):
        return (row, (z + dz + 8) % 8)

    def message(name, src, dst, to):
        i = number(name)
        return pltpu.make_async_remote_copy(
            src_ref=src, dst_ref=dst, send_sem=send.at[i], recv_sem=recv.at[i], device_id=to, device_id_type=MESH
        )

    def post(name, src, dst, to):
        copy = message(name, src, dst, to)
        copy.start()
        pending.append(copy)

    def sent(n):
        for copy in pending[:n]:
            copy.wait_send()
        del pending[:n]

    def arrived(name, dst):
        message(name, dst, dst, up(1)).wait_recv()

    def a_ref(dz, h):
        return au.at[pl.ds(A_POS[dz] * BLOCK + h * PIECE, PIECE), :]

    def k_ref(s, dq, dp, h):
        return ku.at[pl.ds(key_row(s, dq, dp) + h * PIECE, PIECE), :]

    peers = [(s, dq, dp) for s in (0, 1) for dq, dp in K_ORDER if (s, dq, dp) != (0, 0, 0)]

    barrier = pltpu.get_barrier_semaphore()
    for dz in range(1, N_Z):
        pl.semaphore_signal(barrier, inc=1, device_id=up(dz), device_id_type=MESH)
    for s, dq, dp in peers:
        pl.semaphore_signal(barrier, inc=1, device_id=chip(-dp, -dq, s), device_id_type=MESH)

    fetch = pltpu.make_async_copy(emb, own, load.at[0])
    fetch.start()
    fetch_line = pltpu.make_async_copy(lab, own_line, load.at[1])
    fetch_line.start()
    est[...] = jnp.zeros_like(est)
    cst[...] = jnp.zeros_like(cst)
    cs[...] = jnp.zeros_like(cs)
    al[0] = jnp.zeros((1, 128), F32)
    fetch_line.wait()
    al[0, :, 0:BLOCK] = own_line[...].astype(F32)
    own_label = al[0]
    for p, shift in enumerate(SHIFTS):
        var[p] = pltpu.roll(own_label, shift, 1) if shift else own_label
    kl[0] = own_label
    fetch.wait()
    wide = own[...].astype(F32)
    scale = lax.rsqrt(jnp.sum(wide * wide, axis=1, keepdims=True) + 1e-6)
    unit = wide * scale
    uf[...] = unit
    inv[...] = jnp.broadcast_to(scale, (BLOCK, 128))
    rounded = unit.astype(BF16)
    au[pl.ds(0, BLOCK), :] = rounded
    ku[pl.ds(0, BLOCK), :] = rounded
    pl.semaphore_wait(barrier, N_Z - 1 + len(peers))

    def upward(dp, h):
        return h == 0 or (h == 1 and dp < 2)

    def ways_of(what):
        if what[0] == "A":
            _, dz, h = what
            if dz == 0:
                return [(0, 0, 1, 0, ("A", 7, h)), (0, 0, -1, 0, ("A", 1, h))]
            if dz in (7, 6) or (dz == 5 and upward(0, h)):
                return [(0, 0, 1, 0, ("A", dz - 1, h))]
            if dz in (1, 2) or (dz == 3 and not upward(0, h)):
                return [(0, 0, -1, 0, ("A", dz + 1, h))]
            return []
        _, dq, dp, h = what
        ways = []
        if (dq, dp) == (0, 0):
            ways += [(1, 0, 0, 0, ("K", 0, 3, h)), (-1, 0, 0, 0, ("K", 0, 1, h))]
        elif (dq, dp) == (0, 3) and upward(2, h):
            ways += [(1, 0, 0, 0, ("K", 0, 2, h))]
        elif (dq, dp) == (0, 1) and not upward(2, h):
            ways += [(-1, 0, 0, 0, ("K", 0, 2, h))]
        if dq == 0:
            ways += [(0, 1, 0, 0, ("K", 3, dp, h)), (0, -1, 0, 0, ("K", 1, dp, h))]
        elif dq == 3 and upward(dp, h):
            ways += [(0, 1, 0, 0, ("K", 2, dp, h))]
        elif dq == 1 and not upward(dp, h):
            ways += [(0, -1, 0, 0, ("K", 2, dp, h))]
        return ways + [(0, 0, 0, 1, ("S", dq, dp, h))]

    def place(what):
        if what[0] == "A":
            return a_ref(what[1], what[2])
        return k_ref(1 if what[0] == "S" else 0, *what[1:])

    def forward(what, way):
        tp, tq, tz, ts, there = way
        post(there, place(what), place(there), up(tz) if tz else chip(tp, tq, bool(ts)))

    def hand_on(what):
        for way in ways_of(what):
            forward(what, way)

    for axes in ((0, 2), (1,), (3,)):
        for h in range(PIECES):
            for what in (("K", 0, 0, h), ("A", 0, h)):
                for way in ways_of(what):
                    if any(way[i] for i in axes):
                        forward(what, way)
    for dz in range(1, N_Z):
        post(("L", 8 - dz), al.at[0], al.at[8 - dz], up(dz))
    for s, dq, dp in peers:
        post(("M", s, dq, dp), var.at[K_POS[(dq, dp)] % 4], kl.at[key_slot(s, dq, dp)], chip(-dp, -dq, s))

    lane = lax.broadcasted_iota(jnp.int32, (1, 128), 1)

    def columns(rows, out):
        turned = jnp.transpose(jnp.concatenate([rows, jnp.zeros((128 - N_Z, 128), F32)], axis=0))
        for dz, p in A_POS.items():
            out[pl.ds(p * BLOCK, BLOCK), :] = jnp.broadcast_to(turned[:BLOCK, dz : dz + 1], (BLOCK, 128))

    def lines(stat, out):
        for dz in range(N_Z):
            part = jnp.transpose(stat[pl.ds(A_POS[dz] * BLOCK, 128), :])
            out[dz : dz + 1, :] = jnp.sum(part, axis=0, keepdims=True)

    def exchange(name, out, into):
        for dz in (4, 3, 5, 2, 6, 1, 7):
            post((name, 8 - dz), out, into.at[8 - dz], up(dz))

    def gathered(name, out, into):
        total = out[...]
        for dz in range(1, N_Z):
            arrived((name, dz), into.at[dz])
            total = total + pltpu.roll(into[dz], dz, 0)
        return total

    def key_line(line_of, out):
        for s in (0, 1):
            for q in range(4):
                m = [line_of(s, q * 4 + p) for p in range(4)]
                base = q * GROUP + s * (GROUP // 2)
                for t, (cut, a, b) in enumerate(((96, 0, 1), (64, 1, 2), (32, 2, 3))):
                    line = jnp.where(lane < cut, m[a], m[b])
                    out[:, pl.ds(base + t * 128, 128)] = jnp.broadcast_to(line, (8, 128))

    def labels_ready():
        for dz in range(1, N_Z):
            arrived(("L", dz), al.at[dz])
        for s, dq, dp in peers:
            arrived(("M", s, dq, dp), kl.at[key_slot(s, dq, dp)])
        columns(jnp.concatenate([al[dz] for dz in range(N_Z)], axis=0), labc)
        key_line(lambda s, q: kl[s * 16 + q], klab)

    def count(r0):
        for r in range(r0, r0 + 192, 32):
            label = labc[pl.ds(r, 32), :]
            total = jnp.zeros((32, 128), F32)
            for t in range(KEYS // 128):
                total = total + jnp.where(label == klab[0:1, t * 128 : (t + 1) * 128], 1.0, 0.0)
            cst[pl.ds(r, 32), :] = total
        if r0 == ANCHORS - 192:
            lines(cst, cto)
            exchange("C", cto, cti)

    def counts_ready():
        positives = gathered("C", cto, cti) - 1.0
        cto8 = jnp.where(lane < BLOCK, 2.0 / jnp.maximum(positives, 1.0), 0.0)
        columns(cto8, idc)
        eio[...] = positives[0:1] / jnp.maximum(positives[0:1], 1.0)

    def on_diagonal(rows):
        r = lax.broadcasted_iota(jnp.int32, (rows, 128), 0)
        c = lax.broadcasted_iota(jnp.int32, (rows, 128), 1)
        return (r == c) & (r < BLOCK)

    def score(r0, rows, c0, cols):
        at = pl.ds(r0, rows)
        acc = lax.dot_general(au[at, :], ku[pl.ds(c0, cols), :], NT, preferred_element_type=F32)
        total = None
        for t in range(cols // 128):
            here = pl.ds(c0 + t * 128, 128)
            s = acc[:, t * 128 : (t + 1) * 128]
            w[at, here] = s
            e = jnp.exp2(s * (10.0 * LOG2E))
            if r0 == 0 and c0 + t == 0:
                e = jnp.where(on_diagonal(rows), 0.0, e)
            cs[:, here] += jnp.sum(e.reshape(rows // 8, 8, 128), axis=0)
            total = e if t == 0 else total + e
        est[at, :] += total

    def positives():
        for r in range(0, ANCHORS, 32):
            at = pl.ds(r, 32)
            label = labc[at, :]
            total = jnp.zeros((32, 128), F32)
            for c in range(0, KEYS, 128):
                here = pl.ds(c, 128)
                same = label == klab[0:1, here]
                if c == 0 and r < BLOCK:
                    i = lax.broadcasted_iota(jnp.int32, (32, 128), 0) + r
                    same = same & (i != lax.broadcasted_iota(jnp.int32, (32, 128), 1))
                total = total + jnp.where(same, w[at, here], 0.0)
            pst[at, :] = total

    def need(r0, rows, c0, cols):
        wants = set()
        for dz, p in A_POS.items():
            if dz and p * BLOCK < r0 + rows and (p + 1) * BLOCK > r0:
                wants |= {("A", dz, h) for h in range(PIECES)}
        for s in (0, 1):
            for dq, dp in K_ORDER:
                k0 = key_row(s, dq, dp)
                if k0 < c0 + cols and k0 + BLOCK > c0 and (s, dq, dp) != (0, 0, 0):
                    wants |= {("S" if s else "K", dq, dp, h) for h in range(PIECES)}
        return wants

    work = [("count", r) for r in range(0, ANCHORS, 192)]
    for r0, rows, c0, c1, wide in (
        (0, 288, 0, GROUP, 256),
        (288, 192, 0, GROUP, 256),
        (0, 480, GROUP, 2 * GROUP, 256),
        (480, 192, 0, 2 * GROUP, 256),
        (0, 672, 2 * GROUP, 3 * GROUP, 256),
        (672, 96, 0, 3 * GROUP, GROUP),
        (0, 768, 3 * GROUP, 4 * GROUP, 256),
    ):
        work += [(r0, rows, c, wide) for c in range(c0, c1, wide)]
    work.insert(10, ("done",))

    seen = set()

    def receive(what):
        if what in seen:
            return
        seen.add(what)
        if what[0] == "A":
            arrived(what, a_ref(what[1], what[2]))
        else:
            arrived(what, k_ref(1 if what[0] == "S" else 0, *what[1:]))
        if what[0] != "S":
            hand_on(what)

    def can_run(wants):
        return all(v in seen for v in wants if v[0] != "S")

    def do(job):
        if job[0] == "count":
            count(job[1])
        elif job[0] == "done":
            counts_ready()
        else:
            for v in sorted(need(*job) - seen):
                receive(v)
            score(*job)

    left = list(range(len(work)))
    for n, what in enumerate(ARRIVALS):
        receive(what)
        if n == LABELS_AT:
            labels_ready()
        for i in JOBS_AFTER.get(n, ()):
            do(work[i])
            left.remove(i)
    for i in left:
        do(work[i])

    gathered_by = len(pending)
    tiles = [jnp.sum(cs[:, t * 128 : (t + 1) * 128], axis=0, keepdims=True) for t in range(KEYS // 128)]
    for s in (0, 1):
        for dq, dp in K_ORDER:
            t, off = divmod(key_row(s, dq, dp), 128)
            line = tiles[t]
            if off:
                line = pltpu.roll(line, 128 - off, 1)
                if off + BLOCK > 128:
                    line = jnp.where(lane < 128 - off, line, pltpu.roll(tiles[t + 1], 128 - off, 1))
            r = s * 16 + dq * 4 + dp
            kso[r : r + 1, :] = line
    post(("X",), kso, ksi, chip(0, 0, True))
    lines(est, eto)
    exchange("E", eto, eti)
    arrived(("X",), ksi)
    both = [kso[0:16, :] + ksi[16:32, :], kso[16:32, :] + ksi[0:16, :]]
    kvo[0:16, :] = both[0].astype(BF16)
    kvo[16:32, :] = both[1].astype(BF16)
    plane = [(dq, dp) for dq, dp in reversed(K_ORDER) if (dq, dp) != (0, 0)]
    for dq, dp in plane:
        post(("V", dq, dp), kvo, kvi.at[dq * 4 + dp], chip(-dp, -dq, False))
    real = lane < BLOCK
    totals = jnp.where(real, gathered("E", eto, eti), 1.0)
    inverse_total = 1.0 / totals
    columns(inverse_total, iec)
    positives()
    sent(gathered_by)
    share = jnp.sum(pst[0:ANCHORS, :] * idc[...], axis=0, keepdims=True) * -5.0
    tail = jnp.where(real, eio[...] * jnp.log(totals[0:1]), 0.0)
    lz[...] = share + tail
    for dz in range(1, N_Z):
        post(("P", 8 - dz), lz, lzi.at[8 - dz], up(dz))
    for dq, dp in plane:
        arrived(("V", dq, dp), kvi.at[dq * 4 + dp])
    within = lax.broadcasted_iota(jnp.int32, (16, 128), 0) % 4
    turned = []
    for s in (0, 1):
        total = both[s]
        for b in range(4):
            by_q = None
            for a in range(4):
                dq, dp = (b, a) if s else (a, b)
                if (dq, dp) == (0, 0):
                    continue
                value = kvi[dq * 4 + dp, s * 16 : s * 16 + 16, :].astype(F32)
                if a:
                    value = pltpu.roll(value, 4 * a, 0)
                by_q = value if by_q is None else by_q + value
            if b:
                by_q = jnp.where(within < b, pltpu.roll(by_q, 12 + b, 0), pltpu.roll(by_q, b, 0))
            total = total + by_q
        inverse = 1.0 / total
        turned.append([pltpu.roll(inverse, shift, 1) if shift else inverse for shift in SHIFTS])

    def inverse_line(s, q):
        dq, dp = K_ORDER[q]
        r = dq * 4 + dp
        return turned[s][q % 4][r : r + 1, :]

    key_line(inverse_line, kie)

    def coupling(r0, rows):
        for r in range(r0, r0 + rows, 16):
            at = pl.ds(r, 16)
            ie, d2, label = iec[at, :], idc[at, :], labc[at, :]
            for c in range(0, KEYS, 128):
                here = pl.ds(c, 128)
                same = label == klab[0:1, here]
                e = jnp.exp2(w[at, here] * (10.0 * LOG2E))
                if c == 0 and r < BLOCK:
                    i = lax.broadcasted_iota(jnp.int32, (16, 128), 0) + r
                    other = i != lax.broadcasted_iota(jnp.int32, (16, 128), 1)
                    same, e = same & other, jnp.where(other, e, 0.0)
                v = e * (ie + kie[0:1, here]) - jnp.where(same, d2, 0.0)
                cm[at, here] = v.astype(BF16)

    def product(j, r0, rows):
        at = pl.ds(r0, rows)
        g[j, at, :] = jnp.dot(cm[at, :], ku[:, j * WIDE : (j + 1) * WIDE], preferred_element_type=F32)

    def part(j, dz, first, n):
        return g[j, pl.ds(A_POS[dz] * BLOCK + first, n), :]

    def push(j, step):
        for way, sign in enumerate((1, -1)):
            dz = (sign * (4 - step)) % 8
            at, n = (way * HALF, HALF) if step == 0 else (0, BLOCK)
            value = part(j, dz, at, n)
            rows = pl.ds(at, n)
            if step == 1:
                half = pl.ds(way * HALF, HALF)
                arrived(("R", j, way, 0), rb.at[j, way, 0, half, :])
                pieces = [value[:HALF], value[HALF:]]
                pieces[way] = pieces[way] + rb[j, way, 0, half, :].astype(F32)
                sb[j, way, step, 0:HALF, :] = pieces[0].astype(BF16)
                sb[j, way, step, HALF:BLOCK, :] = pieces[1].astype(BF16)
            else:
                if step > 1:
                    arrived(("R", j, way, step - 1), rb.at[j, way, step - 1])
                    value = value + rb[j, way, step - 1].astype(F32)
                sb[j, way, step, rows, :] = value.astype(BF16)
            post(("R", j, way, step), sb.at[j, way, step, rows, :], rb.at[j, way, step, rows, :], up(sign))

    coupling(672, 96)
    for j in range(CHUNKS):
        product(j, 672, 96)
        push(j, 0)
    coupling(480, 192)
    for j in range(CHUNKS):
        product(j, 480, 192)
    coupling(288, 192)
    for j in range(CHUNKS):
        push(j, 1)
        product(j, 288, 192)
    coupling(96, 192)
    for j in range(CHUNKS):
        product(j, 96, 192)
    coupling(0, 96)
    whole = lz[...]
    for dz in range(1, N_Z):
        arrived(("P", dz), lzi.at[dz])
        whole = whole + lzi[dz]
    lo[...] = whole
    before = len(pending)
    for j in range(CHUNKS):
        push(j, 2)
        product(j, 0, 96)
        for s, dq, dp in peers[j::CHUNKS]:
            post(("W", s, dq, dp), lo, li.at[key_slot(s, dq, dp)], chip(-dp, -dq, s))
    for j in range(CHUNKS):
        push(j, 3)
    sent(before)

    every = lo[...]
    for s, dq, dp in peers:
        arrived(("W", s, dq, dp), li.at[key_slot(s, dq, dp)])
        every = every + li[key_slot(s, dq, dp)]
    loss[...] = jnp.broadcast_to(jnp.sum(every, axis=1, keepdims=True) * (1.0 / TOKENS), (1, 128))

    sent(len(pending) - 2 * CHUNKS)
    along = jnp.zeros((BLOCK, 1), F32)
    for j in range(CHUNKS):
        value = part(j, 0, 0, BLOCK)
        for way in (0, 1):
            arrived(("R", j, way, 3), rb.at[j, way, 3])
            value = value + rb[j, way, 3].astype(F32)
        value = value * 10.0
        g[j, pl.ds(0, BLOCK), :] = value
        along = along + jnp.sum(uf[:, j * WIDE : (j + 1) * WIDE] * value, axis=1, keepdims=True)
    scale = inv[:, 0:1]
    for j in range(CHUNKS):
        cut = slice(j * WIDE, (j + 1) * WIDE)
        grad[:, cut] = (g[j, pl.ds(0, BLOCK), :] - uf[:, cut] * along) * scale

    sent(len(pending))
    assert len(number.numbers) <= N_SEM


def per_device(embeddings, labels):
    vmem = pl.BlockSpec(memory_space=pltpu.VMEM)
    line = labels.reshape(1, BLOCK)
    scratch = [
        ((BLOCK, DEPTH), BF16),
        ((1, BLOCK), jnp.int32),
        ((ANCHORS, DEPTH), BF16),
        ((KEYS, DEPTH), BF16),
        ((ANCHORS, KEYS), F32),
        ((ANCHORS, KEYS), BF16),
        ((CHUNKS, ANCHORS, WIDE), F32),
        ((BLOCK, DEPTH), F32),
        ((BLOCK, 128), F32),
        ((4, 1, 128), F32),
        ((N_Z, 1, 128), F32),
        ((32, 1, 128), F32),
        ((ANCHORS, 128), F32),
        ((8, KEYS), F32),
        ((ANCHORS + 32, 128), F32),
        ((ANCHORS + 32, 128), F32),
        ((ANCHORS + 32, 128), F32),
        ((N_Z, 128), F32),
        ((N_Z, N_Z, 128), F32),
        ((N_Z, 128), F32),
        ((N_Z, N_Z, 128), F32),
        ((1, 128), F32),
        ((ANCHORS, 128), F32),
        ((ANCHORS, 128), F32),
        ((8, KEYS), F32),
        ((32, 128), F32),
        ((32, 128), F32),
        ((32, 128), BF16),
        ((16, 32, 128), BF16),
        ((8, KEYS), F32),
        ((1, 128), F32),
        ((N_Z, 1, 128), F32),
        ((1, 128), F32),
        ((32, 1, 128), F32),
        ((CHUNKS, 2, 4, BLOCK, WIDE), BF16),
        ((CHUNKS, 2, 4, BLOCK, WIDE), BF16),
    ]
    grad, loss = pl.pallas_call(
        kernel,
        out_shape=(
            pltpu.VMEM((BLOCK, DEPTH), F32),
            jax.ShapeDtypeStruct((1, 128), F32),
        ),
        in_specs=[pl.BlockSpec(memory_space=pl.ANY)] * 2,
        out_specs=(vmem, vmem),
        scratch_shapes=[pltpu.VMEM(s, t) for s, t in scratch]
        + [pltpu.SemaphoreType.DMA((2,)), pltpu.SemaphoreType.DMA((N_SEM,)), pltpu.SemaphoreType.DMA((N_SEM,))],
        compiler_params=pltpu.CompilerParams(
            collective_id=0, has_side_effects=True, vmem_limit_bytes=60 * 2**20
        ),
        cost_estimate=pl.CostEstimate(flops=2 * 2 * ANCHORS * KEYS * DEPTH, bytes_accessed=2**20, transcendentals=0),
    )(embeddings, line)
    return grad, loss[0, 0]


def solution(mesh):
    placed = (P(("row", "col"), None), P(("row", "col")))
    return jax.shard_map(
        per_device,
        mesh=mesh,
        in_specs=placed,
        out_specs=(P(("row", "col"), None), P()),
        check_vma=False,
    )
```

```python
import jax
import jax.numpy as jnp
from jax import lax
from jax.experimental import pallas as pl
from jax.experimental.pallas import tpu as pltpu
from jax.sharding import PartitionSpec as P

F32 = jnp.float32
BF16 = jnp.bfloat16
MESH = pl.DeviceIdType.MESH
LOG2E = 1.4426950408889634
NT = (((1,), (1,)), ((), ()))

BLOCK = 96
HALF = 48
PIECES = 3
PIECE = BLOCK // PIECES
DEPTH = 1024
N_Z = 8
ANCHORS = N_Z * BLOCK
KEYS = 32 * BLOCK
GROUP = 8 * BLOCK
CHUNKS = 4
WIDE = DEPTH // CHUNKS
TOKENS = 24576

A_POS = {0: 0, 7: 1, 1: 2, 6: 3, 2: 4, 5: 5, 3: 6, 4: 7}
K_ORDER = [
    (0, 0), (0, 3), (0, 1), (3, 0),
    (1, 0), (3, 3), (1, 3), (3, 1),
    (0, 2), (1, 1), (2, 0), (2, 3),
    (1, 2), (3, 2), (2, 1), (2, 2),
]
K_POS = {d: i for i, d in enumerate(K_ORDER)}
SHIFTS = (0, 96, 64, 32)
ARRIVALS = [
    ("K", 0, 3, 0), ("K", 0, 1, 0), ("K", 0, 3, 1), ("K", 0, 1, 1), ("A", 7, 0), ("A", 1, 0),
    ("K", 0, 3, 2), ("K", 0, 1, 2), ("K", 3, 0, 0), ("K", 1, 0, 0), ("A", 7, 1), ("A", 1, 1),
    ("K", 3, 0, 1), ("K", 1, 0, 1), ("K", 3, 0, 2), ("K", 1, 0, 2), ("A", 7, 2), ("A", 1, 2),
    ("K", 1, 3, 0), ("K", 0, 2, 0), ("K", 3, 3, 0), ("K", 1, 1, 0), ("K", 3, 1, 0), ("K", 1, 3, 1),
    ("A", 6, 0), ("A", 2, 0), ("K", 3, 3, 1), ("K", 1, 1, 1), ("K", 0, 2, 1), ("K", 3, 1, 1),
    ("A", 6, 1), ("A", 2, 1), ("K", 3, 3, 2), ("K", 1, 3, 2), ("K", 3, 1, 2), ("A", 6, 2),
    ("A", 2, 2), ("K", 0, 2, 2), ("K", 1, 1, 2), ("K", 2, 0, 0), ("K", 2, 0, 1), ("K", 2, 0, 2),
    ("K", 3, 2, 0), ("K", 1, 2, 0), ("K", 2, 3, 0), ("K", 2, 3, 1), ("A", 5, 0), ("A", 3, 0),
    ("K", 2, 1, 0), ("K", 1, 2, 1), ("K", 3, 2, 1), ("K", 2, 3, 2), ("A", 5, 1), ("A", 3, 1),
    ("K", 2, 1, 1), ("K", 1, 2, 2), ("K", 3, 2, 2), ("A", 3, 2), ("A", 5, 2), ("K", 2, 1, 2),
    ("K", 2, 2, 0), ("K", 2, 2, 1), ("K", 2, 2, 2), ("A", 4, 2), ("A", 4, 0), ("A", 4, 1),
]
LABELS_AT = 17
JOBS_AFTER = {
    17: (0,), 18: (1, 2), 21: (3, 4), 25: (5,), 26: (6,), 36: (7, 8, 9, 11), 41: (12, 13), 44: (10,), 58: (14,), 59: (15, 16, 17), 60: (18, 19, 20), 61: (21, 22),
}


def key_row(core, dq, dp):
    q = K_POS[(dq, dp)]
    return (q // 4) * GROUP + core * (GROUP // 2) + (q % 4) * BLOCK


def key_slot(core, dq, dp):
    return core * 16 + K_POS[(dq, dp)]


class Semaphores:
    def __init__(self):
        self.numbers = {}

    def __call__(self, name):
        return self.numbers.setdefault(name, len(self.numbers))


N_SEM = 260


def kernel(emb, lab, grad, loss,
           own, own_line, au, ku, w, cm, g, uf, inv,
           var, al, kl, labc, klab,
           est, pst, cst, cto, cti, eto, eti, eio, iec, idc, cs, kso, ksi, kvo, kvi, kie,
           lz, lzi, lo, li, sb, rb, load, send, recv):
    row, z = lax.axis_index("row"), lax.axis_index("col")
    core, x, y = row % 2, (row // 2) % 4, row // 8
    number = Semaphores()
    pending = []

    def chip(dp, dq, other):
        px = (x + dp + core * (dq - dp) + 8) % 4
        py = (y + dq + core * (dp - dq) + 8) % 4
        pc = 1 - core if other else core
        return ((py * 4 + px) * 2 + pc, z)

    def up(dz):
        return (row, (z + dz + 8) % 8)

    def message(name, src, dst, to):
        i = number(name)
        return pltpu.make_async_remote_copy(
            src_ref=src, dst_ref=dst, send_sem=send.at[i], recv_sem=recv.at[i], device_id=to, device_id_type=MESH
        )

    def post(name, src, dst, to):
        copy = message(name, src, dst, to)
        copy.start()
        pending.append(copy)

    def sent(n):
        for copy in pending[:n]:
            copy.wait_send()
        del pending[:n]

    def arrived(name, dst):
        message(name, dst, dst, up(1)).wait_recv()

    def a_ref(dz, h):
        return au.at[pl.ds(A_POS[dz] * BLOCK + h * PIECE, PIECE), :]

    def k_ref(s, dq, dp, h):
        return ku.at[pl.ds(key_row(s, dq, dp) + h * PIECE, PIECE), :]

    peers = [(s, dq, dp) for s in (0, 1) for dq, dp in K_ORDER if (s, dq, dp) != (0, 0, 0)]

    barrier = pltpu.get_barrier_semaphore()
    for dz in range(1, N_Z):
        pl.semaphore_signal(barrier, inc=1, device_id=up(dz), device_id_type=MESH)
    for s, dq, dp in peers:
        pl.semaphore_signal(barrier, inc=1, device_id=chip(-dp, -dq, s), device_id_type=MESH)

    fetch = pltpu.make_async_copy(emb, own, load.at[0])
    fetch.start()
    fetch_line = pltpu.make_async_copy(lab, own_line, load.at[1])
    fetch_line.start()
    est[...] = jnp.zeros_like(est)
    cst[...] = jnp.zeros_like(cst)
    cs[...] = jnp.zeros_like(cs)
    al[0] = jnp.zeros((1, 128), F32)
    fetch_line.wait()
    al[0, :, 0:BLOCK] = own_line[...].astype(F32)
    own_label = al[0]
    for p, shift in enumerate(SHIFTS):
        var[p] = pltpu.roll(own_label, shift, 1) if shift else own_label
    kl[0] = own_label
    fetch.wait()
    wide = own[...].astype(F32)
    scale = lax.rsqrt(jnp.sum(wide * wide, axis=1, keepdims=True) + 1e-6)
    unit = wide * scale
    uf[...] = unit
    inv[...] = jnp.broadcast_to(scale, (BLOCK, 128))
    rounded = unit.astype(BF16)
    au[pl.ds(0, BLOCK), :] = rounded
    ku[pl.ds(0, BLOCK), :] = rounded
    pl.semaphore_wait(barrier, N_Z - 1 + len(peers))

    def upward(dp, h):
        return h == 0 or (h == 1 and dp < 2)

    def ways_of(what):
        if what[0] == "A":
            _, dz, h = what
            if dz == 0:
                return [(0, 0, 1, 0, ("A", 7, h)), (0, 0, -1, 0, ("A", 1, h))]
            if dz in (7, 6) or (dz == 5 and upward(0, h)):
                return [(0, 0, 1, 0, ("A", dz - 1, h))]
            if dz in (1, 2) or (dz == 3 and not upward(0, h)):
                return [(0, 0, -1, 0, ("A", dz + 1, h))]
            return []
        _, dq, dp, h = what
        ways = []
        if (dq, dp) == (0, 0):
            ways += [(1, 0, 0, 0, ("K", 0, 3, h)), (-1, 0, 0, 0, ("K", 0, 1, h))]
        elif (dq, dp) == (0, 3) and upward(2, h):
            ways += [(1, 0, 0, 0, ("K", 0, 2, h))]
        elif (dq, dp) == (0, 1) and not upward(2, h):
            ways += [(-1, 0, 0, 0, ("K", 0, 2, h))]
        if dq == 0:
            ways += [(0, 1, 0, 0, ("K", 3, dp, h)), (0, -1, 0, 0, ("K", 1, dp, h))]
        elif dq == 3 and upward(dp, h):
            ways += [(0, 1, 0, 0, ("K", 2, dp, h))]
        elif dq == 1 and not upward(dp, h):
            ways += [(0, -1, 0, 0, ("K", 2, dp, h))]
        return ways + [(0, 0, 0, 1, ("S", dq, dp, h))]

    def place(what):
        if what[0] == "A":
            return a_ref(what[1], what[2])
        return k_ref(1 if what[0] == "S" else 0, *what[1:])

    def forward(what, way):
        tp, tq, tz, ts, there = way
        post(there, place(what), place(there), up(tz) if tz else chip(tp, tq, bool(ts)))

    def hand_on(what):
        for way in ways_of(what):
            forward(what, way)

    for axes in ((0, 2), (1,), (3,)):
        for h in range(PIECES):
            for what in (("K", 0, 0, h), ("A", 0, h)):
                for way in ways_of(what):
                    if any(way[i] for i in axes):
                        forward(what, way)
    for dz in range(1, N_Z):
        post(("L", 8 - dz), al.at[0], al.at[8 - dz], up(dz))
    for s, dq, dp in peers:
        post(("M", s, dq, dp), var.at[K_POS[(dq, dp)] % 4], kl.at[key_slot(s, dq, dp)], chip(-dp, -dq, s))

    lane = lax.broadcasted_iota(jnp.int32, (1, 128), 1)

    def columns(rows, out):
        turned = jnp.transpose(jnp.concatenate([rows, jnp.zeros((128 - N_Z, 128), F32)], axis=0))
        for dz, p in A_POS.items():
            out[pl.ds(p * BLOCK, BLOCK), :] = jnp.broadcast_to(turned[:BLOCK, dz : dz + 1], (BLOCK, 128))

    def lines(stat, out):
        for dz in range(N_Z):
            part = jnp.transpose(stat[pl.ds(A_POS[dz] * BLOCK, 128), :])
            out[dz : dz + 1, :] = jnp.sum(part, axis=0, keepdims=True)

    def exchange(name, out, into):
        for dz in (4, 3, 5, 2, 6, 1, 7):
            post((name, 8 - dz), out, into.at[8 - dz], up(dz))

    def gathered(name, out, into):
        total = out[...]
        for dz in range(1, N_Z):
            arrived((name, dz), into.at[dz])
            total = total + pltpu.roll(into[dz], dz, 0)
        return total

    def key_line(line_of, out):
        for s in (0, 1):
            for q in range(4):
                m = [line_of(s, q * 4 + p) for p in range(4)]
                base = q * GROUP + s * (GROUP // 2)
                for t, (cut, a, b) in enumerate(((96, 0, 1), (64, 1, 2), (32, 2, 3))):
                    line = jnp.where(lane < cut, m[a], m[b])
                    out[:, pl.ds(base + t * 128, 128)] = jnp.broadcast_to(line, (8, 128))

    def labels_ready():
        for dz in range(1, N_Z):
            arrived(("L", dz), al.at[dz])
        for s, dq, dp in peers:
            arrived(("M", s, dq, dp), kl.at[key_slot(s, dq, dp)])
        columns(jnp.concatenate([al[dz] for dz in range(N_Z)], axis=0), labc)
        key_line(lambda s, q: kl[s * 16 + q], klab)

    def count(r0):
        for r in range(r0, r0 + 192, 32):
            label = labc[pl.ds(r, 32), :]
            total = jnp.zeros((32, 128), F32)
            for t in range(KEYS // 128):
                total = total + jnp.where(label == klab[0:1, t * 128 : (t + 1) * 128], 1.0, 0.0)
            cst[pl.ds(r, 32), :] = total
        if r0 == ANCHORS - 192:
            lines(cst, cto)
            exchange("C", cto, cti)

    def counts_ready():
        positives = gathered("C", cto, cti) - 1.0
        cto8 = jnp.where(lane < BLOCK, 2.0 / jnp.maximum(positives, 1.0), 0.0)
        columns(cto8, idc)
        eio[...] = positives[0:1] / jnp.maximum(positives[0:1], 1.0)

    def on_diagonal(rows):
        r = lax.broadcasted_iota(jnp.int32, (rows, 128), 0)
        c = lax.broadcasted_iota(jnp.int32, (rows, 128), 1)
        return (r == c) & (r < BLOCK)

    def score(r0, rows, c0, cols):
        at = pl.ds(r0, rows)
        acc = lax.dot_general(au[at, :], ku[pl.ds(c0, cols), :], NT, preferred_element_type=F32)
        total = None
        for t in range(cols // 128):
            here = pl.ds(c0 + t * 128, 128)
            s = acc[:, t * 128 : (t + 1) * 128]
            w[at, here] = s
            e = jnp.exp2(s * (10.0 * LOG2E))
            if r0 == 0 and c0 + t == 0:
                e = jnp.where(on_diagonal(rows), 0.0, e)
            cs[:, here] += jnp.sum(e.reshape(rows // 8, 8, 128), axis=0)
            total = e if t == 0 else total + e
        est[at, :] += total

    def positives():
        for r in range(0, ANCHORS, 32):
            at = pl.ds(r, 32)
            label = labc[at, :]
            total = jnp.zeros((32, 128), F32)
            for c in range(0, KEYS, 128):
                here = pl.ds(c, 128)
                same = label == klab[0:1, here]
                if c == 0 and r < BLOCK:
                    i = lax.broadcasted_iota(jnp.int32, (32, 128), 0) + r
                    same = same & (i != lax.broadcasted_iota(jnp.int32, (32, 128), 1))
                total = total + jnp.where(same, w[at, here], 0.0)
            pst[at, :] = total

    def need(r0, rows, c0, cols):
        wants = set()
        for dz, p in A_POS.items():
            if dz and p * BLOCK < r0 + rows and (p + 1) * BLOCK > r0:
                wants |= {("A", dz, h) for h in range(PIECES)}
        for s in (0, 1):
            for dq, dp in K_ORDER:
                k0 = key_row(s, dq, dp)
                if k0 < c0 + cols and k0 + BLOCK > c0 and (s, dq, dp) != (0, 0, 0):
                    wants |= {("S" if s else "K", dq, dp, h) for h in range(PIECES)}
        return wants

    work = [("count", r) for r in range(0, ANCHORS, 192)]
    for r0, rows, c0, c1, wide in (
        (0, 288, 0, GROUP, 256),
        (288, 192, 0, GROUP, 256),
        (0, 480, GROUP, 2 * GROUP, 256),
        (480, 192, 0, 2 * GROUP, 256),
        (0, 672, 2 * GROUP, 3 * GROUP, 256),
        (672, 96, 0, 3 * GROUP, GROUP),
        (0, 768, 3 * GROUP, 4 * GROUP, 256),
    ):
        work += [(r0, rows, c, wide) for c in range(c0, c1, wide)]
    work.insert(10, ("done",))

    seen = set()

    def receive(what):
        if what in seen:
            return
        seen.add(what)
        if what[0] == "A":
            arrived(what, a_ref(what[1], what[2]))
        else:
            arrived(what, k_ref(1 if what[0] == "S" else 0, *what[1:]))
        if what[0] != "S":
            hand_on(what)

    def can_run(wants):
        return all(v in seen for v in wants if v[0] != "S")

    def do(job):
        if job[0] == "count":
            count(job[1])
        elif job[0] == "done":
            counts_ready()
        else:
            for v in sorted(need(*job) - seen):
                receive(v)
            score(*job)

    left = list(range(len(work)))
    for n, what in enumerate(ARRIVALS):
        receive(what)
        if n == LABELS_AT:
            labels_ready()
        for i in JOBS_AFTER.get(n, ()):
            do(work[i])
            left.remove(i)
    for i in left:
        do(work[i])

    gathered_by = len(pending)
    tiles = [jnp.sum(cs[:, t * 128 : (t + 1) * 128], axis=0, keepdims=True) for t in range(KEYS // 128)]
    for s in (0, 1):
        for dq, dp in K_ORDER:
            t, off = divmod(key_row(s, dq, dp), 128)
            line = tiles[t]
            if off:
                line = pltpu.roll(line, 128 - off, 1)
                if off + BLOCK > 128:
                    line = jnp.where(lane < 128 - off, line, pltpu.roll(tiles[t + 1], 128 - off, 1))
            r = s * 16 + dq * 4 + dp
            kso[r : r + 1, :] = line
    post(("X",), kso, ksi, chip(0, 0, True))
    lines(est, eto)
    exchange("E", eto, eti)
    arrived(("X",), ksi)
    both = [kso[0:16, :] + ksi[16:32, :], kso[16:32, :] + ksi[0:16, :]]
    kvo[0:16, :] = both[0].astype(BF16)
    kvo[16:32, :] = both[1].astype(BF16)
    plane = [(dq, dp) for dq, dp in reversed(K_ORDER) if (dq, dp) != (0, 0)]
    for dq, dp in plane:
        post(("V", dq, dp), kvo, kvi.at[dq * 4 + dp], chip(-dp, -dq, False))
    positives()
    sent(gathered_by)
    real = lane < BLOCK
    totals = jnp.where(real, gathered("E", eto, eti), 1.0)
    inverse_total = 1.0 / totals
    columns(inverse_total, iec)
    share = jnp.sum(pst[0:ANCHORS, :] * idc[...], axis=0, keepdims=True) * -5.0
    tail = jnp.where(real, eio[...] * jnp.log(totals[0:1]), 0.0)
    lz[...] = share + tail
    for dz in range(1, N_Z):
        post(("P", 8 - dz), lz, lzi.at[8 - dz], up(dz))
    for dq, dp in plane:
        arrived(("V", dq, dp), kvi.at[dq * 4 + dp])
    within = lax.broadcasted_iota(jnp.int32, (16, 128), 0) % 4
    turned = []
    for s in (0, 1):
        total = both[s]
        for b in range(4):
            by_q = None
            for a in range(4):
                dq, dp = (b, a) if s else (a, b)
                if (dq, dp) == (0, 0):
                    continue
                value = kvi[dq * 4 + dp, s * 16 : s * 16 + 16, :].astype(F32)
                if a:
                    value = pltpu.roll(value, 4 * a, 0)
                by_q = value if by_q is None else by_q + value
            if b:
                by_q = jnp.where(within < b, pltpu.roll(by_q, 12 + b, 0), pltpu.roll(by_q, b, 0))
            total = total + by_q
        inverse = 1.0 / total
        turned.append([pltpu.roll(inverse, shift, 1) if shift else inverse for shift in SHIFTS])

    def inverse_line(s, q):
        dq, dp = K_ORDER[q]
        r = dq * 4 + dp
        return turned[s][q % 4][r : r + 1, :]

    key_line(inverse_line, kie)

    def coupling(r0, rows):
        for r in range(r0, r0 + rows, 16):
            at = pl.ds(r, 16)
            ie, d2, label = iec[at, :], idc[at, :], labc[at, :]
            for c in range(0, KEYS, 128):
                here = pl.ds(c, 128)
                same = label == klab[0:1, here]
                e = jnp.exp2(w[at, here] * (10.0 * LOG2E))
                if c == 0 and r < BLOCK:
                    i = lax.broadcasted_iota(jnp.int32, (16, 128), 0) + r
                    other = i != lax.broadcasted_iota(jnp.int32, (16, 128), 1)
                    same, e = same & other, jnp.where(other, e, 0.0)
                v = e * (ie + kie[0:1, here]) - jnp.where(same, d2, 0.0)
                cm[at, here] = v.astype(BF16)

    def product(j, r0, rows):
        at = pl.ds(r0, rows)
        g[j, at, :] = jnp.dot(cm[at, :], ku[:, j * WIDE : (j + 1) * WIDE], preferred_element_type=F32)

    def part(j, dz, first, n):
        return g[j, pl.ds(A_POS[dz] * BLOCK + first, n), :]

    def push(j, step):
        for way, sign in enumerate((1, -1)):
            dz = (sign * (4 - step)) % 8
            at, n = (way * HALF, HALF) if step == 0 else (0, BLOCK)
            value = part(j, dz, at, n)
            rows = pl.ds(at, n)
            if step == 1:
                half = pl.ds(way * HALF, HALF)
                arrived(("R", j, way, 0), rb.at[j, way, 0, half, :])
                pieces = [value[:HALF], value[HALF:]]
                pieces[way] = pieces[way] + rb[j, way, 0, half, :].astype(F32)
                sb[j, way, step, 0:HALF, :] = pieces[0].astype(BF16)
                sb[j, way, step, HALF:BLOCK, :] = pieces[1].astype(BF16)
            else:
                if step > 1:
                    arrived(("R", j, way, step - 1), rb.at[j, way, step - 1])
                    value = value + rb[j, way, step - 1].astype(F32)
                sb[j, way, step, rows, :] = value.astype(BF16)
            post(("R", j, way, step), sb.at[j, way, step, rows, :], rb.at[j, way, step, rows, :], up(sign))

    coupling(672, 96)
    for j in range(CHUNKS):
        product(j, 672, 96)
        push(j, 0)
    coupling(480, 192)
    for j in range(CHUNKS):
        product(j, 480, 192)
    coupling(288, 192)
    for j in range(CHUNKS):
        push(j, 1)
        product(j, 288, 192)
    coupling(96, 192)
    for j in range(CHUNKS):
        product(j, 96, 192)
    coupling(0, 96)
    whole = lz[...]
    for dz in range(1, N_Z):
        arrived(("P", dz), lzi.at[dz])
        whole = whole + lzi[dz]
    lo[...] = whole
    before = len(pending)
    for j in range(CHUNKS):
        push(j, 2)
        product(j, 0, 96)
        for s, dq, dp in peers[j::CHUNKS]:
            post(("W", s, dq, dp), lo, li.at[key_slot(s, dq, dp)], chip(-dp, -dq, s))
    for j in range(CHUNKS):
        push(j, 3)
    sent(before)

    every = lo[...]
    for s, dq, dp in peers:
        arrived(("W", s, dq, dp), li.at[key_slot(s, dq, dp)])
        every = every + li[key_slot(s, dq, dp)]
    loss[...] = jnp.broadcast_to(jnp.sum(every, axis=1, keepdims=True) * (1.0 / TOKENS), (1, 128))

    sent(len(pending) - 2 * CHUNKS)
    along = jnp.zeros((BLOCK, 1), F32)
    for j in range(CHUNKS):
        value = part(j, 0, 0, BLOCK)
        for way in (0, 1):
            arrived(("R", j, way, 3), rb.at[j, way, 3])
            value = value + rb[j, way, 3].astype(F32)
        value = value * 10.0
        g[j, pl.ds(0, BLOCK), :] = value
        along = along + jnp.sum(uf[:, j * WIDE : (j + 1) * WIDE] * value, axis=1, keepdims=True)
    scale = inv[:, 0:1]
    for j in range(CHUNKS):
        cut = slice(j * WIDE, (j + 1) * WIDE)
        grad[:, cut] = (g[j, pl.ds(0, BLOCK), :] - uf[:, cut] * along) * scale

    sent(len(pending))
    assert len(number.numbers) <= N_SEM


def per_device(embeddings, labels):
    vmem = pl.BlockSpec(memory_space=pltpu.VMEM)
    line = labels.reshape(1, BLOCK)
    scratch = [
        ((BLOCK, DEPTH), BF16),
        ((1, BLOCK), jnp.int32),
        ((ANCHORS, DEPTH), BF16),
        ((KEYS, DEPTH), BF16),
        ((ANCHORS, KEYS), F32),
        ((ANCHORS, KEYS), BF16),
        ((CHUNKS, ANCHORS, WIDE), F32),
        ((BLOCK, DEPTH), F32),
        ((BLOCK, 128), F32),
        ((4, 1, 128), F32),
        ((N_Z, 1, 128), F32),
        ((32, 1, 128), F32),
        ((ANCHORS, 128), F32),
        ((8, KEYS), F32),
        ((ANCHORS + 32, 128), F32),
        ((ANCHORS + 32, 128), F32),
        ((ANCHORS + 32, 128), F32),
        ((N_Z, 128), F32),
        ((N_Z, N_Z, 128), F32),
        ((N_Z, 128), F32),
        ((N_Z, N_Z, 128), F32),
        ((1, 128), F32),
        ((ANCHORS, 128), F32),
        ((ANCHORS, 128), F32),
        ((8, KEYS), F32),
        ((32, 128), F32),
        ((32, 128), F32),
        ((32, 128), BF16),
        ((16, 32, 128), BF16),
        ((8, KEYS), F32),
        ((1, 128), F32),
        ((N_Z, 1, 128), F32),
        ((1, 128), F32),
        ((32, 1, 128), F32),
        ((CHUNKS, 2, 4, BLOCK, WIDE), BF16),
        ((CHUNKS, 2, 4, BLOCK, WIDE), BF16),
    ]
    grad, loss = pl.pallas_call(
        kernel,
        out_shape=(
            pltpu.VMEM((BLOCK, DEPTH), F32),
            jax.ShapeDtypeStruct((1, 128), F32),
        ),
        in_specs=[pl.BlockSpec(memory_space=pl.ANY)] * 2,
        out_specs=(vmem, vmem),
        scratch_shapes=[pltpu.VMEM(s, t) for s, t in scratch]
        + [pltpu.SemaphoreType.DMA((2,)), pltpu.SemaphoreType.DMA((N_SEM,)), pltpu.SemaphoreType.DMA((N_SEM,))],
        compiler_params=pltpu.CompilerParams(
            collective_id=0, has_side_effects=True, vmem_limit_bytes=60 * 2**20
        ),
        cost_estimate=pl.CostEstimate(flops=2 * 2 * ANCHORS * KEYS * DEPTH, bytes_accessed=2**20, transcendentals=0),
    )(embeddings, line)
    return grad, loss[0, 0]


def solution(mesh):
    placed = (P(("row", "col"), None), P(("row", "col")))
    return jax.shard_map(
        per_device,
        mesh=mesh,
        in_specs=placed,
        out_specs=(P(("row", "col"), None), P()),
        check_vma=False,
    )
```

```python
import jax
import jax.numpy as jnp
from jax import lax
from jax.experimental import pallas as pl
from jax.experimental.pallas import tpu as pltpu
from jax.sharding import PartitionSpec as P

F32 = jnp.float32
BF16 = jnp.bfloat16
MESH = pl.DeviceIdType.MESH
LOG2E = 1.4426950408889634
NT = (((1,), (1,)), ((), ()))

BLOCK = 96
HALF = 48
PIECES = 3
PIECE = BLOCK // PIECES
DEPTH = 1024
N_Z = 8
ANCHORS = N_Z * BLOCK
KEYS = 32 * BLOCK
GROUP = 8 * BLOCK
CHUNKS = 4
WIDE = DEPTH // CHUNKS
TOKENS = 24576

A_POS = {0: 0, 7: 1, 1: 2, 6: 3, 2: 4, 5: 5, 3: 6, 4: 7}
K_ORDER = [
    (0, 0), (0, 3), (0, 1), (3, 0),
    (1, 0), (3, 3), (1, 3), (3, 1),
    (0, 2), (1, 1), (2, 0), (2, 3),
    (1, 2), (3, 2), (2, 1), (2, 2),
]
K_POS = {d: i for i, d in enumerate(K_ORDER)}
SHIFTS = (0, 96, 64, 32)
ARRIVALS = [
    ("K", 0, 3, 0), ("K", 0, 1, 0), ("K", 0, 3, 1), ("K", 0, 1, 1), ("A", 7, 0), ("A", 1, 0),
    ("K", 0, 3, 2), ("K", 0, 1, 2), ("K", 3, 0, 0), ("K", 1, 0, 0), ("A", 7, 1), ("A", 1, 1),
    ("K", 3, 0, 1), ("K", 1, 0, 1), ("K", 3, 0, 2), ("K", 1, 0, 2), ("A", 7, 2), ("A", 1, 2),
    ("K", 1, 3, 0), ("K", 0, 2, 0), ("K", 3, 3, 0), ("K", 1, 1, 0), ("K", 3, 1, 0), ("K", 1, 3, 1),
    ("A", 6, 0), ("A", 2, 0), ("K", 3, 3, 1), ("K", 1, 1, 1), ("K", 0, 2, 1), ("K", 3, 1, 1),
    ("A", 6, 1), ("A", 2, 1), ("K", 3, 3, 2), ("K", 1, 3, 2), ("K", 3, 1, 2), ("A", 6, 2),
    ("A", 2, 2), ("K", 0, 2, 2), ("K", 1, 1, 2), ("K", 2, 0, 0), ("K", 2, 0, 1), ("K", 2, 0, 2),
    ("K", 3, 2, 0), ("K", 1, 2, 0), ("K", 2, 3, 0), ("K", 2, 3, 1), ("A", 5, 0), ("A", 3, 0),
    ("K", 2, 1, 0), ("K", 1, 2, 1), ("K", 3, 2, 1), ("K", 2, 3, 2), ("A", 5, 1), ("A", 3, 1),
    ("K", 2, 1, 1), ("K", 1, 2, 2), ("K", 3, 2, 2), ("A", 3, 2), ("A", 5, 2), ("K", 2, 1, 2),
    ("K", 2, 2, 0), ("K", 2, 2, 1), ("K", 2, 2, 2), ("A", 4, 2), ("A", 4, 0), ("A", 4, 1),
]
LABELS_AT = 17
JOBS_AFTER = {
    17: (0,), 18: (1, 2), 21: (3, 4), 25: (5,), 26: (6,), 36: (7, 8, 9, 11), 41: (12, 13), 44: (10,), 58: (14,), 59: (15, 16, 17), 60: (18, 19, 20), 61: (21, 22),
}


def key_row(core, dq, dp):
    q = K_POS[(dq, dp)]
    return (q // 4) * GROUP + core * (GROUP // 2) + (q % 4) * BLOCK


def key_slot(core, dq, dp):
    return core * 16 + K_POS[(dq, dp)]


class Semaphores:
    def __init__(self):
        self.numbers = {}

    def __call__(self, name):
        return self.numbers.setdefault(name, len(self.numbers))


N_SEM = 260


def kernel(emb, lab, grad, loss,
           own, own_line, au, ku, w, cm, g, uf, inv,
           var, al, kl, labc, klab,
           est, pst, cst, cto, cti, eto, eti, eio, iec, idc, cs, kso, ksi, kvo, kvi, kie,
           lz, lzi, lo, li, sb, rb, load, send, recv):
    row, z = lax.axis_index("row"), lax.axis_index("col")
    core, x, y = row % 2, (row // 2) % 4, row // 8
    number = Semaphores()
    pending = []

    def chip(dp, dq, other):
        px = (x + dp + core * (dq - dp) + 8) % 4
        py = (y + dq + core * (dp - dq) + 8) % 4
        pc = 1 - core if other else core
        return ((py * 4 + px) * 2 + pc, z)

    def up(dz):
        return (row, (z + dz + 8) % 8)

    def message(name, src, dst, to):
        i = number(name)
        return pltpu.make_async_remote_copy(
            src_ref=src, dst_ref=dst, send_sem=send.at[i], recv_sem=recv.at[i], device_id=to, device_id_type=MESH
        )

    def post(name, src, dst, to):
        copy = message(name, src, dst, to)
        copy.start()
        pending.append(copy)

    def sent(n):
        for copy in pending[:n]:
            copy.wait_send()
        del pending[:n]

    def arrived(name, dst):
        message(name, dst, dst, up(1)).wait_recv()

    def a_ref(dz, h):
        return au.at[pl.ds(A_POS[dz] * BLOCK + h * PIECE, PIECE), :]

    def k_ref(s, dq, dp, h):
        return ku.at[pl.ds(key_row(s, dq, dp) + h * PIECE, PIECE), :]

    peers = [(s, dq, dp) for s in (0, 1) for dq, dp in K_ORDER if (s, dq, dp) != (0, 0, 0)]

    barrier = pltpu.get_barrier_semaphore()
    for dz in range(1, N_Z):
        pl.semaphore_signal(barrier, inc=1, device_id=up(dz), device_id_type=MESH)
    for s, dq, dp in peers:
        pl.semaphore_signal(barrier, inc=1, device_id=chip(-dp, -dq, s), device_id_type=MESH)

    fetch = pltpu.make_async_copy(emb, own, load.at[0])
    fetch.start()
    fetch_line = pltpu.make_async_copy(lab, own_line, load.at[1])
    fetch_line.start()
    est[...] = jnp.zeros_like(est)
    cst[...] = jnp.zeros_like(cst)
    cs[...] = jnp.zeros_like(cs)
    al[0] = jnp.zeros((1, 128), F32)
    fetch_line.wait()
    al[0, :, 0:BLOCK] = own_line[...].astype(F32)
    own_label = al[0]
    for p, shift in enumerate(SHIFTS):
        var[p] = pltpu.roll(own_label, shift, 1) if shift else own_label
    kl[0] = own_label
    fetch.wait()
    wide = own[...].astype(F32)
    scale = lax.rsqrt(jnp.sum(wide * wide, axis=1, keepdims=True) + 1e-6)
    unit = wide * scale
    uf[...] = unit
    inv[...] = jnp.broadcast_to(scale, (BLOCK, 128))
    rounded = unit.astype(BF16)
    au[pl.ds(0, BLOCK), :] = rounded
    ku[pl.ds(0, BLOCK), :] = rounded
    pl.semaphore_wait(barrier, N_Z - 1 + len(peers))

    def upward(dp, h):
        return h == 0 or (h == 1 and dp < 2)

    def ways_of(what):
        if what[0] == "A":
            _, dz, h = what
            if dz == 0:
                return [(0, 0, 1, 0, ("A", 7, h)), (0, 0, -1, 0, ("A", 1, h))]
            if dz in (7, 6) or (dz == 5 and upward(0, h)):
                return [(0, 0, 1, 0, ("A", dz - 1, h))]
            if dz in (1, 2) or (dz == 3 and not upward(0, h)):
                return [(0, 0, -1, 0, ("A", dz + 1, h))]
            return []
        _, dq, dp, h = what
        ways = []
        if (dq, dp) == (0, 0):
            ways += [(1, 0, 0, 0, ("K", 0, 3, h)), (-1, 0, 0, 0, ("K", 0, 1, h))]
        elif (dq, dp) == (0, 3) and upward(2, h):
            ways += [(1, 0, 0, 0, ("K", 0, 2, h))]
        elif (dq, dp) == (0, 1) and not upward(2, h):
            ways += [(-1, 0, 0, 0, ("K", 0, 2, h))]
        if dq == 0:
            ways += [(0, 1, 0, 0, ("K", 3, dp, h)), (0, -1, 0, 0, ("K", 1, dp, h))]
        elif dq == 3 and upward(dp, h):
            ways += [(0, 1, 0, 0, ("K", 2, dp, h))]
        elif dq == 1 and not upward(dp, h):
            ways += [(0, -1, 0, 0, ("K", 2, dp, h))]
        return ways + [(0, 0, 0, 1, ("S", dq, dp, h))]

    def place(what):
        if what[0] == "A":
            return a_ref(what[1], what[2])
        return k_ref(1 if what[0] == "S" else 0, *what[1:])

    def forward(what, way):
        tp, tq, tz, ts, there = way
        post(there, place(what), place(there), up(tz) if tz else chip(tp, tq, bool(ts)))

    def hand_on(what):
        for way in ways_of(what):
            forward(what, way)

    for axes in ((0, 2), (1,), (3,)):
        for h in range(PIECES):
            for what in (("K", 0, 0, h), ("A", 0, h)):
                for way in ways_of(what):
                    if any(way[i] for i in axes):
                        forward(what, way)
    for dz in range(1, N_Z):
        post(("L", 8 - dz), al.at[0], al.at[8 - dz], up(dz))
    for s, dq, dp in peers:
        post(("M", s, dq, dp), var.at[K_POS[(dq, dp)] % 4], kl.at[key_slot(s, dq, dp)], chip(-dp, -dq, s))

    lane = lax.broadcasted_iota(jnp.int32, (1, 128), 1)

    def columns(rows, out):
        turned = jnp.transpose(jnp.concatenate([rows, jnp.zeros((128 - N_Z, 128), F32)], axis=0))
        for dz, p in A_POS.items():
            out[pl.ds(p * BLOCK, BLOCK), :] = jnp.broadcast_to(turned[:BLOCK, dz : dz + 1], (BLOCK, 128))

    def lines(stat, out):
        for dz in range(N_Z):
            part = jnp.transpose(stat[pl.ds(A_POS[dz] * BLOCK, 128), :])
            out[dz : dz + 1, :] = jnp.sum(part, axis=0, keepdims=True)

    def exchange(name, out, into):
        for dz in (4, 3, 5, 2, 6, 1, 7):
            post((name, 8 - dz), out, into.at[8 - dz], up(dz))

    def gathered(name, out, into):
        total = out[...]
        for dz in range(1, N_Z):
            arrived((name, dz), into.at[dz])
            total = total + pltpu.roll(into[dz], dz, 0)
        return total

    def key_line(line_of, out):
        for s in (0, 1):
            for q in range(4):
                m = [line_of(s, q * 4 + p) for p in range(4)]
                base = q * GROUP + s * (GROUP // 2)
                for t, (cut, a, b) in enumerate(((96, 0, 1), (64, 1, 2), (32, 2, 3))):
                    line = jnp.where(lane < cut, m[a], m[b])
                    out[:, pl.ds(base + t * 128, 128)] = jnp.broadcast_to(line, (8, 128))

    def labels_ready():
        for dz in range(1, N_Z):
            arrived(("L", dz), al.at[dz])
        for s, dq, dp in peers:
            arrived(("M", s, dq, dp), kl.at[key_slot(s, dq, dp)])
        columns(jnp.concatenate([al[dz] for dz in range(N_Z)], axis=0), labc)
        key_line(lambda s, q: kl[s * 16 + q], klab)

    def count(r0):
        for r in range(r0, r0 + 192, 32):
            label = labc[pl.ds(r, 32), :]
            total = jnp.zeros((32, 128), F32)
            for t in range(KEYS // 128):
                total = total + jnp.where(label == klab[0:1, t * 128 : (t + 1) * 128], 1.0, 0.0)
            cst[pl.ds(r, 32), :] = total
        if r0 == ANCHORS - 192:
            lines(cst, cto)
            exchange("C", cto, cti)

    def counts_ready():
        positives = gathered("C", cto, cti) - 1.0
        cto8 = jnp.where(lane < BLOCK, 2.0 / jnp.maximum(positives, 1.0), 0.0)
        columns(cto8, idc)
        eio[...] = positives[0:1] / jnp.maximum(positives[0:1], 1.0)

    def on_diagonal(rows):
        r = lax.broadcasted_iota(jnp.int32, (rows, 128), 0)
        c = lax.broadcasted_iota(jnp.int32, (rows, 128), 1)
        return (r == c) & (r < BLOCK)

    def score(r0, rows, c0, cols):
        at = pl.ds(r0, rows)
        acc = lax.dot_general(au[at, :], ku[pl.ds(c0, cols), :], NT, preferred_element_type=F32)
        total = None
        for t in range(cols // 128):
            here = pl.ds(c0 + t * 128, 128)
            s = acc[:, t * 128 : (t + 1) * 128]
            w[at, here] = s
            e = jnp.exp2(s * (10.0 * LOG2E))
            if r0 == 0 and c0 + t == 0:
                e = jnp.where(on_diagonal(rows), 0.0, e)
            cs[:, here] += jnp.sum(e.reshape(rows // 8, 8, 128), axis=0)
            total = e if t == 0 else total + e
        est[at, :] += total

    def positives():
        for r in range(0, ANCHORS, 32):
            at = pl.ds(r, 32)
            label = labc[at, :]
            total = jnp.zeros((32, 128), F32)
            for c in range(0, KEYS, 128):
                here = pl.ds(c, 128)
                same = label == klab[0:1, here]
                if c == 0 and r < BLOCK:
                    i = lax.broadcasted_iota(jnp.int32, (32, 128), 0) + r
                    same = same & (i != lax.broadcasted_iota(jnp.int32, (32, 128), 1))
                total = total + jnp.where(same, w[at, here], 0.0)
            pst[at, :] = total

    def need(r0, rows, c0, cols):
        wants = set()
        for dz, p in A_POS.items():
            if dz and p * BLOCK < r0 + rows and (p + 1) * BLOCK > r0:
                wants |= {("A", dz, h) for h in range(PIECES)}
        for s in (0, 1):
            for dq, dp in K_ORDER:
                k0 = key_row(s, dq, dp)
                if k0 < c0 + cols and k0 + BLOCK > c0 and (s, dq, dp) != (0, 0, 0):
                    wants |= {("S" if s else "K", dq, dp, h) for h in range(PIECES)}
        return wants

    work = [("count", r) for r in range(0, ANCHORS, 192)]
    for r0, rows, c0, c1, wide in (
        (0, 288, 0, GROUP, 256),
        (288, 192, 0, GROUP, 256),
        (0, 480, GROUP, 2 * GROUP, 256),
        (480, 192, 0, 2 * GROUP, 256),
        (0, 672, 2 * GROUP, 3 * GROUP, 256),
        (672, 96, 0, 3 * GROUP, GROUP),
        (0, 768, 3 * GROUP, 4 * GROUP, 256),
    ):
        work += [(r0, rows, c, wide) for c in range(c0, c1, wide)]
    work.insert(10, ("done",))

    seen = set()

    def receive(what):
        if what in seen:
            return
        seen.add(what)
        if what[0] == "A":
            arrived(what, a_ref(what[1], what[2]))
        else:
            arrived(what, k_ref(1 if what[0] == "S" else 0, *what[1:]))
        if what[0] != "S":
            hand_on(what)

    def can_run(wants):
        return all(v in seen for v in wants if v[0] != "S")

    def do(job):
        if job[0] == "count":
            count(job[1])
        elif job[0] == "done":
            counts_ready()
        else:
            for v in sorted(need(*job) - seen):
                receive(v)
            score(*job)

    left = list(range(len(work)))
    for n, what in enumerate(ARRIVALS):
        receive(what)
        if n == LABELS_AT:
            labels_ready()
        for i in JOBS_AFTER.get(n, ()):
            do(work[i])
            left.remove(i)
    for i in left:
        do(work[i])

    gathered_by = len(pending)
    tiles = [jnp.sum(cs[:, t * 128 : (t + 1) * 128], axis=0, keepdims=True) for t in range(KEYS // 128)]
    for s in (0, 1):
        for dq, dp in K_ORDER:
            t, off = divmod(key_row(s, dq, dp), 128)
            line = tiles[t]
            if off:
                line = pltpu.roll(line, 128 - off, 1)
                if off + BLOCK > 128:
                    line = jnp.where(lane < 128 - off, line, pltpu.roll(tiles[t + 1], 128 - off, 1))
            r = s * 16 + dq * 4 + dp
            kso[r : r + 1, :] = line
    post(("X",), kso, ksi, chip(0, 0, True))
    lines(est, eto)
    exchange("E", eto, eti)
    arrived(("X",), ksi)
    both = [kso[0:16, :] + ksi[16:32, :], kso[16:32, :] + ksi[0:16, :]]
    kvo[0:16, :] = both[0].astype(BF16)
    kvo[16:32, :] = both[1].astype(BF16)
    plane = [(dq, dp) for dq, dp in reversed(K_ORDER) if (dq, dp) != (0, 0)]
    for dq, dp in plane:
        post(("V", dq, dp), kvo, kvi.at[dq * 4 + dp], chip(-dp, -dq, False))
    real = lane < BLOCK
    totals = jnp.where(real, gathered("E", eto, eti), 1.0)
    inverse_total = 1.0 / totals
    columns(inverse_total, iec)
    positives()
    share = jnp.sum(pst[0:ANCHORS, :] * idc[...], axis=0, keepdims=True) * -5.0
    tail = jnp.where(real, eio[...] * jnp.log(totals[0:1]), 0.0)
    lz[...] = share + tail
    for dz in range(1, N_Z):
        post(("P", 8 - dz), lz, lzi.at[8 - dz], up(dz))
    for dq, dp in plane:
        arrived(("V", dq, dp), kvi.at[dq * 4 + dp])
    within = lax.broadcasted_iota(jnp.int32, (16, 128), 0) % 4
    turned = []
    for s in (0, 1):
        total = both[s]
        for b in range(4):
            by_q = None
            for a in range(4):
                dq, dp = (b, a) if s else (a, b)
                if (dq, dp) == (0, 0):
                    continue
                value = kvi[dq * 4 + dp, s * 16 : s * 16 + 16, :].astype(F32)
                if a:
                    value = pltpu.roll(value, 4 * a, 0)
                by_q = value if by_q is None else by_q + value
            if b:
                by_q = jnp.where(within < b, pltpu.roll(by_q, 12 + b, 0), pltpu.roll(by_q, b, 0))
            total = total + by_q
        inverse = 1.0 / total
        turned.append([pltpu.roll(inverse, shift, 1) if shift else inverse for shift in SHIFTS])

    def inverse_line(s, q):
        dq, dp = K_ORDER[q]
        r = dq * 4 + dp
        return turned[s][q % 4][r : r + 1, :]

    key_line(inverse_line, kie)

    def coupling(r0, rows):
        for r in range(r0, r0 + rows, 16):
            at = pl.ds(r, 16)
            ie, d2, label = iec[at, :], idc[at, :], labc[at, :]
            for c in range(0, KEYS, 128):
                here = pl.ds(c, 128)
                same = label == klab[0:1, here]
                e = jnp.exp2(w[at, here] * (10.0 * LOG2E))
                if c == 0 and r < BLOCK:
                    i = lax.broadcasted_iota(jnp.int32, (16, 128), 0) + r
                    other = i != lax.broadcasted_iota(jnp.int32, (16, 128), 1)
                    same, e = same & other, jnp.where(other, e, 0.0)
                v = e * (ie + kie[0:1, here]) - jnp.where(same, d2, 0.0)
                cm[at, here] = v.astype(BF16)

    def product(j, r0, rows):
        at = pl.ds(r0, rows)
        g[j, at, :] = jnp.dot(cm[at, :], ku[:, j * WIDE : (j + 1) * WIDE], preferred_element_type=F32)

    def part(j, dz, first, n):
        return g[j, pl.ds(A_POS[dz] * BLOCK + first, n), :]

    def push(j, step):
        for way, sign in enumerate((1, -1)):
            dz = (sign * (4 - step)) % 8
            at, n = (way * HALF, HALF) if step == 0 else (0, BLOCK)
            value = part(j, dz, at, n)
            rows = pl.ds(at, n)
            if step == 1:
                half = pl.ds(way * HALF, HALF)
                arrived(("R", j, way, 0), rb.at[j, way, 0, half, :])
                pieces = [value[:HALF], value[HALF:]]
                pieces[way] = pieces[way] + rb[j, way, 0, half, :].astype(F32)
                sb[j, way, step, 0:HALF, :] = pieces[0].astype(BF16)
                sb[j, way, step, HALF:BLOCK, :] = pieces[1].astype(BF16)
            else:
                if step > 1:
                    arrived(("R", j, way, step - 1), rb.at[j, way, step - 1])
                    value = value + rb[j, way, step - 1].astype(F32)
                sb[j, way, step, rows, :] = value.astype(BF16)
            post(("R", j, way, step), sb.at[j, way, step, rows, :], rb.at[j, way, step, rows, :], up(sign))

    coupling(672, 96)
    for j in range(CHUNKS):
        product(j, 672, 96)
        push(j, 0)
    coupling(480, 192)
    for j in range(CHUNKS):
        product(j, 480, 192)
    coupling(288, 192)
    for j in range(CHUNKS):
        push(j, 1)
        product(j, 288, 192)
    coupling(96, 192)
    for j in range(CHUNKS):
        product(j, 96, 192)
    sent(gathered_by)
    coupling(0, 96)
    whole = lz[...]
    for dz in range(1, N_Z):
        arrived(("P", dz), lzi.at[dz])
        whole = whole + lzi[dz]
    lo[...] = whole
    before = len(pending)
    for j in range(CHUNKS):
        push(j, 2)
        product(j, 0, 96)
        for s, dq, dp in peers[j::CHUNKS]:
            post(("W", s, dq, dp), lo, li.at[key_slot(s, dq, dp)], chip(-dp, -dq, s))
    for j in range(CHUNKS):
        push(j, 3)
    sent(before)

    every = lo[...]
    for s, dq, dp in peers:
        arrived(("W", s, dq, dp), li.at[key_slot(s, dq, dp)])
        every = every + li[key_slot(s, dq, dp)]
    loss[...] = jnp.broadcast_to(jnp.sum(every, axis=1, keepdims=True) * (1.0 / TOKENS), (1, 128))

    sent(len(pending) - 2 * CHUNKS)
    along = jnp.zeros((BLOCK, 1), F32)
    for j in range(CHUNKS):
        value = part(j, 0, 0, BLOCK)
        for way in (0, 1):
            arrived(("R", j, way, 3), rb.at[j, way, 3])
            value = value + rb[j, way, 3].astype(F32)
        value = value * 10.0
        g[j, pl.ds(0, BLOCK), :] = value
        along = along + jnp.sum(uf[:, j * WIDE : (j + 1) * WIDE] * value, axis=1, keepdims=True)
    scale = inv[:, 0:1]
    for j in range(CHUNKS):
        cut = slice(j * WIDE, (j + 1) * WIDE)
        grad[:, cut] = (g[j, pl.ds(0, BLOCK), :] - uf[:, cut] * along) * scale

    sent(len(pending))
    assert len(number.numbers) <= N_SEM


def per_device(embeddings, labels):
    vmem = pl.BlockSpec(memory_space=pltpu.VMEM)
    line = labels.reshape(1, BLOCK)
    scratch = [
        ((BLOCK, DEPTH), BF16),
        ((1, BLOCK), jnp.int32),
        ((ANCHORS, DEPTH), BF16),
        ((KEYS, DEPTH), BF16),
        ((ANCHORS, KEYS), F32),
        ((ANCHORS, KEYS), BF16),
        ((CHUNKS, ANCHORS, WIDE), F32),
        ((BLOCK, DEPTH), F32),
        ((BLOCK, 128), F32),
        ((4, 1, 128), F32),
        ((N_Z, 1, 128), F32),
        ((32, 1, 128), F32),
        ((ANCHORS, 128), F32),
        ((8, KEYS), F32),
        ((ANCHORS + 32, 128), F32),
        ((ANCHORS + 32, 128), F32),
        ((ANCHORS + 32, 128), F32),
        ((N_Z, 128), F32),
        ((N_Z, N_Z, 128), F32),
        ((N_Z, 128), F32),
        ((N_Z, N_Z, 128), F32),
        ((1, 128), F32),
        ((ANCHORS, 128), F32),
        ((ANCHORS, 128), F32),
        ((8, KEYS), F32),
        ((32, 128), F32),
        ((32, 128), F32),
        ((32, 128), BF16),
        ((16, 32, 128), BF16),
        ((8, KEYS), F32),
        ((1, 128), F32),
        ((N_Z, 1, 128), F32),
        ((1, 128), F32),
        ((32, 1, 128), F32),
        ((CHUNKS, 2, 4, BLOCK, WIDE), BF16),
        ((CHUNKS, 2, 4, BLOCK, WIDE), BF16),
    ]
    grad, loss = pl.pallas_call(
        kernel,
        out_shape=(
            pltpu.VMEM((BLOCK, DEPTH), F32),
            jax.ShapeDtypeStruct((1, 128), F32),
        ),
        in_specs=[pl.BlockSpec(memory_space=pl.ANY)] * 2,
        out_specs=(vmem, vmem),
        scratch_shapes=[pltpu.VMEM(s, t) for s, t in scratch]
        + [pltpu.SemaphoreType.DMA((2,)), pltpu.SemaphoreType.DMA((N_SEM,)), pltpu.SemaphoreType.DMA((N_SEM,))],
        compiler_params=pltpu.CompilerParams(
            collective_id=0, has_side_effects=True, vmem_limit_bytes=60 * 2**20
        ),
        cost_estimate=pl.CostEstimate(flops=2 * 2 * ANCHORS * KEYS * DEPTH, bytes_accessed=2**20, transcendentals=0),
    )(embeddings, line)
    return grad, loss[0, 0]


def solution(mesh):
    placed = (P(("row", "col"), None), P(("row", "col")))
    return jax.shard_map(
        per_device,
        mesh=mesh,
        in_specs=placed,
        out_specs=(P(("row", "col"), None), P()),
        check_vma=False,
    )
```
